32 devices in a mesh: blk: 8 (over z, core), uly: 4 (over y, x).
Axes of the slice: x: 2, y: 2, z: 4, core: 2. Of those that a mesh axis runs over, the one named last changes fastest.
Arguments:
- queries: bfloat16 [8192, 4096], P(('blk', 'uly')), may hold values from -140 to 140
- keys: bfloat16 [8192, 1024], P(('blk', 'uly')), may hold values from -6 to 6
- values: bfloat16 [8192, 1024], P(('blk', 'uly')), may hold values from -6 to 6
- doc_lengths: int32 [4], replicated, may hold values from 1 to 6144, 8192 in all
- selected: int32 [8, 8], replicated, may hold values from 0 to 6, as said below
Outputs:
- attended: bfloat16 [8192, 4096], P(('blk', 'uly'))
The draws below stay inside these ranges and needn't reach their ends.
Inputs may be any that keep to these rules, and one draw needn't show every extreme that they name: selected[b, g] <= b, and equals b only for b = 0. For every device index along blk (blocks b with equal b) and every key head, the blocks it selects that lie outside its own 1 block lie in distinct blocks of blk, so one other index of blk supplies at most one selected block a key head to it.
All inputs are finite; a program needn't handle non-finite values.
Results may differ from the reference program's by a relative error of at most 0.004.
Values may be sent and summed in bfloat16 or wider, within the bound.
No kernel may reach another device: no remote copies, remote signals or barrier semaphores. Data moves between devices by JAX's collectives and lax.ppermute only.
A program may use at most 128 MiB of HBM per device.

```python
import math
import jax
import jax.numpy as jnp
import numpy as np
from jax import lax

HQ = 32
KVH = 8
HD = 128
MB = 1024
NDOC = 4
QPD = 1
NQB = 8
TOKENS = 8192
N_BLK = 8


def paired_keys(key):
    base = jax.random.normal(jax.random.fold_in(key, 11), (TOKENS, KVH * HD), jnp.float32)
    return jnp.clip(base, -6.0, 6.0)


def draw_keys(key, part):
    return paired_keys(key).astype(jnp.bfloat16)


def draw_queries(key, part):
    base = jax.random.normal(jax.random.fold_in(key, 12), (TOKENS, HQ * HD), jnp.float32)
    return jnp.clip(base, -6.0, 6.0).astype(jnp.bfloat16)


def draw_selected(key, part):
    block = jnp.arange(NQB, dtype=jnp.int32)
    device = block // QPD
    rank = block % QPD
    places = jnp.arange(N_BLK, dtype=jnp.int32)
    spread = jnp.maximum(places, 1)
    first = jax.random.randint(jax.random.fold_in(key, 21), (N_BLK, KVH), 0, spread[:, None])
    across = (places >= N_BLK // 2)[:, None] & (jnp.arange(KVH, dtype=jnp.int32) == 0)[None, :]
    first = jnp.where(across, (places - N_BLK // 2)[:, None], first)
    within = jax.random.randint(jax.random.fold_in(key, 22), (NQB, KVH), 0, QPD)
    earlier = jax.random.randint(jax.random.fold_in(key, 23), (NQB, KVH), 0, jnp.maximum(rank, 1)[:, None])
    source = (first[device] + rank[:, None]) % jnp.maximum(device, 1)[:, None]
    remote = source * QPD + within
    local = jnp.where(rank[:, None] == 0, block[:, None], device[:, None] * QPD + earlier)
    picked = jnp.where((rank < device)[:, None], remote, local).astype(jnp.int32)
    last_row = (block == NQB - 1)[:, None] & (jnp.arange(KVH, dtype=jnp.int32) == 1)[None, :]
    return jnp.where(last_row, NQB - 2, picked).astype(jnp.int32)


def levels(rng, shape, shards, low, high):
    level, own = 1.0, jax.random.fold_in(rng, 6)
    for position, parts in shards:
        heights = jnp.exp(jax.random.uniform(jax.random.fold_in(own, position), (parts,), jnp.float32, low / len(shards), high / len(shards)))
        level = level * jnp.repeat(heights, shape[position] // parts).reshape([-1 if axis == position else 1 for axis in range(len(shape))])
    return level


def split_up(count, total, bound, lean):
    weights = [(1 << 20) // math.isqrt(rank ** lean) + 1 for rank in range(2, count + 1)]
    rest, holding = total - bound - (count - 1), [1] * (count - 1)
    while rest > 0:
        movable = [i for i in range(count - 1) if holding[i] < bound]
        whole, budget = sum([weights[i] for i in movable]), rest
        for i in movable:
            more = min(bound - holding[i], max(1, budget * weights[i] // whole), rest)
            holding[i] = holding[i] + more
            rest = rest - more
    return np.array([bound] + holding)


def ragged_sizes(key, count, total, bound, lean):
    if count == 2:
        one = jax.random.randint(key, (), max(1, total - bound), min(bound, total - 1) + 1)
        return jnp.stack([one, total - one])
    tallies = jnp.asarray(split_up(count, total, bound, lean), jnp.int32)
    couples = (count - 1) // 2
    donor, sink = tallies[1:1 + 2 * couples:2], tallies[2:2 + 2 * couples:2]
    room = jnp.minimum(donor - 1, bound - sink)
    passed = jax.random.randint(jax.random.fold_in(key, 1), (couples,), 0, 1 << 20) % (room + 1)
    tallies = tallies.at[1:1 + 2 * couples:2].set(donor - passed).at[2:2 + 2 * couples:2].set(sink + passed)
    return tallies[jax.random.permutation(jax.random.fold_in(key, 2), count)]


def centred(key, extent, deviation, limit, pieces=(), kind=jnp.bfloat16):
    array = jax.random.normal(key, extent, jnp.float32) * deviation
    if len(pieces) > 0:
        array = levels(key, extent, pieces, -0.22, 0.18) * array
    return jnp.clip(array, min=-limit, max=limit).astype(kind)


def setup_inputs(seed: int = 0) -> dict:
    key_of = jax.random.split(jax.random.key(seed), 6)
    return {
        "queries": draw_queries(jax.random.fold_in(key_of[5], 71), 0),
        "keys": draw_keys(jax.random.fold_in(key_of[5], 71), 0),
        "values": centred(key_of[2], (TOKENS, KVH * HD), 1.0, 6.0, ((0, 32),)),
        "doc_lengths": ragged_sizes(key_of[3], NDOC, TOKENS, 3 * TOKENS // 4, 2).astype(jnp.int32),
        "selected": draw_selected(jax.random.fold_in(key_of[5], 71), 0),
    }


def reference(queries, keys, values, doc_lengths, selected):
    group = HQ // KVH
    scale = 1.0 / (HD ** 0.5)
    ends = jnp.cumsum(doc_lengths)
    places = jnp.arange(TOKENS, dtype=jnp.int32)
    doc = jnp.sum((ends[None, :] <= places[:, None]).astype(jnp.int32), axis=1).reshape(NQB, MB)
    q_five = queries.reshape(NQB, MB, KVH, group, HD)
    k_four = keys.reshape(NQB, MB, KVH, HD)
    v_four = values.reshape(NQB, MB, KVH, HD)
    heads = jnp.arange(KVH, dtype=jnp.int32)
    line = jnp.arange(MB, dtype=jnp.int32)
    causal = line[:, None] >= line[None, :]

    def one_block(block):
        q_now = q_five[block].astype(jnp.float32)
        picks = selected[block]
        k_own = jnp.transpose(k_four[block], (1, 0, 2))
        v_own = jnp.transpose(v_four[block], (1, 0, 2))
        k_sel = k_four[picks, :, heads]
        v_sel = v_four[picks, :, heads]
        k_all = jnp.concatenate([k_own, k_sel], axis=1).astype(jnp.float32)
        v_all = jnp.concatenate([v_own, v_sel], axis=1).astype(jnp.float32)
        scores = jnp.einsum("mhgd,hnd->hgmn", q_now, k_all) * scale
        doc_q = doc[block]
        doc_s = doc[picks]
        own_mask = causal & (doc_q[:, None] == doc_q[None, :])
        own_mask = jnp.broadcast_to(own_mask[None], (KVH, MB, MB))
        sel_mask = (doc_q[None, :, None] == doc_s[:, None, :]) & (picks != block)[:, None, None]
        mask = jnp.concatenate([own_mask, sel_mask], axis=2)[:, None]
        top = jnp.max(jnp.where(mask, scores, -jnp.inf), axis=-1, keepdims=True)
        weight = jnp.where(mask, jnp.exp(scores - top), 0.0)
        total = jnp.sum(weight, axis=-1)
        rounded = lax.optimization_barrier(weight.astype(jnp.bfloat16)).astype(jnp.float32)
        acc = jnp.einsum("hgmn,hnd->mhgd", rounded, v_all)
        out = acc / jnp.transpose(total, (2, 0, 1))[..., None]
        return out.astype(jnp.bfloat16).reshape(MB, HQ * HD)

    return lax.map(one_block, jnp.arange(NQB, dtype=jnp.int32)).reshape(TOKENS, HQ * HD)
```

```python
import functools

import jax
import jax.numpy as jnp
from jax import lax
from jax.experimental import pallas as pl
from jax.experimental.pallas import tpu as pltpu
from jax.sharding import PartitionSpec as P

HQ = 32
KVH = 8
HD = 128
MB = 1024
GROUP = HQ // KVH
LOG2E = 1.4426950408889634
HIDDEN = -1e30
VMEM = 50 * 1024 * 1024


def pick_kernel(info, k_ref, v_ref, k_out, v_out):
    k_out[...] = k_ref[...]
    v_out[...] = v_ref[...]


def pick(source, k_all, v_all, rows):
    spec = pl.BlockSpec((rows, HD), lambda g, info: (info[g], g))
    out = pl.BlockSpec((rows, HD), lambda g, info: (0, g))
    shape = jax.ShapeDtypeStruct((rows, KVH * HD), k_all.dtype)
    return pl.pallas_call(
        pick_kernel,
        grid_spec=pltpu.PrefetchScalarGridSpec(
            num_scalar_prefetch=1, grid=(KVH,), in_specs=[spec, spec], out_specs=[out, out]
        ),
        out_shape=[shape, shape],
        cost_estimate=pl.CostEstimate(
            flops=0, bytes_accessed=4 * rows * KVH * HD * 2, transcendentals=0
        ),
        name="pick",
    )(source, k_all, v_all)


def starts_of(info, ndoc, places):
    first = jnp.zeros_like(places)
    for d in range(ndoc):
        end = info[d]
        first = jnp.maximum(first, jnp.where(end <= places, end, 0))
    return first


def split_query(q):
    scaled = q.astype(jnp.float32) * (LOG2E / HD**0.5)
    high = scaled.astype(jnp.bfloat16)
    low = (scaled - high.astype(jnp.float32)).astype(jnp.bfloat16)
    return jnp.concatenate([high, low], axis=1)


def doubled(k):
    return jnp.concatenate([k, k], axis=1)


def with_ones(v):
    return jnp.concatenate([v, jnp.ones_like(v)], axis=1)


def own_kernel(ndoc, info, q_ref, k_ref, v_ref, acc_ref, stat_ref, bias):
    rows = q_ref.shape[0]

    @pl.when(pl.program_id(0) == 0)
    def _():
        base = info[ndoc]
        place = base + lax.broadcasted_iota(jnp.int32, (rows, 1), 0)
        first = starts_of(info, ndoc, place)
        key = info[ndoc + 1] * MB + lax.broadcasted_iota(jnp.int32, (rows, MB), 1)
        bias[...] = jnp.where((key <= place) & (key >= first), 0.0, HIDDEN)

    kk = doubled(k_ref[...])
    vv = with_ones(v_ref[...])
    lane = lax.broadcasted_iota(jnp.int32, (rows, HD), 1)
    stat = jnp.zeros((rows, HD), jnp.float32)
    for h in range(GROUP):
        cols = slice(h * HD, (h + 1) * HD)
        qq = split_query(q_ref[:, cols])
        s = lax.dot_general(qq, kk, (((1,), (1,)), ((), ())), preferred_element_type=jnp.float32)
        s = s + bias[...]
        top = jnp.max(s, axis=1, keepdims=True)
        p = jnp.exp2(s - top).astype(jnp.bfloat16)
        both = lax.dot_general(p, vv, (((1,), (0,)), ((), ())), preferred_element_type=jnp.float32)
        acc_ref[:, cols] = both[:, :HD]
        stat = jnp.where(lane == h, top, stat)
        stat = jnp.where(lane == GROUP + h, both[:, HD:], stat)
    stat_ref[...] = stat


def own_attention(info, ndoc, own_row, queries, k_own, v_own):
    rows = queries.shape[0]
    wide = GROUP * HD
    per_head = lambda g, info: (0, g)
    kv = pl.BlockSpec((MB, HD), lambda g, info: (info[own_row], g))
    return pl.pallas_call(
        functools.partial(own_kernel, ndoc),
        grid_spec=pltpu.PrefetchScalarGridSpec(
            num_scalar_prefetch=1,
            grid=(KVH,),
            in_specs=[pl.BlockSpec((rows, wide), per_head), kv, kv],
            out_specs=[pl.BlockSpec((rows, wide), per_head), pl.BlockSpec((rows, HD), per_head)],
            scratch_shapes=[pltpu.VMEM((rows, MB), jnp.float32)],
        ),
        out_shape=[
            jax.ShapeDtypeStruct((rows, HQ * HD), jnp.float32),
            jax.ShapeDtypeStruct((rows, KVH * HD), jnp.float32),
        ],
        compiler_params=pltpu.CompilerParams(vmem_limit_bytes=VMEM),
        cost_estimate=pl.CostEstimate(
            flops=8 * rows * MB * HQ * HD, bytes_accessed=12 << 20, transcendentals=rows * MB * HQ
        ),
        name="own_block",
    )(info, queries, k_own, v_own)


def chosen_kernel(ndoc, head_at, info, q_ref, k_ref, v_ref, acc_ref, stat_ref, out_ref):
    rows = q_ref.shape[0]
    base = info[ndoc]
    source = info[head_at + pl.program_id(0)]

    def bound(place):
        first = jnp.int32(0)
        for d in range(ndoc):
            first = jnp.maximum(first, jnp.where(info[d] <= place, info[d], 0))
        return first - source * MB

    low, high = bound(base), bound(base + rows - 1)
    live = source >= 0

    def merge(masked):
        kk = doubled(k_ref[...])
        vv = with_ones(v_ref[...])
        stat = stat_ref[...]
        if masked:
            place = base + lax.broadcasted_iota(jnp.int32, (rows, 1), 0)
            limit = starts_of(info, ndoc, place) - source * MB
            key = lax.broadcasted_iota(jnp.int32, (rows, MB), 1)
            hide = key < limit
        for h in range(GROUP):
            cols = slice(h * HD, (h + 1) * HD)
            qq = split_query(q_ref[:, cols])
            s = lax.dot_general(
                qq, kk, (((1,), (1,)), ((), ())), preferred_element_type=jnp.float32
            )
            if masked:
                s = jnp.where(hide, HIDDEN, s)
            before = stat[:, h : h + 1]
            top = jnp.maximum(jnp.max(s, axis=1, keepdims=True), before)
            p = jnp.exp2(s - top).astype(jnp.bfloat16)
            both = lax.dot_general(
                p, vv, (((1,), (0,)), ((), ())), preferred_element_type=jnp.float32
            )
            keep = jnp.exp2(before - top)
            total = both[:, HD:] + keep * stat[:, GROUP + h : GROUP + h + 1]
            acc = both[:, :HD] + keep * acc_ref[:, cols]
            out_ref[:, cols] = (acc / total).astype(out_ref.dtype)

    some = live & (low < MB)

    @pl.when(some & (high <= 0))
    def _():
        merge(False)

    @pl.when(some & (high > 0))
    def _():
        merge(True)

    @pl.when(jnp.logical_not(some))
    def _():
        stat = stat_ref[...]
        for h in range(GROUP):
            cols = slice(h * HD, (h + 1) * HD)
            total = stat[:, GROUP + h : GROUP + h + 1]
            out_ref[:, cols] = (acc_ref[:, cols] / total).astype(out_ref.dtype)


def chosen_attention(info, ndoc, head_at, row_at, queries, k_chosen, v_chosen, acc, stat):
    rows = queries.shape[0]
    wide = GROUP * HD
    per_head = lambda g, info: (0, g)
    kv = pl.BlockSpec((MB, HD), lambda g, info: (info[row_at + g], g))
    return pl.pallas_call(
        functools.partial(chosen_kernel, ndoc, head_at),
        grid_spec=pltpu.PrefetchScalarGridSpec(
            num_scalar_prefetch=1,
            grid=(KVH,),
            in_specs=[
                pl.BlockSpec((rows, wide), per_head),
                kv,
                kv,
                pl.BlockSpec((rows, wide), per_head),
                pl.BlockSpec((rows, HD), per_head),
            ],
            out_specs=pl.BlockSpec((rows, wide), per_head),
        ),
        out_shape=jax.ShapeDtypeStruct((rows, HQ * HD), queries.dtype),
        compiler_params=pltpu.CompilerParams(vmem_limit_bytes=VMEM),
        cost_estimate=pl.CostEstimate(
            flops=8 * rows * MB * HQ * HD, bytes_accessed=14 << 20, transcendentals=rows * MB * HQ
        ),
        name="chosen_block",
    )(info, queries, k_chosen, v_chosen, acc, stat)


def on_device(n_blk, n_uly, queries, keys, values, doc_lengths, selected):
    rows = queries.shape[0]
    ndoc = doc_lengths.shape[0]
    per_dev = n_uly * rows // MB
    slices = MB // rows
    blk, uly = lax.axis_index("blk"), lax.axis_index("uly")
    mine = uly // slices
    block = blk * per_dev + mine
    ends = jnp.cumsum(doc_lengths)
    place = (blk * n_uly + uly) * rows
    picks = selected[block]
    wanted = jnp.where(picks == block, -1, picks)
    info = jnp.concatenate(
        [ends, jnp.stack([place, block, mine]), wanted, picks % per_dev]
    ).astype(jnp.int32)
    head_at = ndoc + 3
    row_at = head_at + KVH

    k_all = lax.all_gather(keys, "blk", axis=0, tiled=True)
    v_all = lax.all_gather(values, "blk", axis=0, tiled=True)
    k_own = lax.all_gather(keys, "uly", axis=0, tiled=True)
    v_own = lax.all_gather(values, "uly", axis=0, tiled=True)
    acc, stat = own_attention(info, ndoc, ndoc + 2, queries, k_own, v_own)

    k_sets, v_sets = [], []
    for row in range(per_dev):
        source = selected[blk * per_dev + row] // per_dev
        k_part, v_part = pick(source, k_all, v_all, rows)
        k_sets.append(lax.all_gather(k_part, "uly", axis=0, tiled=True))
        v_sets.append(lax.all_gather(v_part, "uly", axis=0, tiled=True))
    if per_dev == 1:
        k_chosen, v_chosen = k_sets[0], v_sets[0]
    else:
        k_chosen = lax.dynamic_index_in_dim(jnp.stack(k_sets), mine, 0, keepdims=False)
        v_chosen = lax.dynamic_index_in_dim(jnp.stack(v_sets), mine, 0, keepdims=False)
    return chosen_attention(info, ndoc, head_at, row_at, queries, k_chosen, v_chosen, acc, stat)


def solution(mesh):
    placed = (P(("blk", "uly"), None), P(("blk", "uly"), None), P(("blk", "uly"), None), P(), P())
    return jax.shard_map(
        functools.partial(on_device, mesh.shape["blk"], mesh.shape["uly"]),
        mesh=mesh,
        in_specs=placed,
        out_specs=P(("blk", "uly"), None),
        check_vma=False,
    )
```

```python
import functools

import jax
import jax.numpy as jnp
from jax import lax
from jax.experimental import pallas as pl
from jax.experimental.pallas import tpu as pltpu
from jax.sharding import PartitionSpec as P

HQ = 32
KVH = 8
HD = 128
MB = 1024
GROUP = HQ // KVH
LOG2E = 1.4426950408889634
HIDDEN = -1e30
VMEM = 50 * 1024 * 1024


def pick_kernel(info, k_ref, v_ref, k_out, v_out):
    k_out[...] = k_ref[...]
    v_out[...] = v_ref[...]


def pick(source, k_all, v_all, rows):
    spec = pl.BlockSpec((rows, HD), lambda g, info: (info[g], g))
    out = pl.BlockSpec((rows, HD), lambda g, info: (0, g))
    shape = jax.ShapeDtypeStruct((rows, KVH * HD), k_all.dtype)
    return pl.pallas_call(
        pick_kernel,
        grid_spec=pltpu.PrefetchScalarGridSpec(
            num_scalar_prefetch=1, grid=(KVH,), in_specs=[spec, spec], out_specs=[out, out]
        ),
        out_shape=[shape, shape],
        cost_estimate=pl.CostEstimate(
            flops=0, bytes_accessed=4 * rows * KVH * HD * 2, transcendentals=0
        ),
        name="pick",
    )(source, k_all, v_all)


def starts_of(info, ndoc, places):
    first = jnp.zeros_like(places)
    for d in range(ndoc):
        end = info[d]
        first = jnp.maximum(first, jnp.where(end <= places, end, 0))
    return first


def split_query(q):
    scaled = q.astype(jnp.float32) * (LOG2E / HD**0.5)
    high = scaled.astype(jnp.bfloat16)
    low = (scaled - high.astype(jnp.float32)).astype(jnp.bfloat16)
    return jnp.concatenate([high, low], axis=1)


def doubled(k):
    return jnp.concatenate([k, k], axis=1)


def with_ones(v):
    return jnp.concatenate([v, jnp.ones_like(v)], axis=1)


def own_kernel(ndoc, info, q_ref, k_ref, v_ref, acc_ref, stat_ref, bias):
    rows = q_ref.shape[0]

    @pl.when(pl.program_id(0) == 0)
    def _():
        base = info[ndoc]
        place = base + lax.broadcasted_iota(jnp.int32, (rows, 1), 0)
        first = starts_of(info, ndoc, place)
        key = info[ndoc + 1] * MB + lax.broadcasted_iota(jnp.int32, (rows, MB), 1)
        bias[...] = jnp.where((key <= place) & (key >= first), 0.0, HIDDEN)

    kk = doubled(k_ref[...])
    vv = with_ones(v_ref[...])
    lane = lax.broadcasted_iota(jnp.int32, (rows, HD), 1)
    stat = jnp.zeros((rows, HD), jnp.float32)
    for h in range(GROUP):
        cols = slice(h * HD, (h + 1) * HD)
        qq = split_query(q_ref[:, cols])
        s = lax.dot_general(qq, kk, (((1,), (1,)), ((), ())), preferred_element_type=jnp.float32)
        s = s + bias[...]
        top = jnp.max(s, axis=1, keepdims=True)
        p = jnp.exp2(s - top).astype(jnp.bfloat16)
        both = lax.dot_general(p, vv, (((1,), (0,)), ((), ())), preferred_element_type=jnp.float32)
        acc_ref[:, cols] = both[:, :HD]
        stat = jnp.where(lane == h, top, stat)
        stat = jnp.where(lane == GROUP + h, both[:, HD:], stat)
    stat_ref[...] = stat


def own_attention(info, ndoc, own_row, queries, k_own, v_own):
    rows = queries.shape[0]
    wide = GROUP * HD
    per_head = lambda g, info: (0, g)
    kv = pl.BlockSpec((MB, HD), lambda g, info: (info[own_row], g))
    return pl.pallas_call(
        functools.partial(own_kernel, ndoc),
        grid_spec=pltpu.PrefetchScalarGridSpec(
            num_scalar_prefetch=1,
            grid=(KVH,),
            in_specs=[pl.BlockSpec((rows, wide), per_head), kv, kv],
            out_specs=[pl.BlockSpec((rows, wide), per_head), pl.BlockSpec((rows, HD), per_head)],
            scratch_shapes=[pltpu.VMEM((rows, MB), jnp.float32)],
        ),
        out_shape=[
            jax.ShapeDtypeStruct((rows, HQ * HD), jnp.float32),
            jax.ShapeDtypeStruct((rows, KVH * HD), jnp.float32),
        ],
        compiler_params=pltpu.CompilerParams(vmem_limit_bytes=VMEM),
        cost_estimate=pl.CostEstimate(
            flops=8 * rows * MB * HQ * HD, bytes_accessed=12 << 20, transcendentals=rows * MB * HQ
        ),
        name="own_block",
    )(info, queries, k_own, v_own)


def chosen_kernel(ndoc, head_at, info, q_ref, k_ref, v_ref, acc_ref, stat_ref, out_ref):
    rows = q_ref.shape[0]
    base = info[ndoc]
    source = info[head_at + pl.program_id(0)]

    def bound(place):
        first = jnp.int32(0)
        for d in range(ndoc):
            first = jnp.maximum(first, jnp.where(info[d] <= place, info[d], 0))
        return first - source * MB

    low, high = bound(base), bound(base + rows - 1)
    live = source >= 0

    def merge(masked):
        kk = doubled(k_ref[...])
        vv = with_ones(v_ref[...])
        stat = stat_ref[...]
        if masked:
            place = base + lax.broadcasted_iota(jnp.int32, (rows, 1), 0)
            limit = starts_of(info, ndoc, place) - source * MB
            key = lax.broadcasted_iota(jnp.int32, (rows, MB), 1)
            hide = key < limit
        for h in range(GROUP):
            cols = slice(h * HD, (h + 1) * HD)
            qq = split_query(q_ref[:, cols])
            s = lax.dot_general(
                qq, kk, (((1,), (1,)), ((), ())), preferred_element_type=jnp.float32
            )
            if masked:
                s = jnp.where(hide, HIDDEN, s)
            before = stat[:, h : h + 1]
            top = jnp.maximum(jnp.max(s, axis=1, keepdims=True), before)
            p = jnp.exp2(s - top).astype(jnp.bfloat16)
            both = lax.dot_general(
                p, vv, (((1,), (0,)), ((), ())), preferred_element_type=jnp.float32
            )
            keep = jnp.exp2(before - top)
            total = both[:, HD:] + keep * stat[:, GROUP + h : GROUP + h + 1]
            acc = both[:, :HD] + keep * acc_ref[:, cols]
            out_ref[:, cols] = (acc / total).astype(out_ref.dtype)

    some = live & (low < MB)

    @pl.when(some & (high <= 0))
    def _():
        merge(False)

    @pl.when(some & (high > 0))
    def _():
        merge(True)

    @pl.when(jnp.logical_not(some))
    def _():
        stat = stat_ref[...]
        for h in range(GROUP):
            cols = slice(h * HD, (h + 1) * HD)
            total = stat[:, GROUP + h : GROUP + h + 1]
            out_ref[:, cols] = (acc_ref[:, cols] / total).astype(out_ref.dtype)


def chosen_attention(info, ndoc, head_at, row_at, queries, k_chosen, v_chosen, acc, stat):
    rows = queries.shape[0]
    wide = GROUP * HD
    per_head = lambda g, info: (0, g)
    kv = pl.BlockSpec((MB, HD), lambda g, info: (info[row_at + g], g))
    return pl.pallas_call(
        functools.partial(chosen_kernel, ndoc, head_at),
        grid_spec=pltpu.PrefetchScalarGridSpec(
            num_scalar_prefetch=1,
            grid=(KVH,),
            in_specs=[
                pl.BlockSpec((rows, wide), per_head),
                kv,
                kv,
                pl.BlockSpec((rows, wide), per_head),
                pl.BlockSpec((rows, HD), per_head),
            ],
            out_specs=pl.BlockSpec((rows, wide), per_head),
        ),
        out_shape=jax.ShapeDtypeStruct((rows, HQ * HD), queries.dtype),
        compiler_params=pltpu.CompilerParams(vmem_limit_bytes=VMEM),
        cost_estimate=pl.CostEstimate(
            flops=8 * rows * MB * HQ * HD, bytes_accessed=14 << 20, transcendentals=rows * MB * HQ
        ),
        name="chosen_block",
    )(info, queries, k_chosen, v_chosen, acc, stat)


def whole(shape):
    return pl.BlockSpec(shape, lambda i, *_: (0, 0))


SCALARS = 2


def on_scalars(kernel, scalars, operands, in_specs, name, grid=(1,), **call):
    out_specs, scratch = call.pop("out_specs"), call.pop("scratch_shapes", ())
    return pl.pallas_call(
        kernel,
        grid_spec=pltpu.PrefetchScalarGridSpec(
            num_scalar_prefetch=SCALARS,
            grid=grid,
            in_specs=in_specs,
            out_specs=out_specs,
            scratch_shapes=scratch,
        ),
        compiler_params=pltpu.CompilerParams(vmem_limit_bytes=VMEM),
        cost_estimate=pl.CostEstimate(flops=1, bytes_accessed=1, transcendentals=0),
        name=name,
        **call,
    )(*scalars, *operands)


def copy_head(out, at, source, source_at, heads, g):
    rows = source.shape[0] if source_at is None else source_at[1]
    take = slice(None) if source_at is None else slice(source_at[0], source_at[0] + rows)
    for half in (g, heads + g):
        cols = slice(half * HD, (half + 1) * HD)
        out[at : at + rows, cols] = source[take, cols]


def copy_held(out, at, held, back, heads, g, usable):
    for step in range(len(held)):
        here = back == 2 * step
        if step == len(held) - 1:
            here = here | (back > 2 * step)

        @pl.when(here & usable)
        def _(step=step):
            copy_head(out, at, held[step], None, heads, g)


def share_kernel(chunk, heads, n_blk, docs, selected, *refs):
    *held, out = refs
    rows = held[0].shape[0]
    blk = lax.axis_index("blk")
    other = blk ^ 1
    above = jnp.minimum(other + 2, n_blk - 1)
    for at, consumer in ((0, other), (rows, above)):
        for g in range(heads):
            back = blk - selected[consumer, chunk * heads + g]
            usable = (back >= 0) & (back % 2 == 0)
            copy_held(out, at, held, back, heads, g, usable)

            @pl.when(jnp.logical_not(usable))
            def _():
                copy_head(out, at, held[0], None, heads, g)


def share(scalars, chunk, heads, n_blk, held):
    rows, wide = held[0].shape
    return on_scalars(
        functools.partial(share_kernel, chunk, heads, n_blk),
        scalars,
        held,
        [whole((rows, wide))] * len(held),
        "share",
        out_specs=whole((2 * rows, wide)),
        out_shape=jax.ShapeDtypeStruct((2 * rows, wide), held[0].dtype),
    )


def settle_kernel(chunk, heads, n_blk, docs, selected, *refs):
    *held, passed, mine, upward = refs
    rows = mine.shape[0]
    blk = lax.axis_index("blk")
    above = jnp.minimum(blk + 2, n_blk - 1)
    for at, consumer, out in ((0, blk, mine), (rows, above, upward)):
        for g in range(heads):
            back = blk - selected[consumer, chunk * heads + g]
            usable = (back >= 0) & (back % 2 == 0)
            copy_held(out, 0, held, back, heads, g, usable)

            @pl.when(jnp.logical_not(usable))
            def _():
                copy_head(out, 0, passed, (at, rows), heads, g)


def settle(scalars, chunk, heads, n_blk, held, passed):
    rows, wide = held[0].shape
    shape = jax.ShapeDtypeStruct((rows, wide), held[0].dtype)
    return on_scalars(
        functools.partial(settle_kernel, chunk, heads, n_blk),
        scalars,
        [*held, passed],
        [whole((rows, wide))] * len(held) + [whole((2 * rows, wide))],
        "settle",
        out_specs=[whole((rows, wide))] * 2,
        out_shape=[shape, shape],
    )


def finish_kernel(chunk, heads, n_blk, docs, selected, mine, below, out):
    blk = lax.axis_index("blk")
    for g in range(heads):
        arrived = (blk >= n_blk - 2) & (selected[blk, chunk * heads + g] < n_blk - 2)

        @pl.when(arrived)
        def _():
            copy_head(out, 0, below, None, heads, g)

        @pl.when(jnp.logical_not(arrived))
        def _():
            copy_head(out, 0, mine, None, heads, g)


def finish(scalars, chunk, heads, n_blk, mine, below):
    return on_scalars(
        functools.partial(finish_kernel, chunk, heads, n_blk),
        scalars,
        [mine, below],
        [whole(mine.shape)] * 2,
        "finish",
        out_specs=whole(mine.shape),
        out_shape=jax.ShapeDtypeStruct(mine.shape, mine.dtype),
    )


def first_of(docs, place):
    end = jnp.int32(0)
    first = jnp.zeros_like(place)
    for d in range(docs.shape[0]):
        end = end + docs[d]
        first = jnp.maximum(first, jnp.where(end <= place, end, 0))
    return first


def scores(qq, kk):
    return lax.dot_general(qq, kk, (((1,), (1,)), ((), ())), preferred_element_type=jnp.float32)


def weighted(p, vv):
    return lax.dot_general(p, vv, (((1,), (0,)), ((), ())), preferred_element_type=jnp.float32)


def columns_of(pieces, half):
    heads = pieces[0].shape[1] // (2 * HD)
    at = pl.multiple_of((half * heads + pl.program_id(0)) * HD, HD)
    return jnp.concatenate([piece[:, pl.ds(at, HD)] for piece in pieces], axis=0)


def each_head(q_ref, pieces, s_ref, change, use):
    kk = doubled(columns_of(pieces, 0))
    vv = with_ones(columns_of(pieces, 1))
    for h in range(GROUP + 1):
        if h < GROUP:
            s = scores(split_query(q_ref[:, h * HD : (h + 1) * HD]), kk)
            s_ref[h % 2] = s if change is None else change(s)
        if h > 0:
            use(h - 1, s_ref.at[(h - 1) % 2], vv)


def own_piece_kernel(n_uly, count, docs, selected, q_ref, *refs):
    pieces, (acc_ref, stat_ref, bias, s_ref) = refs[:count], refs[count:]
    rows = q_ref.shape[0]

    @pl.when(pl.program_id(0) == 0)
    def _():
        blk, uly = lax.axis_index("blk"), lax.axis_index("uly")
        place = (blk * n_uly + uly) * rows + lax.broadcasted_iota(jnp.int32, (rows, 1), 0)
        first = first_of(docs, place)
        lane = lax.broadcasted_iota(jnp.int32, (rows, rows), 1)
        for j in range(count):
            key = blk * MB + (uly ^ j) * rows + lane
            bias[:, j * rows : (j + 1) * rows] = jnp.where(
                (key <= place) & (key >= first), 0.0, HIDDEN
            )

    lane = lax.broadcasted_iota(jnp.int32, (rows, HD), 1)
    stats = [jnp.zeros((rows, HD), jnp.float32)]

    def use(h, s, vv):
        top = jnp.max(s[...], axis=1, keepdims=True)
        p = jnp.exp2(s[...] - top).astype(jnp.bfloat16)
        both = weighted(p, vv)
        acc_ref[:, h * HD : (h + 1) * HD] = both[:, :HD]
        stat = jnp.where(lane == h, top, stats[-1])
        stats.append(jnp.where(lane == GROUP + h, both[:, HD:], stat))

    each_head(q_ref, pieces, s_ref, lambda s: s + bias[...], use)
    stat_ref[...] = stats[-1]


def piece_specs(pieces, rows, chunk):
    def spec(piece):
        at = chunk if piece.shape[0] > rows else 0
        return pl.BlockSpec((rows, piece.shape[1]), lambda g, *_: (at, 0))

    return [spec(piece) for piece in pieces]


def own_pieces(scalars, n_uly, chunk, queries, pieces):
    rows = queries.shape[0]
    heads = pieces[0].shape[1] // (2 * HD)
    wide = GROUP * HD
    here = lambda g, *_: (0, g)
    return on_scalars(
        functools.partial(own_piece_kernel, n_uly, len(pieces)),
        scalars,
        [queries, *pieces],
        [pl.BlockSpec((rows, wide), lambda g, *_: (0, chunk * heads + g))]
        + piece_specs(pieces, rows, chunk),
        "own_block",
        grid=(heads,),
        out_specs=[pl.BlockSpec((rows, wide), here), pl.BlockSpec((rows, HD), here)],
        scratch_shapes=[
            pltpu.VMEM((rows, MB), jnp.float32),
            pltpu.VMEM((2, rows, MB), jnp.float32),
        ],
        out_shape=[
            jax.ShapeDtypeStruct((rows, heads * wide), jnp.float32),
            jax.ShapeDtypeStruct((rows, heads * HD), jnp.float32),
        ],
    )


def chosen_piece_kernel(n_uly, chunk, heads, count, docs, selected, q_ref, *refs):
    pieces, (acc_ref, stat_ref) = refs[:count], refs[count : count + 2]
    out_ref, s_ref = refs[-2:]
    rows = q_ref.shape[0]
    blk, uly = lax.axis_index("blk"), lax.axis_index("uly")
    base = (blk * n_uly + uly) * rows
    source = selected[blk, chunk * heads + pl.program_id(0)]
    low = first_of(docs, base) - source * MB
    high = first_of(docs, base + rows - 1) - source * MB

    def merge(masked):
        change = None
        if masked:
            place = base + lax.broadcasted_iota(jnp.int32, (rows, 1), 0)
            limit = first_of(docs, place) - source * MB
            lane = lax.broadcasted_iota(jnp.int32, (1, rows), 1)
            key = jnp.concatenate([(uly ^ j) * rows + lane for j in range(count)], axis=1)
            change = lambda s: jnp.where(key < limit, HIDDEN, s)
        stat = stat_ref[...]

        def use(h, s, vv):
            cols = slice(h * HD, (h + 1) * HD)
            before = stat[:, h : h + 1]
            top = jnp.maximum(jnp.max(s[...], axis=1, keepdims=True), before)
            p = jnp.exp2(s[...] - top).astype(jnp.bfloat16)
            both = weighted(p, vv)
            keep = jnp.exp2(before - top)
            total = both[:, HD:] + keep * stat[:, GROUP + h : GROUP + h + 1]
            acc = both[:, :HD] + keep * acc_ref[:, cols]
            out_ref[:, cols] = (acc / total).astype(out_ref.dtype)

        each_head(q_ref, pieces, s_ref, change, use)

    some = (source != blk) & (low < MB)

    @pl.when(some & (high <= 0))
    def _():
        merge(False)

    @pl.when(some & (high > 0))
    def _():
        merge(True)

    @pl.when(jnp.logical_not(some))
    def _():
        stat = stat_ref[...]
        for h in range(GROUP):
            cols = slice(h * HD, (h + 1) * HD)
            total = stat[:, GROUP + h : GROUP + h + 1]
            out_ref[:, cols] = (acc_ref[:, cols] / total).astype(out_ref.dtype)


def chosen_pieces(scalars, n_uly, chunk, queries, pieces, acc, stat, result):
    rows = queries.shape[0]
    count = len(pieces)
    heads = pieces[0].shape[1] // (2 * HD)
    wide = GROUP * HD
    here = lambda g, *_: (0, g)
    there = lambda g, *_: (0, chunk * heads + g)
    specs = [pl.BlockSpec((rows, wide), there)] + piece_specs(pieces, rows, chunk)
    specs += [pl.BlockSpec((rows, wide), here), pl.BlockSpec((rows, HD), here)]
    operands = [queries, *pieces, acc, stat]
    aliases = {}
    if result is not None:
        aliases = {SCALARS + len(operands): 0}
        operands.append(result)
        specs.append(pl.BlockSpec(memory_space=pl.ANY))
    return on_scalars(
        functools.partial(chosen_piece_kernel, n_uly, chunk, heads, count),
        scalars,
        operands,
        specs,
        "chosen_block",
        grid=(heads,),
        out_specs=pl.BlockSpec((rows, wide), there),
        scratch_shapes=[pltpu.VMEM((2, rows, MB), jnp.float32)],
        out_shape=jax.ShapeDtypeStruct((rows, HQ * HD), queries.dtype),
        input_output_aliases=aliases,
    )


def up_line(part, chips, sources):
    return lax.ppermute(part, "blk", [(b, b + 2 * chips) for b in sources])


def across_chip(part, n_blk):
    return lax.ppermute(part, "blk", [(b, b ^ 1) for b in range(n_blk)])


def along(part, bit):
    return lax.ppermute(part, "uly", [(u, u ^ bit) for u in range(4)])


CHUNKS = 2


def by_permutes(n_blk, n_uly, queries, keys, values, doc_lengths, selected):
    scalars = (doc_lengths, selected)
    heads = KVH // CHUNKS
    chunks = range(CHUNKS)
    parts = [
        jnp.concatenate([a[:, c * heads * HD : (c + 1) * heads * HD] for a in (keys, values)], axis=1)
        for c in chunks
    ]
    hold = lax.optimization_barrier
    packed = jnp.concatenate(parts, axis=0)

    def lower_blocks(part):
        reach = range(1, n_blk // 2 - 1)
        return [part] + [up_line(part, k, range(n_blk - 2 - 2 * k)) for k in reach]

    def offer(c, held):
        return share(scalars, c, heads, n_blk, held)

    def take(c, held, offered):
        kept, upward = settle(scalars, c, heads, n_blk, held, across_chip(offered, n_blk))
        return kept, upward, up_line(upward, 1, range(n_blk - 4, n_blk - 2))

    def square(part):
        return [part] + [along(part, bits) for bits in (1, 2, 3)]

    near, far = along(packed, 1), along(packed, 2)
    first = lower_blocks(parts[0])
    near, far, first, parts = hold((near, far, first, parts))
    corner = [along(part, 3) for part in parts]
    second = lower_blocks(parts[1])
    kept, upward, below = take(0, first, offer(0, first))
    asked, _ = hold((queries, upward))
    own = [[parts[c], near, far, corner[c]] for c in chunks]
    partial = [own_pieces(scalars, n_uly, 0, asked, own[0])]
    own[1], kept, below, partial[0], second = hold((own[1], kept, below, partial[0], second))
    offered = offer(1, second)
    kept, offered = hold((kept, offered))
    chosen = [finish(scalars, 0, heads, n_blk, kept, below)]
    gathered = [square(chosen[0])]
    kept, upward, below = take(1, second, offered)
    asked, _ = hold((queries, (upward, chosen)))
    partial.append(own_pieces(scalars, n_uly, 1, asked, own[1]))
    kept, gathered[0], _ = hold((kept, gathered[0], partial[1]))
    chosen.append(finish(scalars, 1, heads, n_blk, kept, below))
    gathered.append(square(chosen[1]))
    result = None
    for c in chunks:
        result = chosen_pieces(scalars, n_uly, c, queries, gathered[c], *partial[c], result)
    return result


def on_device(n_blk, n_uly, queries, keys, values, doc_lengths, selected):
    rows = queries.shape[0]
    ndoc = doc_lengths.shape[0]
    per_dev = n_uly * rows // MB
    slices = MB // rows
    if per_dev == 1 and n_uly == 4 and n_blk % 2 == 0 and n_blk >= 4:
        return by_permutes(n_blk, n_uly, queries, keys, values, doc_lengths, selected)
    blk, uly = lax.axis_index("blk"), lax.axis_index("uly")
    mine = uly // slices
    block = blk * per_dev + mine
    ends = jnp.cumsum(doc_lengths)
    place = (blk * n_uly + uly) * rows
    picks = selected[block]
    wanted = jnp.where(picks == block, -1, picks)
    info = jnp.concatenate(
        [ends, jnp.stack([place, block, mine]), wanted, picks % per_dev]
    ).astype(jnp.int32)
    head_at = ndoc + 3
    row_at = head_at + KVH

    k_all = lax.all_gather(keys, "blk", axis=0, tiled=True)
    v_all = lax.all_gather(values, "blk", axis=0, tiled=True)
    k_own = lax.all_gather(keys, "uly", axis=0, tiled=True)
    v_own = lax.all_gather(values, "uly", axis=0, tiled=True)
    acc, stat = own_attention(info, ndoc, ndoc + 2, queries, k_own, v_own)

    k_sets, v_sets = [], []
    for row in range(per_dev):
        source = selected[blk * per_dev + row] // per_dev
        k_part, v_part = pick(source, k_all, v_all, rows)
        k_sets.append(lax.all_gather(k_part, "uly", axis=0, tiled=True))
        v_sets.append(lax.all_gather(v_part, "uly", axis=0, tiled=True))
    if per_dev == 1:
        k_chosen, v_chosen = k_sets[0], v_sets[0]
    else:
        k_chosen = lax.dynamic_index_in_dim(jnp.stack(k_sets), mine, 0, keepdims=False)
        v_chosen = lax.dynamic_index_in_dim(jnp.stack(v_sets), mine, 0, keepdims=False)
    return chosen_attention(info, ndoc, head_at, row_at, queries, k_chosen, v_chosen, acc, stat)


def solution(mesh):
    placed = (P(("blk", "uly"), None), P(("blk", "uly"), None), P(("blk", "uly"), None), P(), P())
    return jax.shard_map(
        functools.partial(on_device, mesh.shape["blk"], mesh.shape["uly"]),
        mesh=mesh,
        in_specs=placed,
        out_specs=P(("blk", "uly"), None),
        check_vma=False,
    )
```

```python
import functools

import jax
import jax.numpy as jnp
from jax import lax
from jax.experimental import pallas as pl
from jax.experimental.pallas import tpu as pltpu
from jax.sharding import PartitionSpec as P

HQ = 32
KVH = 8
HD = 128
MB = 1024
GROUP = HQ // KVH
LOG2E = 1.4426950408889634
HIDDEN = -1e30
VMEM = 50 * 1024 * 1024


def pick_kernel(info, k_ref, v_ref, k_out, v_out):
    k_out[...] = k_ref[...]
    v_out[...] = v_ref[...]


def pick(source, k_all, v_all, rows):
    spec = pl.BlockSpec((rows, HD), lambda g, info: (info[g], g))
    out = pl.BlockSpec((rows, HD), lambda g, info: (0, g))
    shape = jax.ShapeDtypeStruct((rows, KVH * HD), k_all.dtype)
    return pl.pallas_call(
        pick_kernel,
        grid_spec=pltpu.PrefetchScalarGridSpec(
            num_scalar_prefetch=1, grid=(KVH,), in_specs=[spec, spec], out_specs=[out, out]
        ),
        out_shape=[shape, shape],
        cost_estimate=pl.CostEstimate(
            flops=0, bytes_accessed=4 * rows * KVH * HD * 2, transcendentals=0
        ),
        name="pick",
    )(source, k_all, v_all)


def starts_of(info, ndoc, places):
    first = jnp.zeros_like(places)
    for d in range(ndoc):
        end = info[d]
        first = jnp.maximum(first, jnp.where(end <= places, end, 0))
    return first


def split_query(q):
    scaled = q.astype(jnp.float32) * (LOG2E / HD**0.5)
    high = scaled.astype(jnp.bfloat16)
    low = (scaled - high.astype(jnp.float32)).astype(jnp.bfloat16)
    return jnp.concatenate([high, low], axis=1)


def doubled(k):
    return jnp.concatenate([k, k], axis=1)


def with_ones(v):
    return jnp.concatenate([v, jnp.ones_like(v)], axis=1)


def own_kernel(ndoc, info, q_ref, k_ref, v_ref, acc_ref, stat_ref, bias):
    rows = q_ref.shape[0]

    @pl.when(pl.program_id(0) == 0)
    def _():
        base = info[ndoc]
        place = base + lax.broadcasted_iota(jnp.int32, (rows, 1), 0)
        first = starts_of(info, ndoc, place)
        key = info[ndoc + 1] * MB + lax.broadcasted_iota(jnp.int32, (rows, MB), 1)
        bias[...] = jnp.where((key <= place) & (key >= first), 0.0, HIDDEN)

    kk = doubled(k_ref[...])
    vv = with_ones(v_ref[...])
    lane = lax.broadcasted_iota(jnp.int32, (rows, HD), 1)
    stat = jnp.zeros((rows, HD), jnp.float32)
    for h in range(GROUP):
        cols = slice(h * HD, (h + 1) * HD)
        qq = split_query(q_ref[:, cols])
        s = lax.dot_general(qq, kk, (((1,), (1,)), ((), ())), preferred_element_type=jnp.float32)
        s = s + bias[...]
        top = jnp.max(s, axis=1, keepdims=True)
        p = jnp.exp2(s - top).astype(jnp.bfloat16)
        both = lax.dot_general(p, vv, (((1,), (0,)), ((), ())), preferred_element_type=jnp.float32)
        acc_ref[:, cols] = both[:, :HD]
        stat = jnp.where(lane == h, top, stat)
        stat = jnp.where(lane == GROUP + h, both[:, HD:], stat)
    stat_ref[...] = stat


def own_attention(info, ndoc, own_row, queries, k_own, v_own):
    rows = queries.shape[0]
    wide = GROUP * HD
    per_head = lambda g, info: (0, g)
    kv = pl.BlockSpec((MB, HD), lambda g, info: (info[own_row], g))
    return pl.pallas_call(
        functools.partial(own_kernel, ndoc),
        grid_spec=pltpu.PrefetchScalarGridSpec(
            num_scalar_prefetch=1,
            grid=(KVH,),
            in_specs=[pl.BlockSpec((rows, wide), per_head), kv, kv],
            out_specs=[pl.BlockSpec((rows, wide), per_head), pl.BlockSpec((rows, HD), per_head)],
            scratch_shapes=[pltpu.VMEM((rows, MB), jnp.float32)],
        ),
        out_shape=[
            jax.ShapeDtypeStruct((rows, HQ * HD), jnp.float32),
            jax.ShapeDtypeStruct((rows, KVH * HD), jnp.float32),
        ],
        compiler_params=pltpu.CompilerParams(vmem_limit_bytes=VMEM),
        cost_estimate=pl.CostEstimate(
            flops=8 * rows * MB * HQ * HD, bytes_accessed=12 << 20, transcendentals=rows * MB * HQ
        ),
        name="own_block",
    )(info, queries, k_own, v_own)


def chosen_kernel(ndoc, head_at, info, q_ref, k_ref, v_ref, acc_ref, stat_ref, out_ref):
    rows = q_ref.shape[0]
    base = info[ndoc]
    source = info[head_at + pl.program_id(0)]

    def bound(place):
        first = jnp.int32(0)
        for d in range(ndoc):
            first = jnp.maximum(first, jnp.where(info[d] <= place, info[d], 0))
        return first - source * MB

    low, high = bound(base), bound(base + rows - 1)
    live = source >= 0

    def merge(masked):
        kk = doubled(k_ref[...])
        vv = with_ones(v_ref[...])
        stat = stat_ref[...]
        if masked:
            place = base + lax.broadcasted_iota(jnp.int32, (rows, 1), 0)
            limit = starts_of(info, ndoc, place) - source * MB
            key = lax.broadcasted_iota(jnp.int32, (rows, MB), 1)
            hide = key < limit
        for h in range(GROUP):
            cols = slice(h * HD, (h + 1) * HD)
            qq = split_query(q_ref[:, cols])
            s = lax.dot_general(
                qq, kk, (((1,), (1,)), ((), ())), preferred_element_type=jnp.float32
            )
            if masked:
                s = jnp.where(hide, HIDDEN, s)
            before = stat[:, h : h + 1]
            top = jnp.maximum(jnp.max(s, axis=1, keepdims=True), before)
            p = jnp.exp2(s - top).astype(jnp.bfloat16)
            both = lax.dot_general(
                p, vv, (((1,), (0,)), ((), ())), preferred_element_type=jnp.float32
            )
            keep = jnp.exp2(before - top)
            total = both[:, HD:] + keep * stat[:, GROUP + h : GROUP + h + 1]
            acc = both[:, :HD] + keep * acc_ref[:, cols]
            out_ref[:, cols] = (acc / total).astype(out_ref.dtype)

    some = live & (low < MB)

    @pl.when(some & (high <= 0))
    def _():
        merge(False)

    @pl.when(some & (high > 0))
    def _():
        merge(True)

    @pl.when(jnp.logical_not(some))
    def _():
        stat = stat_ref[...]
        for h in range(GROUP):
            cols = slice(h * HD, (h + 1) * HD)
            total = stat[:, GROUP + h : GROUP + h + 1]
            out_ref[:, cols] = (acc_ref[:, cols] / total).astype(out_ref.dtype)


def chosen_attention(info, ndoc, head_at, row_at, queries, k_chosen, v_chosen, acc, stat):
    rows = queries.shape[0]
    wide = GROUP * HD
    per_head = lambda g, info: (0, g)
    kv = pl.BlockSpec((MB, HD), lambda g, info: (info[row_at + g], g))
    return pl.pallas_call(
        functools.partial(chosen_kernel, ndoc, head_at),
        grid_spec=pltpu.PrefetchScalarGridSpec(
            num_scalar_prefetch=1,
            grid=(KVH,),
            in_specs=[
                pl.BlockSpec((rows, wide), per_head),
                kv,
                kv,
                pl.BlockSpec((rows, wide), per_head),
                pl.BlockSpec((rows, HD), per_head),
            ],
            out_specs=pl.BlockSpec((rows, wide), per_head),
        ),
        out_shape=jax.ShapeDtypeStruct((rows, HQ * HD), queries.dtype),
        compiler_params=pltpu.CompilerParams(vmem_limit_bytes=VMEM),
        cost_estimate=pl.CostEstimate(
            flops=8 * rows * MB * HQ * HD, bytes_accessed=14 << 20, transcendentals=rows * MB * HQ
        ),
        name="chosen_block",
    )(info, queries, k_chosen, v_chosen, acc, stat)


def whole(shape):
    return pl.BlockSpec(shape, lambda i, *_: (0, 0))


SCALARS = 2


def on_scalars(kernel, scalars, operands, in_specs, name, grid=(1,), **call):
    out_specs, scratch = call.pop("out_specs"), call.pop("scratch_shapes", ())
    return pl.pallas_call(
        kernel,
        grid_spec=pltpu.PrefetchScalarGridSpec(
            num_scalar_prefetch=SCALARS,
            grid=grid,
            in_specs=in_specs,
            out_specs=out_specs,
            scratch_shapes=scratch,
        ),
        compiler_params=pltpu.CompilerParams(vmem_limit_bytes=VMEM),
        cost_estimate=pl.CostEstimate(flops=1, bytes_accessed=1, transcendentals=0),
        name=name,
        **call,
    )(*scalars, *operands)


def copy_head(out, at, source, source_at, heads, g):
    rows = source.shape[0] if source_at is None else source_at[1]
    take = slice(None) if source_at is None else slice(source_at[0], source_at[0] + rows)
    for half in (g, heads + g):
        cols = slice(half * HD, (half + 1) * HD)
        out[at : at + rows, cols] = source[take, cols]


def copy_held(out, at, held, back, heads, g, usable):
    for step in range(len(held)):
        here = back == 2 * step
        if step == len(held) - 1:
            here = here | (back > 2 * step)

        @pl.when(here & usable)
        def _(step=step):
            copy_head(out, at, held[step], None, heads, g)


def share_kernel(chunk, heads, n_blk, docs, selected, *refs):
    *held, out = refs
    rows = held[0].shape[0]
    blk = lax.axis_index("blk")
    other = blk ^ 1
    above = jnp.minimum(other + 2, n_blk - 1)
    for at, consumer in ((0, other), (rows, above)):
        for g in range(heads):
            back = blk - selected[consumer, chunk * heads + g]
            usable = (back >= 0) & (back % 2 == 0)
            copy_held(out, at, held, back, heads, g, usable)

            @pl.when(jnp.logical_not(usable))
            def _():
                copy_head(out, at, held[0], None, heads, g)


def share(scalars, chunk, heads, n_blk, held):
    rows, wide = held[0].shape
    return on_scalars(
        functools.partial(share_kernel, chunk, heads, n_blk),
        scalars,
        held,
        [whole((rows, wide))] * len(held),
        "share",
        out_specs=whole((2 * rows, wide)),
        out_shape=jax.ShapeDtypeStruct((2 * rows, wide), held[0].dtype),
    )


def settle_kernel(chunk, heads, n_blk, docs, selected, *refs):
    *held, passed, mine, upward = refs
    rows = mine.shape[0]
    blk = lax.axis_index("blk")
    above = jnp.minimum(blk + 2, n_blk - 1)
    for at, consumer, out in ((0, blk, mine), (rows, above, upward)):
        for g in range(heads):
            back = blk - selected[consumer, chunk * heads + g]
            usable = (back >= 0) & (back % 2 == 0)
            copy_held(out, 0, held, back, heads, g, usable)

            @pl.when(jnp.logical_not(usable))
            def _():
                copy_head(out, 0, passed, (at, rows), heads, g)


def settle(scalars, chunk, heads, n_blk, held, passed):
    rows, wide = held[0].shape
    shape = jax.ShapeDtypeStruct((rows, wide), held[0].dtype)
    return on_scalars(
        functools.partial(settle_kernel, chunk, heads, n_blk),
        scalars,
        [*held, passed],
        [whole((rows, wide))] * len(held) + [whole((2 * rows, wide))],
        "settle",
        out_specs=[whole((rows, wide))] * 2,
        out_shape=[shape, shape],
    )


def finish_kernel(chunk, heads, n_blk, docs, selected, mine, below, out):
    blk = lax.axis_index("blk")
    for g in range(heads):
        arrived = (blk >= n_blk - 2) & (selected[blk, chunk * heads + g] < n_blk - 2)

        @pl.when(arrived)
        def _():
            copy_head(out, 0, below, None, heads, g)

        @pl.when(jnp.logical_not(arrived))
        def _():
            copy_head(out, 0, mine, None, heads, g)


def finish(scalars, chunk, heads, n_blk, mine, below):
    return on_scalars(
        functools.partial(finish_kernel, chunk, heads, n_blk),
        scalars,
        [mine, below],
        [whole(mine.shape)] * 2,
        "finish",
        out_specs=whole(mine.shape),
        out_shape=jax.ShapeDtypeStruct(mine.shape, mine.dtype),
    )


def first_of(docs, place):
    end = jnp.int32(0)
    first = jnp.zeros_like(place)
    for d in range(docs.shape[0]):
        end = end + docs[d]
        first = jnp.maximum(first, jnp.where(end <= place, end, 0))
    return first


def scores(qq, kk):
    return lax.dot_general(qq, kk, (((1,), (1,)), ((), ())), preferred_element_type=jnp.float32)


def weighted(p, vv):
    return lax.dot_general(p, vv, (((1,), (0,)), ((), ())), preferred_element_type=jnp.float32)


def columns_of(pieces, half):
    heads = pieces[0].shape[1] // (2 * HD)
    here = pl.program_id(0) * HD
    found = [piece[:, pl.ds(pl.multiple_of(half * heads * HD + here, HD), HD)] for piece in pieces[:3]]
    if len(pieces) == 4:
        found.append(pieces[3][:, pl.ds(pl.multiple_of(half * heads * HD + here, HD), HD)])
    else:
        found.append(pieces[3 + half][:, pl.ds(pl.multiple_of(here, HD), HD)])
    return jnp.concatenate(found, axis=0)


def each_head(q_ref, pieces, s_ref, change, use):
    kk = doubled(columns_of(pieces, 0))
    vv = with_ones(columns_of(pieces, 1))
    for h in range(GROUP + 1):
        if h < GROUP:
            s = scores(split_query(q_ref[:, h * HD : (h + 1) * HD]), kk)
            s_ref[h % 2] = s if change is None else change(s)
        if h > 0:
            use(h - 1, s_ref.at[(h - 1) % 2], vv)


def own_piece_kernel(n_uly, count, docs, selected, q_ref, *refs):
    pieces, (acc_ref, stat_ref, bias, s_ref) = refs[:count], refs[count:]
    rows = q_ref.shape[0]

    @pl.when(pl.program_id(0) == 0)
    def _():
        blk, uly = lax.axis_index("blk"), lax.axis_index("uly")
        place = (blk * n_uly + uly) * rows + lax.broadcasted_iota(jnp.int32, (rows, 1), 0)
        first = first_of(docs, place)
        lane = lax.broadcasted_iota(jnp.int32, (rows, rows), 1)
        for j in range(MB // rows):
            key = blk * MB + (uly ^ j) * rows + lane
            bias[:, j * rows : (j + 1) * rows] = jnp.where(
                (key <= place) & (key >= first), 0.0, HIDDEN
            )

    lane = lax.broadcasted_iota(jnp.int32, (rows, HD), 1)
    stats = [jnp.zeros((rows, HD), jnp.float32)]

    def use(h, s, vv):
        top = jnp.max(s[...], axis=1, keepdims=True)
        p = jnp.exp2(s[...] - top).astype(jnp.bfloat16)
        both = weighted(p, vv)
        acc_ref[:, h * HD : (h + 1) * HD] = both[:, :HD]
        stat = jnp.where(lane == h, top, stats[-1])
        stats.append(jnp.where(lane == GROUP + h, both[:, HD:], stat))

    each_head(q_ref, pieces, s_ref, lambda s: s + bias[...], use)
    stat_ref[...] = stats[-1]


def piece_specs(pieces, rows, chunk):
    def spec(piece):
        at = chunk if piece.shape[0] > rows else 0
        return pl.BlockSpec((rows, piece.shape[1]), lambda g, *_: (at, 0))

    return [spec(piece) for piece in pieces]


def own_pieces(scalars, n_uly, chunk, queries, pieces):
    rows = queries.shape[0]
    heads = pieces[0].shape[1] // (2 * HD)
    wide = GROUP * HD
    here = lambda g, *_: (0, g)
    return on_scalars(
        functools.partial(own_piece_kernel, n_uly, len(pieces)),
        scalars,
        [queries, *pieces],
        [pl.BlockSpec((rows, wide), lambda g, *_: (0, chunk * heads + g))]
        + piece_specs(pieces, rows, chunk),
        "own_block",
        grid=(heads,),
        out_specs=[pl.BlockSpec((rows, wide), here), pl.BlockSpec((rows, HD), here)],
        scratch_shapes=[
            pltpu.VMEM((rows, MB), jnp.float32),
            pltpu.VMEM((2, rows, MB), jnp.float32),
        ],
        out_shape=[
            jax.ShapeDtypeStruct((rows, heads * wide), jnp.float32),
            jax.ShapeDtypeStruct((rows, heads * HD), jnp.float32),
        ],
    )


def chosen_piece_kernel(n_uly, chunk, heads, count, docs, selected, q_ref, *refs):
    pieces, (acc_ref, stat_ref) = refs[:count], refs[count : count + 2]
    out_ref, s_ref = refs[-2:]
    rows = q_ref.shape[0]
    blk, uly = lax.axis_index("blk"), lax.axis_index("uly")
    base = (blk * n_uly + uly) * rows
    source = selected[blk, chunk * heads + pl.program_id(0)]
    low = first_of(docs, base) - source * MB
    high = first_of(docs, base + rows - 1) - source * MB

    def merge(masked):
        change = None
        if masked:
            place = base + lax.broadcasted_iota(jnp.int32, (rows, 1), 0)
            limit = first_of(docs, place) - source * MB
            lane = lax.broadcasted_iota(jnp.int32, (1, rows), 1)
            key = jnp.concatenate([(uly ^ j) * rows + lane for j in range(MB // rows)], axis=1)
            change = lambda s: jnp.where(key < limit, HIDDEN, s)
        stat = stat_ref[...]

        def use(h, s, vv):
            cols = slice(h * HD, (h + 1) * HD)
            before = stat[:, h : h + 1]
            top = jnp.maximum(jnp.max(s[...], axis=1, keepdims=True), before)
            p = jnp.exp2(s[...] - top).astype(jnp.bfloat16)
            both = weighted(p, vv)
            keep = jnp.exp2(before - top)
            total = both[:, HD:] + keep * stat[:, GROUP + h : GROUP + h + 1]
            acc = both[:, :HD] + keep * acc_ref[:, cols]
            out_ref[:, cols] = (acc / total).astype(out_ref.dtype)

        each_head(q_ref, pieces, s_ref, change, use)

    some = (source != blk) & (low < MB)

    @pl.when(some & (high <= 0))
    def _():
        merge(False)

    @pl.when(some & (high > 0))
    def _():
        merge(True)

    @pl.when(jnp.logical_not(some))
    def _():
        stat = stat_ref[...]
        for h in range(GROUP):
            cols = slice(h * HD, (h + 1) * HD)
            total = stat[:, GROUP + h : GROUP + h + 1]
            out_ref[:, cols] = (acc_ref[:, cols] / total).astype(out_ref.dtype)


def chosen_pieces(scalars, n_uly, chunk, queries, pieces, acc, stat, result):
    rows = queries.shape[0]
    count = len(pieces)
    heads = pieces[0].shape[1] // (2 * HD)
    wide = GROUP * HD
    here = lambda g, *_: (0, g)
    there = lambda g, *_: (0, chunk * heads + g)
    specs = [pl.BlockSpec((rows, wide), there)] + piece_specs(pieces, rows, chunk)
    specs += [pl.BlockSpec((rows, wide), here), pl.BlockSpec((rows, HD), here)]
    operands = [queries, *pieces, acc, stat]
    aliases = {}
    if result is not None:
        aliases = {SCALARS + len(operands): 0}
        operands.append(result)
        specs.append(pl.BlockSpec(memory_space=pl.ANY))
    return on_scalars(
        functools.partial(chosen_piece_kernel, n_uly, chunk, heads, count),
        scalars,
        operands,
        specs,
        "chosen_block",
        grid=(heads,),
        out_specs=pl.BlockSpec((rows, wide), there),
        scratch_shapes=[pltpu.VMEM((2, rows, MB), jnp.float32)],
        out_shape=jax.ShapeDtypeStruct((rows, HQ * HD), queries.dtype),
        input_output_aliases=aliases,
    )


def up_line(part, chips, sources):
    return lax.ppermute(part, "blk", [(b, b + 2 * chips) for b in sources])


def across_chip(part, n_blk):
    return lax.ppermute(part, "blk", [(b, b ^ 1) for b in range(n_blk)])


def along(part, bit):
    return lax.ppermute(part, "uly", [(u, u ^ bit) for u in range(4)])


CHUNKS = 2


def by_permutes(n_blk, n_uly, queries, keys, values, doc_lengths, selected):
    scalars = (doc_lengths, selected)
    heads = KVH // CHUNKS
    chunks = range(CHUNKS)
    parts = [
        jnp.concatenate([a[:, c * heads * HD : (c + 1) * heads * HD] for a in (keys, values)], axis=1)
        for c in chunks
    ]
    hold = lax.optimization_barrier
    packed = jnp.concatenate(parts, axis=0)

    def lower_blocks(part):
        reach = range(1, n_blk // 2 - 1)
        return [part] + [up_line(part, k, range(n_blk - 2 - 2 * k)) for k in reach]

    def offer(c, held):
        return share(scalars, c, heads, n_blk, held)

    def take(c, held, offered):
        kept, upward = settle(scalars, c, heads, n_blk, held, across_chip(offered, n_blk))
        return kept, upward, up_line(upward, 1, range(n_blk - 4, n_blk - 2))

    def corner_parts(near, far):
        middle = near.shape[1] // 2
        return near[:, :middle], far[:, middle:]

    near, far = along(packed, 1), along(packed, 2)
    first = lower_blocks(parts[0])
    near, far, first, parts = hold((near, far, first, parts))
    corner = [along(part, 3) for part in parts]
    second = lower_blocks(parts[1])
    kept, upward, below = take(0, first, offer(0, first))
    asked, _ = hold((queries, upward))
    own = [[parts[c], near, far, corner[c]] for c in chunks]
    partial = [own_pieces(scalars, n_uly, 0, asked, own[0])]
    second, own[1], kept, below, partial[0] = hold((second, own[1], kept, below, partial[0]))
    offered = offer(1, second)
    kept, offered = hold((kept, offered))
    chosen = [finish(scalars, 0, heads, n_blk, kept, below)]
    near, far = along(chosen[0], 1), along(chosen[0], 2)
    kept, upward, below = take(1, second, offered)
    asked, _ = hold((queries, (upward, chosen)))
    partial.append(own_pieces(scalars, n_uly, 1, asked, own[1]))
    near, far, _ = hold((near, far, partial[1]))
    passed = corner_parts(near, far)
    passed = [along(passed[0], 2), along(passed[1], 1)]
    gathered = [[chosen[0], near, far, *passed]]
    kept, gathered[0] = hold((kept, gathered[0]))
    chosen.append(finish(scalars, 1, heads, n_blk, kept, below))
    near, far = along(chosen[1], 1), along(chosen[1], 2)
    result = chosen_pieces(scalars, n_uly, 0, queries, gathered[0], *partial[0], None)
    near, far, result = hold((near, far, result))
    passed = corner_parts(near, far)
    passed = [along(passed[0], 2), along(passed[1], 1)]
    return chosen_pieces(
        scalars, n_uly, 1, queries, [chosen[1], near, far, *passed], *partial[1], result
    )


def on_device(n_blk, n_uly, queries, keys, values, doc_lengths, selected):
    rows = queries.shape[0]
    ndoc = doc_lengths.shape[0]
    per_dev = n_uly * rows // MB
    slices = MB // rows
    if per_dev == 1 and n_uly == 4 and n_blk % 2 == 0 and n_blk >= 4:
        return by_permutes(n_blk, n_uly, queries, keys, values, doc_lengths, selected)
    blk, uly = lax.axis_index("blk"), lax.axis_index("uly")
    mine = uly // slices
    block = blk * per_dev + mine
    ends = jnp.cumsum(doc_lengths)
    place = (blk * n_uly + uly) * rows
    picks = selected[block]
    wanted = jnp.where(picks == block, -1, picks)
    info = jnp.concatenate(
        [ends, jnp.stack([place, block, mine]), wanted, picks % per_dev]
    ).astype(jnp.int32)
    head_at = ndoc + 3
    row_at = head_at + KVH

    k_all = lax.all_gather(keys, "blk", axis=0, tiled=True)
    v_all = lax.all_gather(values, "blk", axis=0, tiled=True)
    k_own = lax.all_gather(keys, "uly", axis=0, tiled=True)
    v_own = lax.all_gather(values, "uly", axis=0, tiled=True)
    acc, stat = own_attention(info, ndoc, ndoc + 2, queries, k_own, v_own)

    k_sets, v_sets = [], []
    for row in range(per_dev):
        source = selected[blk * per_dev + row] // per_dev
        k_part, v_part = pick(source, k_all, v_all, rows)
        k_sets.append(lax.all_gather(k_part, "uly", axis=0, tiled=True))
        v_sets.append(lax.all_gather(v_part, "uly", axis=0, tiled=True))
    if per_dev == 1:
        k_chosen, v_chosen = k_sets[0], v_sets[0]
    else:
        k_chosen = lax.dynamic_index_in_dim(jnp.stack(k_sets), mine, 0, keepdims=False)
        v_chosen = lax.dynamic_index_in_dim(jnp.stack(v_sets), mine, 0, keepdims=False)
    return chosen_attention(info, ndoc, head_at, row_at, queries, k_chosen, v_chosen, acc, stat)


def solution(mesh):
    placed = (P(("blk", "uly"), None), P(("blk", "uly"), None), P(("blk", "uly"), None), P(), P())
    return jax.shard_map(
        functools.partial(on_device, mesh.shape["blk"], mesh.shape["uly"]),
        mesh=mesh,
        in_specs=placed,
        out_specs=P(("blk", "uly"), None),
        check_vma=False,
    )
```

```python
import functools

import jax
import jax.numpy as jnp
from jax import lax
from jax.experimental import pallas as pl
from jax.experimental.pallas import tpu as pltpu
from jax.sharding import PartitionSpec as P

HQ = 32
KVH = 8
HD = 128
MB = 1024
GROUP = HQ // KVH
LOG2E = 1.4426950408889634
HIDDEN = -1e30
LEAST, MOST = 2.0**-60, 2.0**100
VMEM = 50 * 1024 * 1024


def pick_kernel(info, k_ref, v_ref, k_out, v_out):
    k_out[...] = k_ref[...]
    v_out[...] = v_ref[...]


def pick(source, k_all, v_all, rows):
    spec = pl.BlockSpec((rows, HD), lambda g, info: (info[g], g))
    out = pl.BlockSpec((rows, HD), lambda g, info: (0, g))
    shape = jax.ShapeDtypeStruct((rows, KVH * HD), k_all.dtype)
    return pl.pallas_call(
        pick_kernel,
        grid_spec=pltpu.PrefetchScalarGridSpec(
            num_scalar_prefetch=1, grid=(KVH,), in_specs=[spec, spec], out_specs=[out, out]
        ),
        out_shape=[shape, shape],
        cost_estimate=pl.CostEstimate(
            flops=0, bytes_accessed=4 * rows * KVH * HD * 2, transcendentals=0
        ),
        name="pick",
    )(source, k_all, v_all)


def starts_of(info, ndoc, places):
    first = jnp.zeros_like(places)
    for d in range(ndoc):
        end = info[d]
        first = jnp.maximum(first, jnp.where(end <= places, end, 0))
    return first


def split_query(q):
    scaled = q.astype(jnp.float32) * (LOG2E / HD**0.5)
    high = scaled.astype(jnp.bfloat16)
    low = (scaled - high.astype(jnp.float32)).astype(jnp.bfloat16)
    return jnp.concatenate([high, low], axis=1)


def doubled(k):
    return jnp.concatenate([k, k], axis=1)


def with_ones(v):
    return jnp.concatenate([v, jnp.ones_like(v)], axis=1)


def own_kernel(ndoc, info, q_ref, k_ref, v_ref, acc_ref, stat_ref, bias):
    rows = q_ref.shape[0]

    @pl.when(pl.program_id(0) == 0)
    def _():
        base = info[ndoc]
        place = base + lax.broadcasted_iota(jnp.int32, (rows, 1), 0)
        first = starts_of(info, ndoc, place)
        key = info[ndoc + 1] * MB + lax.broadcasted_iota(jnp.int32, (rows, MB), 1)
        bias[...] = jnp.where((key <= place) & (key >= first), 0.0, HIDDEN)

    kk = doubled(k_ref[...])
    vv = with_ones(v_ref[...])
    lane = lax.broadcasted_iota(jnp.int32, (rows, HD), 1)
    stat = jnp.zeros((rows, HD), jnp.float32)
    for h in range(GROUP):
        cols = slice(h * HD, (h + 1) * HD)
        qq = split_query(q_ref[:, cols])
        s = lax.dot_general(qq, kk, (((1,), (1,)), ((), ())), preferred_element_type=jnp.float32)
        s = s + bias[...]
        top = jnp.max(s, axis=1, keepdims=True)
        p = jnp.exp2(s - top).astype(jnp.bfloat16)
        both = lax.dot_general(p, vv, (((1,), (0,)), ((), ())), preferred_element_type=jnp.float32)
        acc_ref[:, cols] = both[:, :HD]
        stat = jnp.where(lane == h, top, stat)
        stat = jnp.where(lane == GROUP + h, both[:, HD:], stat)
    stat_ref[...] = stat


def own_attention(info, ndoc, own_row, queries, k_own, v_own):
    rows = queries.shape[0]
    wide = GROUP * HD
    per_head = lambda g, info: (0, g)
    kv = pl.BlockSpec((MB, HD), lambda g, info: (info[own_row], g))
    return pl.pallas_call(
        functools.partial(own_kernel, ndoc),
        grid_spec=pltpu.PrefetchScalarGridSpec(
            num_scalar_prefetch=1,
            grid=(KVH,),
            in_specs=[pl.BlockSpec((rows, wide), per_head), kv, kv],
            out_specs=[pl.BlockSpec((rows, wide), per_head), pl.BlockSpec((rows, HD), per_head)],
            scratch_shapes=[pltpu.VMEM((rows, MB), jnp.float32)],
        ),
        out_shape=[
            jax.ShapeDtypeStruct((rows, HQ * HD), jnp.float32),
            jax.ShapeDtypeStruct((rows, KVH * HD), jnp.float32),
        ],
        compiler_params=pltpu.CompilerParams(vmem_limit_bytes=VMEM),
        cost_estimate=pl.CostEstimate(
            flops=8 * rows * MB * HQ * HD, bytes_accessed=12 << 20, transcendentals=rows * MB * HQ
        ),
        name="own_block",
    )(info, queries, k_own, v_own)


def chosen_kernel(ndoc, head_at, info, q_ref, k_ref, v_ref, acc_ref, stat_ref, out_ref):
    rows = q_ref.shape[0]
    base = info[ndoc]
    source = info[head_at + pl.program_id(0)]

    def bound(place):
        first = jnp.int32(0)
        for d in range(ndoc):
            first = jnp.maximum(first, jnp.where(info[d] <= place, info[d], 0))
        return first - source * MB

    low, high = bound(base), bound(base + rows - 1)
    live = source >= 0

    def merge(masked):
        kk = doubled(k_ref[...])
        vv = with_ones(v_ref[...])
        stat = stat_ref[...]
        if masked:
            place = base + lax.broadcasted_iota(jnp.int32, (rows, 1), 0)
            limit = starts_of(info, ndoc, place) - source * MB
            key = lax.broadcasted_iota(jnp.int32, (rows, MB), 1)
            hide = key < limit
        for h in range(GROUP):
            cols = slice(h * HD, (h + 1) * HD)
            qq = split_query(q_ref[:, cols])
            s = lax.dot_general(
                qq, kk, (((1,), (1,)), ((), ())), preferred_element_type=jnp.float32
            )
            if masked:
                s = jnp.where(hide, HIDDEN, s)
            before = stat[:, h : h + 1]
            top = jnp.maximum(jnp.max(s, axis=1, keepdims=True), before)
            p = jnp.exp2(s - top).astype(jnp.bfloat16)
            both = lax.dot_general(
                p, vv, (((1,), (0,)), ((), ())), preferred_element_type=jnp.float32
            )
            keep = jnp.exp2(before - top)
            total = both[:, HD:] + keep * stat[:, GROUP + h : GROUP + h + 1]
            acc = both[:, :HD] + keep * acc_ref[:, cols]
            out_ref[:, cols] = (acc / total).astype(out_ref.dtype)

    some = live & (low < MB)

    @pl.when(some & (high <= 0))
    def _():
        merge(False)

    @pl.when(some & (high > 0))
    def _():
        merge(True)

    @pl.when(jnp.logical_not(some))
    def _():
        stat = stat_ref[...]
        for h in range(GROUP):
            cols = slice(h * HD, (h + 1) * HD)
            total = stat[:, GROUP + h : GROUP + h + 1]
            out_ref[:, cols] = (acc_ref[:, cols] / total).astype(out_ref.dtype)


def chosen_attention(info, ndoc, head_at, row_at, queries, k_chosen, v_chosen, acc, stat):
    rows = queries.shape[0]
    wide = GROUP * HD
    per_head = lambda g, info: (0, g)
    kv = pl.BlockSpec((MB, HD), lambda g, info: (info[row_at + g], g))
    return pl.pallas_call(
        functools.partial(chosen_kernel, ndoc, head_at),
        grid_spec=pltpu.PrefetchScalarGridSpec(
            num_scalar_prefetch=1,
            grid=(KVH,),
            in_specs=[
                pl.BlockSpec((rows, wide), per_head),
                kv,
                kv,
                pl.BlockSpec((rows, wide), per_head),
                pl.BlockSpec((rows, HD), per_head),
            ],
            out_specs=pl.BlockSpec((rows, wide), per_head),
        ),
        out_shape=jax.ShapeDtypeStruct((rows, HQ * HD), queries.dtype),
        compiler_params=pltpu.CompilerParams(vmem_limit_bytes=VMEM),
        cost_estimate=pl.CostEstimate(
            flops=8 * rows * MB * HQ * HD, bytes_accessed=14 << 20, transcendentals=rows * MB * HQ
        ),
        name="chosen_block",
    )(info, queries, k_chosen, v_chosen, acc, stat)


def whole(shape):
    return pl.BlockSpec(shape, lambda i, *_: (0, 0))


SCALARS = 2


def on_scalars(kernel, scalars, operands, in_specs, name, grid=(1,), **call):
    out_specs, scratch = call.pop("out_specs"), call.pop("scratch_shapes", ())
    return pl.pallas_call(
        kernel,
        grid_spec=pltpu.PrefetchScalarGridSpec(
            num_scalar_prefetch=SCALARS,
            grid=grid,
            in_specs=in_specs,
            out_specs=out_specs,
            scratch_shapes=scratch,
        ),
        compiler_params=pltpu.CompilerParams(vmem_limit_bytes=VMEM),
        cost_estimate=pl.CostEstimate(flops=1, bytes_accessed=1, transcendentals=0),
        name=name,
        **call,
    )(*scalars, *operands)


def copy_head(out, at, source, source_at, heads, g):
    rows = source.shape[0] if source_at is None else source_at[1]
    take = slice(None) if source_at is None else slice(source_at[0], source_at[0] + rows)
    for half in (g, heads + g):
        cols = slice(half * HD, (half + 1) * HD)
        out[at : at + rows, cols] = source[take, cols]


def copy_held(out, at, held, back, heads, g, usable):
    for step in range(len(held)):
        here = back == 2 * step
        if step == len(held) - 1:
            here = here | (back > 2 * step)

        @pl.when(here & usable)
        def _(step=step):
            copy_head(out, at, held[step], None, heads, g)


def share_kernel(chunk, heads, n_blk, docs, selected, *refs):
    *held, out = refs
    rows = held[0].shape[0]
    blk = lax.axis_index("blk")
    other = blk ^ 1
    above = jnp.minimum(other + 2, n_blk - 1)
    for at, consumer in ((0, other), (rows, above)):
        for g in range(heads):
            back = blk - selected[consumer, chunk * heads + g]
            usable = (back >= 0) & (back % 2 == 0)
            copy_held(out, at, held, back, heads, g, usable)

            @pl.when(jnp.logical_not(usable))
            def _():
                copy_head(out, at, held[0], None, heads, g)


def share(scalars, chunk, heads, n_blk, held):
    rows, wide = held[0].shape
    return on_scalars(
        functools.partial(share_kernel, chunk, heads, n_blk),
        scalars,
        held,
        [whole((rows, wide))] * len(held),
        "share",
        out_specs=whole((2 * rows, wide)),
        out_shape=jax.ShapeDtypeStruct((2 * rows, wide), held[0].dtype),
    )


def settle_kernel(chunk, heads, n_blk, docs, selected, *refs):
    *held, passed, mine, upward = refs
    rows = mine.shape[0]
    blk = lax.axis_index("blk")
    above = jnp.minimum(blk + 2, n_blk - 1)
    for at, consumer, out in ((0, blk, mine), (rows, above, upward)):
        for g in range(heads):
            back = blk - selected[consumer, chunk * heads + g]
            usable = (back >= 0) & (back % 2 == 0)
            copy_held(out, 0, held, back, heads, g, usable)

            @pl.when(jnp.logical_not(usable))
            def _():
                copy_head(out, 0, passed, (at, rows), heads, g)


def settle(scalars, chunk, heads, n_blk, held, passed):
    rows, wide = held[0].shape
    shape = jax.ShapeDtypeStruct((rows, wide), held[0].dtype)
    return on_scalars(
        functools.partial(settle_kernel, chunk, heads, n_blk),
        scalars,
        [*held, passed],
        [whole((rows, wide))] * len(held) + [whole((2 * rows, wide))],
        "settle",
        out_specs=[whole((rows, wide))] * 2,
        out_shape=[shape, shape],
    )


def finish_kernel(chunk, heads, n_blk, docs, selected, mine, below, out):
    blk = lax.axis_index("blk")
    for g in range(heads):
        arrived = (blk >= n_blk - 2) & (selected[blk, chunk * heads + g] < n_blk - 2)

        @pl.when(arrived)
        def _():
            copy_head(out, 0, below, None, heads, g)

        @pl.when(jnp.logical_not(arrived))
        def _():
            copy_head(out, 0, mine, None, heads, g)


def finish(scalars, chunk, heads, n_blk, mine, below):
    return on_scalars(
        functools.partial(finish_kernel, chunk, heads, n_blk),
        scalars,
        [mine, below],
        [whole(mine.shape)] * 2,
        "finish",
        out_specs=whole(mine.shape),
        out_shape=jax.ShapeDtypeStruct(mine.shape, mine.dtype),
    )


def first_of(docs, place):
    end = jnp.int32(0)
    first = jnp.zeros_like(place)
    for d in range(docs.shape[0]):
        end = end + docs[d]
        first = jnp.maximum(first, jnp.where(end <= place, end, 0))
    return first


def scores(qq, kk):
    return lax.dot_general(qq, kk, (((1,), (1,)), ((), ())), preferred_element_type=jnp.float32)


def weighted(p, vv):
    return lax.dot_general(p, vv, (((1,), (0,)), ((), ())), preferred_element_type=jnp.float32)


def columns_of(pieces, half):
    heads = pieces[0].shape[1] // (2 * HD)
    here = pl.program_id(0) * HD
    found = [piece[:, pl.ds(pl.multiple_of(half * heads * HD + here, HD), HD)] for piece in pieces[:3]]
    if len(pieces) == 4:
        found.append(pieces[3][:, pl.ds(pl.multiple_of(half * heads * HD + here, HD), HD)])
    else:
        found.append(pieces[3 + half][:, pl.ds(pl.multiple_of(here, HD), HD)])
    return jnp.concatenate(found, axis=0)


def each_head(q_ref, pieces, s_ref, change, use):
    kk = doubled(columns_of(pieces, 0))
    vv = with_ones(columns_of(pieces, 1))
    for h in range(GROUP + 1):
        if h < GROUP:
            s = scores(split_query(q_ref[:, h * HD : (h + 1) * HD]), kk)
            s_ref[h % 2] = s if change is None else change(s)
        if h > 0:
            use(h - 1, s_ref.at[(h - 1) % 2], vv)


def plain_attention(q_ref, pieces, change):
    q = jnp.concatenate([q_ref[:, h * HD : (h + 1) * HD] for h in range(GROUP)], axis=0)
    keys, values = columns_of(pieces, 0), columns_of(pieces, 1)
    rows, tile = q_ref.shape[0], 2 * HD
    weights, wide = [], None
    for at in range(0, MB, tile):
        s = scores(q, keys[at : at + tile]) * (LOG2E / HD**0.5)
        if change is not None:
            parts = [change(s[h * rows : (h + 1) * rows], at) for h in range(GROUP)]
            s = jnp.concatenate(parts, axis=0)
        p = jnp.exp2(s)
        pair = p[:, :HD] + p[:, HD:]
        wide = pair if wide is None else wide + pair
        weights.append(p.astype(jnp.bfloat16))
    acc = weighted(jnp.concatenate(weights, axis=1), values)
    return acc, jnp.sum(wide, axis=1, keepdims=True)


def own_piece_kernel(n_uly, count, docs, selected, q_ref, *refs):
    pieces, (acc_ref, stat_ref, plain, bias, s_ref) = refs[:count], refs[count:]
    rows = q_ref.shape[0]

    @pl.when(pl.program_id(0) == 0)
    def _():
        blk, uly = lax.axis_index("blk"), lax.axis_index("uly")
        place = (blk * n_uly + uly) * rows + lax.broadcasted_iota(jnp.int32, (rows, 1), 0)
        first = first_of(docs, place)
        lane = lax.broadcasted_iota(jnp.int32, (rows, rows), 1)
        for j in range(MB // rows):
            key = blk * MB + (uly ^ j) * rows + lane
            bias[:, j * rows : (j + 1) * rows] = jnp.where(
                (key <= place) & (key >= first), 0.0, HIDDEN
            )

    lane = lax.broadcasted_iota(jnp.int32, (rows, HD), 1)
    acc, total = plain_attention(q_ref, pieces, lambda s, at: s + bias[:, at : at + 2 * HD])
    stat = jnp.zeros((rows, HD), jnp.float32)
    for h in range(GROUP):
        here = slice(h * rows, (h + 1) * rows)
        acc_ref[:, h * HD : (h + 1) * HD] = acc[here]
        stat = jnp.where(lane == GROUP + h, total[here], stat)
    stat_ref[...] = stat
    fits = (jnp.min(total) >= LEAST) & (jnp.max(total) <= MOST)
    plain[pl.program_id(0)] = fits.astype(jnp.int32)

    @pl.when(jnp.logical_not(fits))
    def _():
        stats = [jnp.zeros((rows, HD), jnp.float32)]

        def use(h, s, vv):
            top = jnp.max(s[...], axis=1, keepdims=True)
            p = jnp.exp2(s[...] - top).astype(jnp.bfloat16)
            both = weighted(p, vv)
            acc_ref[:, h * HD : (h + 1) * HD] = both[:, :HD]
            stat = jnp.where(lane == h, top, stats[-1])
            stats.append(jnp.where(lane == GROUP + h, both[:, HD:], stat))

        each_head(q_ref, pieces, s_ref, lambda s: s + bias[...], use)
        stat_ref[...] = stats[-1]


def piece_specs(pieces, rows, chunk):
    def spec(piece):
        at = chunk if piece.shape[0] > rows else 0
        return pl.BlockSpec((rows, piece.shape[1]), lambda g, *_: (at, 0))

    return [spec(piece) for piece in pieces]


def own_pieces(scalars, n_uly, chunk, queries, pieces):
    rows = queries.shape[0]
    heads = pieces[0].shape[1] // (2 * HD)
    wide = GROUP * HD
    here = lambda g, *_: (0, g)
    return on_scalars(
        functools.partial(own_piece_kernel, n_uly, len(pieces)),
        scalars,
        [queries, *pieces],
        [pl.BlockSpec((rows, wide), lambda g, *_: (0, chunk * heads + g))]
        + piece_specs(pieces, rows, chunk),
        "own_block",
        grid=(heads,),
        out_specs=[
            pl.BlockSpec((rows, wide), here),
            pl.BlockSpec((rows, HD), here),
            pl.BlockSpec(memory_space=pltpu.SMEM),
        ],
        scratch_shapes=[
            pltpu.VMEM((rows, MB), jnp.float32),
            pltpu.VMEM((2, rows, MB), jnp.float32),
        ],
        out_shape=[
            jax.ShapeDtypeStruct((rows, heads * wide), jnp.float32),
            jax.ShapeDtypeStruct((rows, heads * HD), jnp.float32),
            jax.ShapeDtypeStruct((heads,), jnp.int32),
        ],
    )


def chosen_piece_kernel(n_uly, chunk, heads, count, docs, selected, q_ref, *refs):
    pieces, (acc_ref, stat_ref, plain) = refs[:count], refs[count : count + 3]
    out_ref, s_ref, again = refs[-3:]
    rows = q_ref.shape[0]
    blk, uly = lax.axis_index("blk"), lax.axis_index("uly")
    base = (blk * n_uly + uly) * rows
    source = selected[blk, chunk * heads + pl.program_id(0)]
    low = first_of(docs, base) - source * MB
    high = first_of(docs, base + rows - 1) - source * MB

    place = base + lax.broadcasted_iota(jnp.int32, (rows, 1), 0)
    limit = first_of(docs, place) - source * MB
    lane = lax.broadcasted_iota(jnp.int32, (1, rows), 1)

    def hidden(at, width):
        quarters = range(at // rows, (at + width) // rows)
        key = jnp.concatenate([(uly ^ j) * rows + lane for j in quarters], axis=1)
        return key < limit

    def total_of(h, stat):
        return stat[:, GROUP + h : GROUP + h + 1]

    def add_plain(masked):
        change = None
        if masked:
            change = lambda s, at: jnp.where(hidden(at, s.shape[1]), HIDDEN, s)
        acc, new = plain_attention(q_ref, pieces, change)
        stat = stat_ref[...]
        for h in range(GROUP):
            cols, here = slice(h * HD, (h + 1) * HD), slice(h * rows, (h + 1) * rows)
            total = new[here] + total_of(h, stat)
            out_ref[:, cols] = ((acc[here] + acc_ref[:, cols]) / total).astype(out_ref.dtype)
        again[0] = jnp.logical_not(jnp.max(new) <= MOST).astype(jnp.int32)

    def add_shifted():
        stat = stat_ref[...]

        def use(h, s, vv):
            cols = slice(h * HD, (h + 1) * HD)
            before = stat[:, h : h + 1]
            top = jnp.maximum(jnp.max(s[...], axis=1, keepdims=True), before)
            p = jnp.exp2(s[...] - top).astype(jnp.bfloat16)
            both = weighted(p, vv)
            keep = jnp.exp2(before - top)
            total = both[:, HD:] + keep * total_of(h, stat)
            acc = both[:, :HD] + keep * acc_ref[:, cols]
            out_ref[:, cols] = (acc / total).astype(out_ref.dtype)

        each_head(
            q_ref, pieces, s_ref, lambda s: jnp.where(hidden(0, s.shape[1]), HIDDEN, s), use
        )

    some = (source != blk) & (low < MB)
    fits = plain[pl.program_id(0)] == 1
    again[0] = (some & jnp.logical_not(fits)).astype(jnp.int32)

    @pl.when(some & fits & (high <= 0))
    def _():
        add_plain(False)

    @pl.when(some & fits & (high > 0))
    def _():
        add_plain(True)

    @pl.when(again[0] == 1)
    def _():
        add_shifted()

    @pl.when(jnp.logical_not(some))
    def _():
        stat = stat_ref[...]
        for h in range(GROUP):
            cols = slice(h * HD, (h + 1) * HD)
            out_ref[:, cols] = (acc_ref[:, cols] / total_of(h, stat)).astype(out_ref.dtype)


def chosen_pieces(scalars, n_uly, chunk, queries, pieces, acc, stat, plain, result):
    rows = queries.shape[0]
    count = len(pieces)
    heads = pieces[0].shape[1] // (2 * HD)
    wide = GROUP * HD
    here = lambda g, *_: (0, g)
    there = lambda g, *_: (0, chunk * heads + g)
    specs = [pl.BlockSpec((rows, wide), there)] + piece_specs(pieces, rows, chunk)
    specs += [pl.BlockSpec((rows, wide), here), pl.BlockSpec((rows, HD), here)]
    specs.append(pl.BlockSpec(memory_space=pltpu.SMEM))
    operands = [queries, *pieces, acc, stat, plain]
    aliases = {}
    if result is not None:
        aliases = {SCALARS + len(operands): 0}
        operands.append(result)
        specs.append(pl.BlockSpec(memory_space=pl.ANY))
    return on_scalars(
        functools.partial(chosen_piece_kernel, n_uly, chunk, heads, count),
        scalars,
        operands,
        specs,
        "chosen_block",
        grid=(heads,),
        out_specs=pl.BlockSpec((rows, wide), there),
        scratch_shapes=[pltpu.VMEM((2, rows, MB), jnp.float32), pltpu.SMEM((1,), jnp.int32)],
        out_shape=jax.ShapeDtypeStruct((rows, HQ * HD), queries.dtype),
        input_output_aliases=aliases,
    )


def up_line(part, chips, sources):
    return lax.ppermute(part, "blk", [(b, b + 2 * chips) for b in sources])


def across_chip(part, n_blk):
    return lax.ppermute(part, "blk", [(b, b ^ 1) for b in range(n_blk)])


def along(part, bit):
    return lax.ppermute(part, "uly", [(u, u ^ bit) for u in range(4)])


CHUNKS = 2


def by_permutes(n_blk, n_uly, queries, keys, values, doc_lengths, selected):
    scalars = (doc_lengths, selected)
    heads = KVH // CHUNKS
    chunks = range(CHUNKS)
    parts = [
        jnp.concatenate([a[:, c * heads * HD : (c + 1) * heads * HD] for a in (keys, values)], axis=1)
        for c in chunks
    ]
    hold = lax.optimization_barrier
    packed = jnp.concatenate(parts, axis=0)

    def lower_blocks(part):
        reach = range(1, n_blk // 2 - 1)
        return [part] + [up_line(part, k, range(n_blk - 2 - 2 * k)) for k in reach]

    def offer(c, held):
        return share(scalars, c, heads, n_blk, held)

    def take(c, held, offered):
        kept, upward = settle(scalars, c, heads, n_blk, held, across_chip(offered, n_blk))
        return kept, upward, up_line(upward, 1, range(n_blk - 4, n_blk - 2))

    def corner_parts(near, far):
        middle = near.shape[1] // 2
        return near[:, :middle], far[:, middle:]

    near, far = along(packed, 1), along(packed, 2)
    first = lower_blocks(parts[0])
    near, far, first, parts = hold((near, far, first, parts))
    corner = [along(part, 3) for part in parts]
    second = lower_blocks(parts[1])
    kept, upward, below = take(0, first, offer(0, first))
    asked, _ = hold((queries, upward))
    own = [[parts[c], near, far, corner[c]] for c in chunks]
    partial = [own_pieces(scalars, n_uly, 0, asked, own[0])]
    second, own[1], kept, below, partial[0] = hold((second, own[1], kept, below, partial[0]))
    offered = offer(1, second)
    kept, offered = hold((kept, offered))
    chosen = [finish(scalars, 0, heads, n_blk, kept, below)]
    near, far = along(chosen[0], 1), along(chosen[0], 2)
    kept, upward, below = take(1, second, offered)
    asked, _ = hold((queries, (upward, chosen)))
    partial.append(own_pieces(scalars, n_uly, 1, asked, own[1]))
    kept, near, far, _ = hold((kept, near, far, partial[1]))
    chosen.append(finish(scalars, 1, heads, n_blk, kept, below))
    near_next, far_next = along(chosen[1], 1), along(chosen[1], 2)
    near, far, _ = hold((near, far, chosen[1]))
    passed = corner_parts(near, far)
    gathered = [[chosen[0], near, far, along(passed[0], 2), along(passed[1], 1)]]
    result = chosen_pieces(scalars, n_uly, 0, queries, gathered[0], *partial[0], None)
    near, far, result = hold((near_next, far_next, result))
    passed = corner_parts(near, far)
    gathered.append([chosen[1], near, far, along(passed[0], 2), along(passed[1], 1)])
    return chosen_pieces(scalars, n_uly, 1, queries, gathered[1], *partial[1], result)


def on_device(n_blk, n_uly, queries, keys, values, doc_lengths, selected):
    rows = queries.shape[0]
    ndoc = doc_lengths.shape[0]
    per_dev = n_uly * rows // MB
    slices = MB // rows
    if per_dev == 1 and n_uly == 4 and n_blk % 2 == 0 and n_blk >= 4:
        return by_permutes(n_blk, n_uly, queries, keys, values, doc_lengths, selected)
    blk, uly = lax.axis_index("blk"), lax.axis_index("uly")
    mine = uly // slices
    block = blk * per_dev + mine
    ends = jnp.cumsum(doc_lengths)
    place = (blk * n_uly + uly) * rows
    picks = selected[block]
    wanted = jnp.where(picks == block, -1, picks)
    info = jnp.concatenate(
        [ends, jnp.stack([place, block, mine]), wanted, picks % per_dev]
    ).astype(jnp.int32)
    head_at = ndoc + 3
    row_at = head_at + KVH

    k_all = lax.all_gather(keys, "blk", axis=0, tiled=True)
    v_all = lax.all_gather(values, "blk", axis=0, tiled=True)
    k_own = lax.all_gather(keys, "uly", axis=0, tiled=True)
    v_own = lax.all_gather(values, "uly", axis=0, tiled=True)
    acc, stat = own_attention(info, ndoc, ndoc + 2, queries, k_own, v_own)

    k_sets, v_sets = [], []
    for row in range(per_dev):
        source = selected[blk * per_dev + row] // per_dev
        k_part, v_part = pick(source, k_all, v_all, rows)
        k_sets.append(lax.all_gather(k_part, "uly", axis=0, tiled=True))
        v_sets.append(lax.all_gather(v_part, "uly", axis=0, tiled=True))
    if per_dev == 1:
        k_chosen, v_chosen = k_sets[0], v_sets[0]
    else:
        k_chosen = lax.dynamic_index_in_dim(jnp.stack(k_sets), mine, 0, keepdims=False)
        v_chosen = lax.dynamic_index_in_dim(jnp.stack(v_sets), mine, 0, keepdims=False)
    return chosen_attention(info, ndoc, head_at, row_at, queries, k_chosen, v_chosen, acc, stat)


def solution(mesh):
    placed = (P(("blk", "uly"), None), P(("blk", "uly"), None), P(("blk", "uly"), None), P(), P())
    return jax.shard_map(
        functools.partial(on_device, mesh.shape["blk"], mesh.shape["uly"]),
        mesh=mesh,
        in_specs=placed,
        out_specs=P(("blk", "uly"), None),
        check_vma=False,
    )
```

```python
import functools

import jax
import jax.numpy as jnp
from jax import lax
from jax.experimental import pallas as pl
from jax.experimental.pallas import tpu as pltpu
from jax.sharding import PartitionSpec as P

HQ = 32
KVH = 8
HD = 128
MB = 1024
GROUP = HQ // KVH
LOG2E = 1.4426950408889634
HIDDEN = -1e30
LEAST, MOST = 2.0**-60, 2.0**100
VMEM = 24 * 1024 * 1024


def pick_kernel(info, k_ref, v_ref, k_out, v_out):
    k_out[...] = k_ref[...]
    v_out[...] = v_ref[...]


def pick(source, k_all, v_all, rows):
    spec = pl.BlockSpec((rows, HD), lambda g, info: (info[g], g))
    out = pl.BlockSpec((rows, HD), lambda g, info: (0, g))
    shape = jax.ShapeDtypeStruct((rows, KVH * HD), k_all.dtype)
    return pl.pallas_call(
        pick_kernel,
        grid_spec=pltpu.PrefetchScalarGridSpec(
            num_scalar_prefetch=1, grid=(KVH,), in_specs=[spec, spec], out_specs=[out, out]
        ),
        out_shape=[shape, shape],
        cost_estimate=pl.CostEstimate(
            flops=0, bytes_accessed=4 * rows * KVH * HD * 2, transcendentals=0
        ),
        name="pick",
    )(source, k_all, v_all)


def starts_of(info, ndoc, places):
    first = jnp.zeros_like(places)
    for d in range(ndoc):
        end = info[d]
        first = jnp.maximum(first, jnp.where(end <= places, end, 0))
    return first


def split_query(q):
    scaled = q.astype(jnp.float32) * (LOG2E / HD**0.5)
    high = scaled.astype(jnp.bfloat16)
    low = (scaled - high.astype(jnp.float32)).astype(jnp.bfloat16)
    return jnp.concatenate([high, low], axis=1)


def doubled(k):
    return jnp.concatenate([k, k], axis=1)


def with_ones(v):
    return jnp.concatenate([v, jnp.ones_like(v)], axis=1)


def own_kernel(ndoc, info, q_ref, k_ref, v_ref, acc_ref, stat_ref, bias):
    rows = q_ref.shape[0]

    @pl.when(pl.program_id(0) == 0)
    def _():
        base = info[ndoc]
        place = base + lax.broadcasted_iota(jnp.int32, (rows, 1), 0)
        first = starts_of(info, ndoc, place)
        key = info[ndoc + 1] * MB + lax.broadcasted_iota(jnp.int32, (rows, MB), 1)
        bias[...] = jnp.where((key <= place) & (key >= first), 0.0, HIDDEN)

    kk = doubled(k_ref[...])
    vv = with_ones(v_ref[...])
    lane = lax.broadcasted_iota(jnp.int32, (rows, HD), 1)
    stat = jnp.zeros((rows, HD), jnp.float32)
    for h in range(GROUP):
        cols = slice(h * HD, (h + 1) * HD)
        qq = split_query(q_ref[:, cols])
        s = lax.dot_general(qq, kk, (((1,), (1,)), ((), ())), preferred_element_type=jnp.float32)
        s = s + bias[...]
        top = jnp.max(s, axis=1, keepdims=True)
        p = jnp.exp2(s - top).astype(jnp.bfloat16)
        both = lax.dot_general(p, vv, (((1,), (0,)), ((), ())), preferred_element_type=jnp.float32)
        acc_ref[:, cols] = both[:, :HD]
        stat = jnp.where(lane == h, top, stat)
        stat = jnp.where(lane == GROUP + h, both[:, HD:], stat)
    stat_ref[...] = stat


def own_attention(info, ndoc, own_row, queries, k_own, v_own):
    rows = queries.shape[0]
    wide = GROUP * HD
    per_head = lambda g, info: (0, g)
    kv = pl.BlockSpec((MB, HD), lambda g, info: (info[own_row], g))
    return pl.pallas_call(
        functools.partial(own_kernel, ndoc),
        grid_spec=pltpu.PrefetchScalarGridSpec(
            num_scalar_prefetch=1,
            grid=(KVH,),
            in_specs=[pl.BlockSpec((rows, wide), per_head), kv, kv],
            out_specs=[pl.BlockSpec((rows, wide), per_head), pl.BlockSpec((rows, HD), per_head)],
            scratch_shapes=[pltpu.VMEM((rows, MB), jnp.float32)],
        ),
        out_shape=[
            jax.ShapeDtypeStruct((rows, HQ * HD), jnp.float32),
            jax.ShapeDtypeStruct((rows, KVH * HD), jnp.float32),
        ],
        compiler_params=pltpu.CompilerParams(vmem_limit_bytes=VMEM),
        cost_estimate=pl.CostEstimate(
            flops=8 * rows * MB * HQ * HD, bytes_accessed=12 << 20, transcendentals=rows * MB * HQ
        ),
        name="own_block",
    )(info, queries, k_own, v_own)


def chosen_kernel(ndoc, head_at, info, q_ref, k_ref, v_ref, acc_ref, stat_ref, out_ref):
    rows = q_ref.shape[0]
    base = info[ndoc]
    source = info[head_at + pl.program_id(0)]

    def bound(place):
        first = jnp.int32(0)
        for d in range(ndoc):
            first = jnp.maximum(first, jnp.where(info[d] <= place, info[d], 0))
        return first - source * MB

    low, high = bound(base), bound(base + rows - 1)
    live = source >= 0

    def merge(masked):
        kk = doubled(k_ref[...])
        vv = with_ones(v_ref[...])
        stat = stat_ref[...]
        if masked:
            place = base + lax.broadcasted_iota(jnp.int32, (rows, 1), 0)
            limit = starts_of(info, ndoc, place) - source * MB
            key = lax.broadcasted_iota(jnp.int32, (rows, MB), 1)
            hide = key < limit
        for h in range(GROUP):
            cols = slice(h * HD, (h + 1) * HD)
            qq = split_query(q_ref[:, cols])
            s = lax.dot_general(
                qq, kk, (((1,), (1,)), ((), ())), preferred_element_type=jnp.float32
            )
            if masked:
                s = jnp.where(hide, HIDDEN, s)
            before = stat[:, h : h + 1]
            top = jnp.maximum(jnp.max(s, axis=1, keepdims=True), before)
            p = jnp.exp2(s - top).astype(jnp.bfloat16)
            both = lax.dot_general(
                p, vv, (((1,), (0,)), ((), ())), preferred_element_type=jnp.float32
            )
            keep = jnp.exp2(before - top)
            total = both[:, HD:] + keep * stat[:, GROUP + h : GROUP + h + 1]
            acc = both[:, :HD] + keep * acc_ref[:, cols]
            out_ref[:, cols] = (acc / total).astype(out_ref.dtype)

    some = live & (low < MB)

    @pl.when(some & (high <= 0))
    def _():
        merge(False)

    @pl.when(some & (high > 0))
    def _():
        merge(True)

    @pl.when(jnp.logical_not(some))
    def _():
        stat = stat_ref[...]
        for h in range(GROUP):
            cols = slice(h * HD, (h + 1) * HD)
            total = stat[:, GROUP + h : GROUP + h + 1]
            out_ref[:, cols] = (acc_ref[:, cols] / total).astype(out_ref.dtype)


def chosen_attention(info, ndoc, head_at, row_at, queries, k_chosen, v_chosen, acc, stat):
    rows = queries.shape[0]
    wide = GROUP * HD
    per_head = lambda g, info: (0, g)
    kv = pl.BlockSpec((MB, HD), lambda g, info: (info[row_at + g], g))
    return pl.pallas_call(
        functools.partial(chosen_kernel, ndoc, head_at),
        grid_spec=pltpu.PrefetchScalarGridSpec(
            num_scalar_prefetch=1,
            grid=(KVH,),
            in_specs=[
                pl.BlockSpec((rows, wide), per_head),
                kv,
                kv,
                pl.BlockSpec((rows, wide), per_head),
                pl.BlockSpec((rows, HD), per_head),
            ],
            out_specs=pl.BlockSpec((rows, wide), per_head),
        ),
        out_shape=jax.ShapeDtypeStruct((rows, HQ * HD), queries.dtype),
        compiler_params=pltpu.CompilerParams(vmem_limit_bytes=VMEM),
        cost_estimate=pl.CostEstimate(
            flops=8 * rows * MB * HQ * HD, bytes_accessed=14 << 20, transcendentals=rows * MB * HQ
        ),
        name="chosen_block",
    )(info, queries, k_chosen, v_chosen, acc, stat)


SCALARS = 2
WHOLE = pl.BlockSpec(memory_space=pltpu.VMEM)


def on_scalars(kernel, scalars, operands, in_specs, name, grid=(1,), **call):
    out_specs, scratch = call.pop("out_specs"), call.pop("scratch_shapes", ())
    return pl.pallas_call(
        kernel,
        grid_spec=pltpu.PrefetchScalarGridSpec(
            num_scalar_prefetch=SCALARS,
            grid=grid,
            in_specs=in_specs,
            out_specs=out_specs,
            scratch_shapes=scratch,
        ),
        compiler_params=pltpu.CompilerParams(vmem_limit_bytes=VMEM),
        cost_estimate=pl.CostEstimate(flops=1, bytes_accessed=1, transcendentals=0),
        name=name,
        **call,
    )(*scalars, *operands)


def copy_head(out, at, source, source_at, heads, g):
    rows = source.shape[0] if source_at is None else source_at[1]
    take = slice(None) if source_at is None else slice(source_at[0], source_at[0] + rows)
    for half in (g, heads + g):
        cols = slice(half * HD, (half + 1) * HD)
        out[at : at + rows, cols] = source[take, cols]


def copy_held(out, at, held, back, heads, g, usable):
    for step in range(len(held)):
        here = back == 2 * step
        if step == len(held) - 1:
            here = here | (back > 2 * step)

        @pl.when(here & usable)
        def _(step=step):
            copy_head(out, at, held[step], None, heads, g)


def share_kernel(chunk, heads, n_blk, docs, selected, *refs):
    *held, out = refs
    rows = held[0].shape[0]
    blk = lax.axis_index("blk")
    other = blk ^ 1
    above = jnp.minimum(other + 2, n_blk - 1)
    for at, consumer in ((0, other), (rows, above)):
        for g in range(heads):
            back = blk - selected[consumer, chunk * heads + g]
            usable = (back >= 0) & (back % 2 == 0)
            copy_held(out, at, held, back, heads, g, usable)

            @pl.when(jnp.logical_not(usable))
            def _():
                copy_head(out, at, held[0], None, heads, g)


def share(scalars, chunk, heads, n_blk, held):
    rows, wide = held[0].shape
    return on_scalars(
        functools.partial(share_kernel, chunk, heads, n_blk),
        scalars,
        held,
        [WHOLE] * len(held),
        "share",
        out_specs=WHOLE,
        out_shape=jax.ShapeDtypeStruct((2 * rows, wide), held[0].dtype),
    )


def settle_kernel(chunk, heads, n_blk, docs, selected, *refs):
    *held, passed, mine, upward = refs
    rows = mine.shape[0]
    blk = lax.axis_index("blk")
    above = jnp.minimum(blk + 2, n_blk - 1)
    for at, consumer, out in ((0, blk, mine), (rows, above, upward)):
        for g in range(heads):
            back = blk - selected[consumer, chunk * heads + g]
            usable = (back >= 0) & (back % 2 == 0)
            copy_held(out, 0, held, back, heads, g, usable)

            @pl.when(jnp.logical_not(usable))
            def _():
                copy_head(out, 0, passed, (at, rows), heads, g)


def settle(scalars, chunk, heads, n_blk, held, passed):
    rows, wide = held[0].shape
    shape = jax.ShapeDtypeStruct((rows, wide), held[0].dtype)
    return on_scalars(
        functools.partial(settle_kernel, chunk, heads, n_blk),
        scalars,
        [*held, passed],
        [WHOLE] * (len(held) + 1),
        "settle",
        out_specs=[WHOLE] * 2,
        out_shape=[shape, shape],
    )


def finish_kernel(chunk, heads, n_blk, docs, selected, mine, below, out):
    blk = lax.axis_index("blk")
    for g in range(heads):
        arrived = (blk >= n_blk - 2) & (selected[blk, chunk * heads + g] < n_blk - 2)

        @pl.when(arrived)
        def _():
            copy_head(out, 0, below, None, heads, g)

        @pl.when(jnp.logical_not(arrived))
        def _():
            copy_head(out, 0, mine, None, heads, g)


def finish(scalars, chunk, heads, n_blk, mine, below):
    return on_scalars(
        functools.partial(finish_kernel, chunk, heads, n_blk),
        scalars,
        [mine, below],
        [WHOLE] * 2,
        "finish",
        out_specs=WHOLE,
        out_shape=jax.ShapeDtypeStruct(mine.shape, mine.dtype),
    )


def first_of(docs, place):
    end = jnp.int32(0)
    first = jnp.zeros_like(place)
    for d in range(docs.shape[0]):
        end = end + docs[d]
        first = jnp.maximum(first, jnp.where(end <= place, end, 0))
    return first


def scores(qq, kk):
    return lax.dot_general(qq, kk, (((1,), (1,)), ((), ())), preferred_element_type=jnp.float32)


def weighted(p, vv):
    return lax.dot_general(p, vv, (((1,), (0,)), ((), ())), preferred_element_type=jnp.float32)


def head_columns(ref, first, count):
    return ref[:, pl.ds(pl.multiple_of(first * HD, HD), count * HD)]


def columns_of(pieces, heads, half, chunk):
    g, found = pl.program_id(0), []
    halves = [piece for piece in pieces if piece.shape[1] == heads * HD]
    for piece in [piece for piece in pieces if piece.shape[1] > heads * HD] + halves[half : half + 1]:
        rows = MB // 4
        at = chunk * rows if piece.shape[0] > rows else 0
        first = g + (half * heads if piece.shape[1] > heads * HD else 0)
        found.append(head_columns(piece.at[pl.ds(at, rows)], first, 1))
    return jnp.concatenate(found, axis=0)


def each_head(q_ref, first, keys, values, s_ref, bias, use):
    kk, vv = doubled(keys), with_ones(values)

    def body(h, carry):
        s_ref[...] = scores(split_query(head_columns(q_ref, first + h, 1)), kk) + bias[...]
        use(h, vv)
        return carry

    lax.fori_loop(0, GROUP, body, 0)


def plain_attention(queries, keys, values, bias):
    q = jnp.concatenate(queries, axis=0)
    tile = 2 * HD
    weights = []
    for at in range(0, keys.shape[0], tile):
        s = scores(q, keys[at : at + tile]) * (LOG2E / HD**0.5)
        if bias is not None:
            s = s + jnp.concatenate([bias[:, at : at + tile]] * GROUP, axis=0)
        weights.append(jnp.exp2(s).astype(jnp.bfloat16))
    both = weighted(jnp.concatenate(weights, axis=1), with_ones(values))
    return both[:, :HD], both[:, HD:]


def first_query(chunk, heads):
    return (chunk * heads + pl.program_id(0)) * GROUP


def group_queries(q_ref, chunk, heads):
    return [head_columns(q_ref, first_query(chunk, heads) + h, 1) for h in range(GROUP)]


def own_piece_kernel(n_uly, chunk, heads, count, docs, selected, q_ref, *refs):
    pieces, (acc_ref, total_ref, top_ref, plain, bias, s_ref) = refs[:count], refs[count:]
    rows, g = q_ref.shape[0], pl.program_id(0)

    @pl.when(g == 0)
    def _():
        blk, uly = lax.axis_index("blk"), lax.axis_index("uly")
        place = (blk * n_uly + uly) * rows + lax.broadcasted_iota(jnp.int32, (rows, 1), 0)
        first = first_of(docs, place)
        lane = lax.broadcasted_iota(jnp.int32, (rows, rows), 1)
        for j in range(MB // rows):
            key = blk * MB + (uly ^ j) * rows + lane
            bias[:, j * rows : (j + 1) * rows] = jnp.where(
                (key <= place) & (key >= first), 0.0, HIDDEN
            )

    queries = group_queries(q_ref, chunk, heads)
    keys, values = (columns_of(pieces, heads, half, chunk) for half in (0, 1))
    lane = lax.broadcasted_iota(jnp.int32, (rows, HD), 1)

    def keep(h, acc, total):
        at = pl.multiple_of((g * GROUP + h) * HD, HD)
        acc_ref[:, pl.ds(at, HD)] = acc
        total_ref[:, pl.ds(at, HD)] = total

    def keep_tops(tops):
        top_ref[:, pl.ds(pl.multiple_of(g * HD, HD), HD)] = tops

    acc, total = plain_attention(queries, keys, values, bias)
    for h in range(GROUP):
        keep(h, acc[h * rows : (h + 1) * rows], total[h * rows : (h + 1) * rows])
    keep_tops(jnp.zeros((rows, HD), jnp.float32))
    fits = (jnp.min(total) >= LEAST) & (jnp.max(total) <= MOST)
    plain[g] = fits.astype(jnp.int32)

    @pl.when(jnp.logical_not(fits))
    def _():
        def use(h, vv):
            top = jnp.max(s_ref[...], axis=1, keepdims=True)
            p = jnp.exp2(s_ref[...] - top).astype(jnp.bfloat16)
            both = weighted(p, vv)
            keep(h, both[:, :HD], both[:, HD:])
            keep_tops(jnp.where(lane == h, top, head_columns(top_ref, g, 1)))

        each_head(q_ref, first_query(chunk, heads), keys, values, s_ref, bias, use)


def own_pieces(scalars, n_uly, chunk, queries, pieces):
    rows = queries.shape[0]
    heads = KVH // CHUNKS
    return on_scalars(
        functools.partial(own_piece_kernel, n_uly, chunk, heads, len(pieces)),
        scalars,
        [queries, *pieces],
        [WHOLE] * (1 + len(pieces)),
        "own_block",
        grid=(heads,),
        out_specs=[WHOLE, WHOLE, WHOLE, pl.BlockSpec(memory_space=pltpu.SMEM)],
        scratch_shapes=[
            pltpu.VMEM((rows, MB), jnp.float32),
            pltpu.VMEM((rows, MB), jnp.float32),
        ],
        out_shape=[
            jax.ShapeDtypeStruct((rows, heads * GROUP * HD), jnp.float32),
            jax.ShapeDtypeStruct((rows, heads * GROUP * HD), jnp.float32),
            jax.ShapeDtypeStruct((rows, heads * HD), jnp.float32),
            jax.ShapeDtypeStruct((heads,), jnp.int32),
        ],
    )


def chosen_piece_kernel(
    n_uly, chunk, heads, count, quarters, last, docs, selected, q_ref, *refs
):
    pieces, (acc_ref, total_ref, top_ref, plain) = refs[:count], refs[count : count + 4]
    bias, s_ref, again = refs[-3:]
    rows, g = q_ref.shape[0], pl.program_id(0)
    blk, uly = lax.axis_index("blk"), lax.axis_index("uly")
    base = (blk * n_uly + uly) * rows
    source = selected[blk, chunk * heads + g]
    low = first_of(docs, base) - source * MB
    high = first_of(docs, base + rows - 1) - source * MB
    some = (source != blk) & (low < MB)
    fits = plain[g] == 1

    @pl.when(some & ((high > 0) | jnp.logical_not(fits)))
    def _():
        place = base + lax.broadcasted_iota(jnp.int32, (rows, 1), 0)
        limit = first_of(docs, place) - source * MB
        lane = lax.broadcasted_iota(jnp.int32, (rows, rows), 1)
        for i, j in enumerate(quarters):
            key = (uly ^ j) * rows + lane
            bias[:, i * rows : (i + 1) * rows] = jnp.where(key < limit, HIDDEN, 0.0)

    def loaded():
        halves = [columns_of(pieces, heads, half, chunk) for half in (0, 1)]
        return [group_queries(q_ref, chunk, heads), *halves]

    def total_of(h):
        return head_columns(total_ref, g * GROUP + h, 1)

    def acc_of(h):
        return head_columns(acc_ref, g * GROUP + h, 1)

    if last:
        out_ref = refs[-4]

        def give(h, acc, total):
            attended = acc * pl.reciprocal(total, approx=True)
            at = h * HD if isinstance(h, int) else pl.multiple_of(h * HD, HD)
            out_ref[:, pl.ds(at, HD)] = attended.astype(out_ref.dtype)

        def give_tops(tops, plainly):
            pass

    else:
        acc_out, total_out, top_out, plain_out = refs[-7:-3]

        def give(h, acc, total):
            at = pl.multiple_of((g * GROUP + h) * HD, HD)
            acc_out[:, pl.ds(at, HD)] = acc
            total_out[:, pl.ds(at, HD)] = total

        def give_tops(tops, plainly):
            top_out[:, pl.ds(pl.multiple_of(g * HD, HD), HD)] = tops
            plain_out[g] = plainly

    def add_plain(bias):
        acc, new = plain_attention(*loaded(), bias)
        for h in range(GROUP):
            here = slice(h * rows, (h + 1) * rows)
            give(h, acc[here] + acc_of(h), new[here] + total_of(h))
        give_tops(head_columns(top_ref, g, 1), 1)
        again[0] = jnp.logical_not(jnp.max(new) <= MOST).astype(jnp.int32)

    def add_shifted():
        tops = head_columns(top_ref, g, 1)
        lane = lax.broadcasted_iota(jnp.int32, (rows, HD), 1)
        give_tops(tops, 0)

        def use(h, vv):
            before = jnp.sum(jnp.where(lane == h, tops, 0.0), axis=1, keepdims=True)
            top = jnp.maximum(jnp.max(s_ref[...], axis=1, keepdims=True), before)
            p = jnp.exp2(s_ref[...] - top).astype(jnp.bfloat16)
            both = weighted(p, vv)
            keep = jnp.exp2(before - top)
            give(h, both[:, :HD] + keep * acc_of(h), both[:, HD:] + keep * total_of(h))
            if not last:
                give_tops(jnp.where(lane == h, top, head_columns(top_out, g, 1)), 0)

        keys, values = loaded()[1:]
        each_head(q_ref, first_query(chunk, heads), keys, values, s_ref, bias, use)

    again[0] = (some & jnp.logical_not(fits)).astype(jnp.int32)

    @pl.when(some & fits & (high <= 0))
    def _():
        add_plain(None)

    @pl.when(some & fits & (high > 0))
    def _():
        add_plain(bias)

    @pl.when((again[0] == 1) & (high <= 0) & fits)
    def _():
        bias[...] = jnp.zeros_like(bias)

    @pl.when(again[0] == 1)
    def _():
        add_shifted()

    @pl.when(jnp.logical_not(some))
    def _():
        for h in range(GROUP):
            give(h, acc_of(h), total_of(h))
        give_tops(head_columns(top_ref, g, 1), plain[g])


def chosen_pieces(scalars, n_uly, chunk, queries, pieces, kept, quarters, last, result=None):
    rows = queries.shape[0]
    heads = KVH // CHUNKS
    wide = GROUP * HD
    operands = [queries, *pieces, *kept]
    scalar_memory = pl.BlockSpec(memory_space=pltpu.SMEM)
    specs = [WHOLE] * (len(operands) - 1) + [scalar_memory]
    aliases = {}
    if last:
        out_specs = pl.BlockSpec((rows, wide), lambda g, *_: (0, chunk * heads + g))
        out_shape = jax.ShapeDtypeStruct((rows, HQ * HD), queries.dtype)
    else:
        out_specs = [WHOLE, WHOLE, WHOLE, scalar_memory]
        out_shape = [jax.ShapeDtypeStruct(a.shape, a.dtype) for a in kept]
    if result is not None:
        aliases = {SCALARS + len(operands): 0}
        operands.append(result)
        specs.append(pl.BlockSpec(memory_space=pl.ANY))
    return on_scalars(
        functools.partial(
            chosen_piece_kernel, n_uly, chunk, heads, len(pieces), quarters, last
        ),
        scalars,
        operands,
        specs,
        "chosen_block",
        grid=(heads,),
        out_specs=out_specs,
        scratch_shapes=[
            pltpu.VMEM((rows, len(quarters) * rows), jnp.float32),
            pltpu.VMEM((rows, len(quarters) * rows), jnp.float32),
            pltpu.SMEM((1,), jnp.int32),
        ],
        out_shape=out_shape,
        input_output_aliases=aliases,
    )


def up_line(part, chips, sources):
    return lax.ppermute(part, "blk", [(b, b + 2 * chips) for b in sources])


def across_chip(part, n_blk):
    return lax.ppermute(part, "blk", [(b, b ^ 1) for b in range(n_blk)])


def along(part, bit):
    return lax.ppermute(part, "uly", [(u, u ^ bit) for u in range(4)])


CHUNKS = 2


def by_permutes(n_blk, n_uly, queries, keys, values, doc_lengths, selected):
    scalars = (doc_lengths, selected)
    heads = KVH // CHUNKS
    chunks = range(CHUNKS)
    parts = [
        jnp.concatenate([a[:, c * heads * HD : (c + 1) * heads * HD] for a in (keys, values)], axis=1)
        for c in chunks
    ]
    hold = lax.optimization_barrier
    packed = jnp.concatenate(parts, axis=0)

    def lower_blocks(part):
        reach = range(1, n_blk // 2 - 1)
        return [part] + [up_line(part, k, range(n_blk - 2 - 2 * k)) for k in reach]

    def offer(c, held):
        return share(scalars, c, heads, n_blk, held)

    def take(c, held, offered):
        kept, upward = settle(scalars, c, heads, n_blk, held, across_chip(offered, n_blk))
        return kept, upward, up_line(upward, 1, range(n_blk - 4, n_blk - 2))

    def corner_parts(near, far):
        middle = near.shape[1] // 2
        return near[:, :middle], far[:, middle:]

    near, far = along(packed, 1), along(packed, 2)
    first = lower_blocks(parts[0])
    near, far, first, parts = hold((near, far, first, parts))
    corner = [along(part, 3) for part in parts]
    second = lower_blocks(parts[1])
    kept, upward, below = take(0, first, offer(0, first))
    asked, _ = hold((queries, upward))
    own = [[parts[c], near, far, corner[c]] for c in chunks]
    partial = [own_pieces(scalars, n_uly, 0, asked, own[0])]
    second, own[1], kept, below, partial[0] = hold((second, own[1], kept, below, partial[0]))
    offered = offer(1, second)
    kept, offered = hold((kept, offered))
    chosen = [finish(scalars, 0, heads, n_blk, kept, below)]
    near, far = along(chosen[0], 1), along(chosen[0], 2)
    kept, upward, below = take(1, second, offered)
    asked, _ = hold((queries, (upward, chosen)))
    partial.append(own_pieces(scalars, n_uly, 1, asked, own[1]))
    near, far, _ = hold((near, far, partial[1]))
    passed = corner_parts(near, far)
    gathered = [[chosen[0], near, far, along(passed[0], 2), along(passed[1], 1)]]
    kept, gathered[0] = hold((kept, gathered[0]))
    chosen.append(finish(scalars, 1, heads, n_blk, kept, below))
    near, far = along(chosen[1], 1), along(chosen[1], 2)
    result = chosen_pieces(
        scalars, n_uly, 0, queries, gathered[0], partial[0], (0, 1, 2, 3), True
    )
    near, far, result = hold((near, far, result))
    passed = corner_parts(near, far)
    asked, passed = hold((queries, passed))
    corner = [along(passed[0], 2), along(passed[1], 1)]
    partial[1] = chosen_pieces(
        scalars, n_uly, 1, asked, [chosen[1], near, far], partial[1], (0, 1, 2), False
    )
    return chosen_pieces(
        scalars, n_uly, 1, queries, corner, partial[1], (3,), True, result
    )


def on_device(n_blk, n_uly, queries, keys, values, doc_lengths, selected):
    rows = queries.shape[0]
    ndoc = doc_lengths.shape[0]
    per_dev = n_uly * rows // MB
    slices = MB // rows
    if per_dev == 1 and n_uly == 4 and n_blk % 2 == 0 and n_blk >= 4:
        return by_permutes(n_blk, n_uly, queries, keys, values, doc_lengths, selected)
    blk, uly = lax.axis_index("blk"), lax.axis_index("uly")
    mine = uly // slices
    block = blk * per_dev + mine
    ends = jnp.cumsum(doc_lengths)
    place = (blk * n_uly + uly) * rows
    picks = selected[block]
    wanted = jnp.where(picks == block, -1, picks)
    info = jnp.concatenate(
        [ends, jnp.stack([place, block, mine]), wanted, picks % per_dev]
    ).astype(jnp.int32)
    head_at = ndoc + 3
    row_at = head_at + KVH

    k_all = lax.all_gather(keys, "blk", axis=0, tiled=True)
    v_all = lax.all_gather(values, "blk", axis=0, tiled=True)
    k_own = lax.all_gather(keys, "uly", axis=0, tiled=True)
    v_own = lax.all_gather(values, "uly", axis=0, tiled=True)
    acc, stat = own_attention(info, ndoc, ndoc + 2, queries, k_own, v_own)

    k_sets, v_sets = [], []
    for row in range(per_dev):
        source = selected[blk * per_dev + row] // per_dev
        k_part, v_part = pick(source, k_all, v_all, rows)
        k_sets.append(lax.all_gather(k_part, "uly", axis=0, tiled=True))
        v_sets.append(lax.all_gather(v_part, "uly", axis=0, tiled=True))
    if per_dev == 1:
        k_chosen, v_chosen = k_sets[0], v_sets[0]
    else:
        k_chosen = lax.dynamic_index_in_dim(jnp.stack(k_sets), mine, 0, keepdims=False)
        v_chosen = lax.dynamic_index_in_dim(jnp.stack(v_sets), mine, 0, keepdims=False)
    return chosen_attention(info, ndoc, head_at, row_at, queries, k_chosen, v_chosen, acc, stat)


def solution(mesh):
    placed = (P(("blk", "uly"), None), P(("blk", "uly"), None), P(("blk", "uly"), None), P(), P())
    return jax.shard_map(
        functools.partial(on_device, mesh.shape["blk"], mesh.shape["uly"]),
        mesh=mesh,
        in_specs=placed,
        out_specs=P(("blk", "uly"), None),
        check_vma=False,
    )
```

```python
import functools

import jax
import jax.numpy as jnp
from jax import lax
from jax.experimental import pallas as pl
from jax.experimental.pallas import tpu as pltpu
from jax.sharding import PartitionSpec as P

HQ = 32
KVH = 8
HD = 128
MB = 1024
GROUP = HQ // KVH
LOG2E = 1.4426950408889634
HIDDEN = -1e30
LEAST, MOST = 2.0**-60, 2.0**100
VMEM = 24 * 1024 * 1024


def pick_kernel(info, k_ref, v_ref, k_out, v_out):
    k_out[...] = k_ref[...]
    v_out[...] = v_ref[...]


def pick(source, k_all, v_all, rows):
    spec = pl.BlockSpec((rows, HD), lambda g, info: (info[g], g))
    out = pl.BlockSpec((rows, HD), lambda g, info: (0, g))
    shape = jax.ShapeDtypeStruct((rows, KVH * HD), k_all.dtype)
    return pl.pallas_call(
        pick_kernel,
        grid_spec=pltpu.PrefetchScalarGridSpec(
            num_scalar_prefetch=1, grid=(KVH,), in_specs=[spec, spec], out_specs=[out, out]
        ),
        out_shape=[shape, shape],
        cost_estimate=pl.CostEstimate(
            flops=0, bytes_accessed=4 * rows * KVH * HD * 2, transcendentals=0
        ),
        name="pick",
    )(source, k_all, v_all)


def starts_of(info, ndoc, places):
    first = jnp.zeros_like(places)
    for d in range(ndoc):
        end = info[d]
        first = jnp.maximum(first, jnp.where(end <= places, end, 0))
    return first


def split_query(q):
    scaled = q.astype(jnp.float32) * (LOG2E / HD**0.5)
    high = scaled.astype(jnp.bfloat16)
    low = (scaled - high.astype(jnp.float32)).astype(jnp.bfloat16)
    return jnp.concatenate([high, low], axis=1)


def doubled(k):
    return jnp.concatenate([k, k], axis=1)


def with_ones(v):
    return jnp.concatenate([v, jnp.ones_like(v)], axis=1)


def own_kernel(ndoc, info, q_ref, k_ref, v_ref, acc_ref, stat_ref, bias):
    rows = q_ref.shape[0]

    @pl.when(pl.program_id(0) == 0)
    def _():
        base = info[ndoc]
        place = base + lax.broadcasted_iota(jnp.int32, (rows, 1), 0)
        first = starts_of(info, ndoc, place)
        key = info[ndoc + 1] * MB + lax.broadcasted_iota(jnp.int32, (rows, MB), 1)
        bias[...] = jnp.where((key <= place) & (key >= first), 0.0, HIDDEN)

    kk = doubled(k_ref[...])
    vv = with_ones(v_ref[...])
    lane = lax.broadcasted_iota(jnp.int32, (rows, HD), 1)
    stat = jnp.zeros((rows, HD), jnp.float32)
    for h in range(GROUP):
        cols = slice(h * HD, (h + 1) * HD)
        qq = split_query(q_ref[:, cols])
        s = lax.dot_general(qq, kk, (((1,), (1,)), ((), ())), preferred_element_type=jnp.float32)
        s = s + bias[...]
        top = jnp.max(s, axis=1, keepdims=True)
        p = jnp.exp2(s - top).astype(jnp.bfloat16)
        both = lax.dot_general(p, vv, (((1,), (0,)), ((), ())), preferred_element_type=jnp.float32)
        acc_ref[:, cols] = both[:, :HD]
        stat = jnp.where(lane == h, top, stat)
        stat = jnp.where(lane == GROUP + h, both[:, HD:], stat)
    stat_ref[...] = stat


def own_attention(info, ndoc, own_row, queries, k_own, v_own):
    rows = queries.shape[0]
    wide = GROUP * HD
    per_head = lambda g, info: (0, g)
    kv = pl.BlockSpec((MB, HD), lambda g, info: (info[own_row], g))
    return pl.pallas_call(
        functools.partial(own_kernel, ndoc),
        grid_spec=pltpu.PrefetchScalarGridSpec(
            num_scalar_prefetch=1,
            grid=(KVH,),
            in_specs=[pl.BlockSpec((rows, wide), per_head), kv, kv],
            out_specs=[pl.BlockSpec((rows, wide), per_head), pl.BlockSpec((rows, HD), per_head)],
            scratch_shapes=[pltpu.VMEM((rows, MB), jnp.float32)],
        ),
        out_shape=[
            jax.ShapeDtypeStruct((rows, HQ * HD), jnp.float32),
            jax.ShapeDtypeStruct((rows, KVH * HD), jnp.float32),
        ],
        compiler_params=pltpu.CompilerParams(vmem_limit_bytes=VMEM),
        cost_estimate=pl.CostEstimate(
            flops=8 * rows * MB * HQ * HD, bytes_accessed=12 << 20, transcendentals=rows * MB * HQ
        ),
        name="own_block",
    )(info, queries, k_own, v_own)


def chosen_kernel(ndoc, head_at, info, q_ref, k_ref, v_ref, acc_ref, stat_ref, out_ref):
    rows = q_ref.shape[0]
    base = info[ndoc]
    source = info[head_at + pl.program_id(0)]

    def bound(place):
        first = jnp.int32(0)
        for d in range(ndoc):
            first = jnp.maximum(first, jnp.where(info[d] <= place, info[d], 0))
        return first - source * MB

    low, high = bound(base), bound(base + rows - 1)
    live = source >= 0

    def merge(masked):
        kk = doubled(k_ref[...])
        vv = with_ones(v_ref[...])
        stat = stat_ref[...]
        if masked:
            place = base + lax.broadcasted_iota(jnp.int32, (rows, 1), 0)
            limit = starts_of(info, ndoc, place) - source * MB
            key = lax.broadcasted_iota(jnp.int32, (rows, MB), 1)
            hide = key < limit
        for h in range(GROUP):
            cols = slice(h * HD, (h + 1) * HD)
            qq = split_query(q_ref[:, cols])
            s = lax.dot_general(
                qq, kk, (((1,), (1,)), ((), ())), preferred_element_type=jnp.float32
            )
            if masked:
                s = jnp.where(hide, HIDDEN, s)
            before = stat[:, h : h + 1]
            top = jnp.maximum(jnp.max(s, axis=1, keepdims=True), before)
            p = jnp.exp2(s - top).astype(jnp.bfloat16)
            both = lax.dot_general(
                p, vv, (((1,), (0,)), ((), ())), preferred_element_type=jnp.float32
            )
            keep = jnp.exp2(before - top)
            total = both[:, HD:] + keep * stat[:, GROUP + h : GROUP + h + 1]
            acc = both[:, :HD] + keep * acc_ref[:, cols]
            out_ref[:, cols] = (acc / total).astype(out_ref.dtype)

    some = live & (low < MB)

    @pl.when(some & (high <= 0))
    def _():
        merge(False)

    @pl.when(some & (high > 0))
    def _():
        merge(True)

    @pl.when(jnp.logical_not(some))
    def _():
        stat = stat_ref[...]
        for h in range(GROUP):
            cols = slice(h * HD, (h + 1) * HD)
            total = stat[:, GROUP + h : GROUP + h + 1]
            out_ref[:, cols] = (acc_ref[:, cols] / total).astype(out_ref.dtype)


def chosen_attention(info, ndoc, head_at, row_at, queries, k_chosen, v_chosen, acc, stat):
    rows = queries.shape[0]
    wide = GROUP * HD
    per_head = lambda g, info: (0, g)
    kv = pl.BlockSpec((MB, HD), lambda g, info: (info[row_at + g], g))
    return pl.pallas_call(
        functools.partial(chosen_kernel, ndoc, head_at),
        grid_spec=pltpu.PrefetchScalarGridSpec(
            num_scalar_prefetch=1,
            grid=(KVH,),
            in_specs=[
                pl.BlockSpec((rows, wide), per_head),
                kv,
                kv,
                pl.BlockSpec((rows, wide), per_head),
                pl.BlockSpec((rows, HD), per_head),
            ],
            out_specs=pl.BlockSpec((rows, wide), per_head),
        ),
        out_shape=jax.ShapeDtypeStruct((rows, HQ * HD), queries.dtype),
        compiler_params=pltpu.CompilerParams(vmem_limit_bytes=VMEM),
        cost_estimate=pl.CostEstimate(
            flops=8 * rows * MB * HQ * HD, bytes_accessed=14 << 20, transcendentals=rows * MB * HQ
        ),
        name="chosen_block",
    )(info, queries, k_chosen, v_chosen, acc, stat)


SCALARS = 2
WHOLE = pl.BlockSpec(memory_space=pltpu.VMEM)


def on_scalars(kernel, scalars, operands, in_specs, name, grid=(1,), **call):
    out_specs, scratch = call.pop("out_specs"), call.pop("scratch_shapes", ())
    return pl.pallas_call(
        kernel,
        grid_spec=pltpu.PrefetchScalarGridSpec(
            num_scalar_prefetch=SCALARS,
            grid=grid,
            in_specs=in_specs,
            out_specs=out_specs,
            scratch_shapes=scratch,
        ),
        compiler_params=pltpu.CompilerParams(vmem_limit_bytes=VMEM),
        cost_estimate=pl.CostEstimate(flops=1, bytes_accessed=1, transcendentals=0),
        name=name,
        **call,
    )(*scalars, *operands)


def copy_head(out, at, source, source_at, heads, g):
    rows = source.shape[0] if source_at is None else source_at[1]
    take = slice(None) if source_at is None else slice(source_at[0], source_at[0] + rows)
    for half in (g, heads + g):
        cols = slice(half * HD, (half + 1) * HD)
        out[at : at + rows, cols] = source[take, cols]


def copy_held(out, at, held, back, heads, g, usable):
    for step in range(len(held)):
        here = back == 2 * step
        if step == len(held) - 1:
            here = here | (back > 2 * step)

        @pl.when(here & usable)
        def _(step=step):
            copy_head(out, at, held[step], None, heads, g)


def share_kernel(chunk, heads, n_blk, docs, selected, *refs):
    *held, out = refs
    rows = held[0].shape[0]
    blk = lax.axis_index("blk")
    other = blk ^ 1
    above = jnp.minimum(other + 2, n_blk - 1)
    for at, consumer in ((0, other), (rows, above)):
        for g in range(heads):
            back = blk - selected[consumer, chunk * heads + g]
            usable = (back >= 0) & (back % 2 == 0)
            copy_held(out, at, held, back, heads, g, usable)

            @pl.when(jnp.logical_not(usable))
            def _():
                copy_head(out, at, held[0], None, heads, g)


def share(scalars, chunk, heads, n_blk, held):
    rows, wide = held[0].shape
    return on_scalars(
        functools.partial(share_kernel, chunk, heads, n_blk),
        scalars,
        held,
        [WHOLE] * len(held),
        "share",
        out_specs=WHOLE,
        out_shape=jax.ShapeDtypeStruct((2 * rows, wide), held[0].dtype),
    )


def settle_kernel(chunk, heads, n_blk, docs, selected, *refs):
    *held, passed, mine, upward = refs
    rows = mine.shape[0]
    blk = lax.axis_index("blk")
    above = jnp.minimum(blk + 2, n_blk - 1)
    for at, consumer, out in ((0, blk, mine), (rows, above, upward)):
        for g in range(heads):
            back = blk - selected[consumer, chunk * heads + g]
            usable = (back >= 0) & (back % 2 == 0)
            copy_held(out, 0, held, back, heads, g, usable)

            @pl.when(jnp.logical_not(usable))
            def _():
                copy_head(out, 0, passed, (at, rows), heads, g)


def settle(scalars, chunk, heads, n_blk, held, passed):
    rows, wide = held[0].shape
    shape = jax.ShapeDtypeStruct((rows, wide), held[0].dtype)
    return on_scalars(
        functools.partial(settle_kernel, chunk, heads, n_blk),
        scalars,
        [*held, passed],
        [WHOLE] * (len(held) + 1),
        "settle",
        out_specs=[WHOLE] * 2,
        out_shape=[shape, shape],
    )


def finish_kernel(chunk, heads, n_blk, docs, selected, mine, below, out):
    blk = lax.axis_index("blk")
    for g in range(heads):
        arrived = (blk >= n_blk - 2) & (selected[blk, chunk * heads + g] < n_blk - 2)

        @pl.when(arrived)
        def _():
            copy_head(out, 0, below, None, heads, g)

        @pl.when(jnp.logical_not(arrived))
        def _():
            copy_head(out, 0, mine, None, heads, g)


def finish(scalars, chunk, heads, n_blk, mine, below):
    return on_scalars(
        functools.partial(finish_kernel, chunk, heads, n_blk),
        scalars,
        [mine, below],
        [WHOLE] * 2,
        "finish",
        out_specs=WHOLE,
        out_shape=jax.ShapeDtypeStruct(mine.shape, mine.dtype),
    )


def first_of(docs, place):
    end = jnp.int32(0)
    first = jnp.zeros_like(place)
    for d in range(docs.shape[0]):
        end = end + docs[d]
        first = jnp.maximum(first, jnp.where(end <= place, end, 0))
    return first


def scores(qq, kk):
    return lax.dot_general(qq, kk, (((1,), (1,)), ((), ())), preferred_element_type=jnp.float32)


def weighted(p, vv):
    return lax.dot_general(p, vv, (((1,), (0,)), ((), ())), preferred_element_type=jnp.float32)


def head_columns(ref, first, count):
    return ref[:, pl.ds(pl.multiple_of(first * HD, HD), count * HD)]


def columns_of(pieces, heads, half, chunk, g):
    found = []
    halves = [piece for piece in pieces if piece.shape[1] == heads * HD]
    for piece in [piece for piece in pieces if piece.shape[1] > heads * HD] + halves[half : half + 1]:
        rows = MB // 4
        at = chunk * rows if piece.shape[0] > rows else 0
        first = g + (half * heads if piece.shape[1] > heads * HD else 0)
        found.append(head_columns(piece.at[pl.ds(at, rows)], first, 1))
    return jnp.concatenate(found, axis=0)


def each_head(q_ref, first, keys, values, s_ref, bias, use):
    kk, vv = doubled(keys), with_ones(values)

    def body(h, carry):
        s_ref[...] = scores(split_query(head_columns(q_ref, first + h, 1)), kk) + bias[...]
        use(h, vv)
        return carry

    lax.fori_loop(0, GROUP, body, 0)


def plain_attention(queries, keys, values, bias):
    q = jnp.concatenate(queries, axis=0)
    tile = 2 * HD
    weights = []
    for at in range(0, keys.shape[0], tile):
        s = scores(q, keys[at : at + tile]) * (LOG2E / HD**0.5)
        if bias is not None:
            s = s + jnp.concatenate([bias[:, at : at + tile]] * GROUP, axis=0)
        weights.append(jnp.exp2(s).astype(jnp.bfloat16))
    both = weighted(jnp.concatenate(weights, axis=1), with_ones(values))
    return both[:, :HD], both[:, HD:]


def first_query(chunk, heads, g):
    return (chunk * heads + g) * GROUP


def group_queries(q_ref, chunk, heads, g):
    return [head_columns(q_ref, first_query(chunk, heads, g) + h, 1) for h in range(GROUP)]


def each_key_head(heads, work):
    def body(g, carry):
        work(g)
        return carry

    lax.fori_loop(0, heads, body, 0)


def own_piece_kernel(n_uly, chunk, heads, count, docs, selected, q_ref, *refs):
    pieces, (acc_ref, total_ref, top_ref, plain, bias, s_ref) = refs[:count], refs[count:]
    rows = q_ref.shape[0]
    blk, uly = lax.axis_index("blk"), lax.axis_index("uly")
    place = (blk * n_uly + uly) * rows + lax.broadcasted_iota(jnp.int32, (rows, 1), 0)
    first = first_of(docs, place)
    lane = lax.broadcasted_iota(jnp.int32, (rows, rows), 1)
    for j in range(MB // rows):
        key = blk * MB + (uly ^ j) * rows + lane
        bias[:, j * rows : (j + 1) * rows] = jnp.where(
            (key <= place) & (key >= first), 0.0, HIDDEN
        )


    def work(g):
        queries = group_queries(q_ref, chunk, heads, g)
        keys, values = (columns_of(pieces, heads, half, chunk, g) for half in (0, 1))
        lane = lax.broadcasted_iota(jnp.int32, (rows, HD), 1)

        def keep(h, acc, total):
            at = pl.multiple_of((g * GROUP + h) * HD, HD)
            acc_ref[:, pl.ds(at, HD)] = acc
            total_ref[:, pl.ds(at, HD)] = total

        def keep_tops(tops):
            top_ref[:, pl.ds(pl.multiple_of(g * HD, HD), HD)] = tops

        acc, total = plain_attention(queries, keys, values, bias)
        for h in range(GROUP):
            keep(h, acc[h * rows : (h + 1) * rows], total[h * rows : (h + 1) * rows])
        keep_tops(jnp.zeros((rows, HD), jnp.float32))
        fits = (jnp.min(total) >= LEAST) & (jnp.max(total) <= MOST)
        plain[g] = fits.astype(jnp.int32)

        @pl.when(jnp.logical_not(fits))
        def _():
            def use(h, vv):
                top = jnp.max(s_ref[...], axis=1, keepdims=True)
                p = jnp.exp2(s_ref[...] - top).astype(jnp.bfloat16)
                both = weighted(p, vv)
                keep(h, both[:, :HD], both[:, HD:])
                keep_tops(jnp.where(lane == h, top, head_columns(top_ref, g, 1)))

            each_head(q_ref, first_query(chunk, heads, g), keys, values, s_ref, bias, use)

    each_key_head(heads, work)


def own_pieces(scalars, n_uly, chunk, queries, pieces):
    rows = queries.shape[0]
    heads = KVH // CHUNKS
    return on_scalars(
        functools.partial(own_piece_kernel, n_uly, chunk, heads, len(pieces)),
        scalars,
        [queries, *pieces],
        [WHOLE] * (1 + len(pieces)),
        "own_block",
        out_specs=[WHOLE, WHOLE, WHOLE, pl.BlockSpec(memory_space=pltpu.SMEM)],
        scratch_shapes=[
            pltpu.VMEM((rows, MB), jnp.float32),
            pltpu.VMEM((rows, MB), jnp.float32),
        ],
        out_shape=[
            jax.ShapeDtypeStruct((rows, heads * GROUP * HD), jnp.float32),
            jax.ShapeDtypeStruct((rows, heads * GROUP * HD), jnp.float32),
            jax.ShapeDtypeStruct((rows, heads * HD), jnp.float32),
            jax.ShapeDtypeStruct((heads,), jnp.int32),
        ],
    )


def chosen_piece_kernel(
    n_uly, chunk, heads, count, quarters, last, docs, selected, q_ref, *refs
):
    pieces, (acc_ref, total_ref, top_ref, plain) = refs[:count], refs[count : count + 4]
    bias, s_ref, again = refs[-3:]
    rows = q_ref.shape[0]
    blk, uly = lax.axis_index("blk"), lax.axis_index("uly")
    base = (blk * n_uly + uly) * rows

    def work(g):
        source = selected[blk, chunk * heads + g]
        low = first_of(docs, base) - source * MB
        high = first_of(docs, base + rows - 1) - source * MB
        some = (source != blk) & (low < MB)
        fits = plain[g] == 1

        @pl.when(some & ((high > 0) | jnp.logical_not(fits)))
        def _():
            place = base + lax.broadcasted_iota(jnp.int32, (rows, 1), 0)
            limit = first_of(docs, place) - source * MB
            lane = lax.broadcasted_iota(jnp.int32, (rows, rows), 1)
            for i, j in enumerate(quarters):
                key = (uly ^ j) * rows + lane
                bias[:, i * rows : (i + 1) * rows] = jnp.where(key < limit, HIDDEN, 0.0)

        def loaded():
            halves = [columns_of(pieces, heads, half, chunk, g) for half in (0, 1)]
            return [group_queries(q_ref, chunk, heads, g), *halves]

        def total_of(h):
            return head_columns(total_ref, g * GROUP + h, 1)

        def acc_of(h):
            return head_columns(acc_ref, g * GROUP + h, 1)

        if last:
            out_ref = refs[-4]

            def give(h, acc, total):
                attended = acc * pl.reciprocal(total, approx=True)
                at = pl.multiple_of((g * GROUP + h) * HD, HD)
                out_ref[:, pl.ds(at, HD)] = attended.astype(out_ref.dtype)

            def give_tops(tops, plainly):
                pass

        else:
            acc_out, total_out, top_out, plain_out = refs[-7:-3]

            def give(h, acc, total):
                at = pl.multiple_of((g * GROUP + h) * HD, HD)
                acc_out[:, pl.ds(at, HD)] = acc
                total_out[:, pl.ds(at, HD)] = total

            def give_tops(tops, plainly):
                top_out[:, pl.ds(pl.multiple_of(g * HD, HD), HD)] = tops
                plain_out[g] = plainly

        def add_plain(bias):
            acc, new = plain_attention(*loaded(), bias)
            for h in range(GROUP):
                here = slice(h * rows, (h + 1) * rows)
                give(h, acc[here] + acc_of(h), new[here] + total_of(h))
            give_tops(head_columns(top_ref, g, 1), 1)
            again[0] = jnp.logical_not(jnp.max(new) <= MOST).astype(jnp.int32)

        def add_shifted():
            tops = head_columns(top_ref, g, 1)
            lane = lax.broadcasted_iota(jnp.int32, (rows, HD), 1)
            give_tops(tops, 0)

            def use(h, vv):
                before = jnp.sum(jnp.where(lane == h, tops, 0.0), axis=1, keepdims=True)
                top = jnp.maximum(jnp.max(s_ref[...], axis=1, keepdims=True), before)
                p = jnp.exp2(s_ref[...] - top).astype(jnp.bfloat16)
                both = weighted(p, vv)
                keep = jnp.exp2(before - top)
                give(h, both[:, :HD] + keep * acc_of(h), both[:, HD:] + keep * total_of(h))
                if not last:
                    give_tops(jnp.where(lane == h, top, head_columns(top_out, g, 1)), 0)

            keys, values = loaded()[1:]
            each_head(q_ref, first_query(chunk, heads, g), keys, values, s_ref, bias, use)

        again[0] = (some & jnp.logical_not(fits)).astype(jnp.int32)

        @pl.when(some & fits & (high <= 0))
        def _():
            add_plain(None)

        @pl.when(some & fits & (high > 0))
        def _():
            add_plain(bias)

        @pl.when((again[0] == 1) & (high <= 0) & fits)
        def _():
            bias[...] = jnp.zeros_like(bias)

        @pl.when(again[0] == 1)
        def _():
            add_shifted()

        @pl.when(jnp.logical_not(some))
        def _():
            for h in range(GROUP):
                give(h, acc_of(h), total_of(h))
            give_tops(head_columns(top_ref, g, 1), plain[g])

    each_key_head(heads, work)


def chosen_pieces(scalars, n_uly, chunk, queries, pieces, kept, quarters, last, result=None):
    rows = queries.shape[0]
    heads = KVH // CHUNKS
    wide = GROUP * HD
    operands = [queries, *pieces, *kept]
    scalar_memory = pl.BlockSpec(memory_space=pltpu.SMEM)
    specs = [WHOLE] * (len(operands) - 1) + [scalar_memory]
    aliases = {}
    if last:
        out_specs = pl.BlockSpec((rows, heads * wide), lambda i, *_: (0, chunk))
        out_shape = jax.ShapeDtypeStruct((rows, HQ * HD), queries.dtype)
    else:
        out_specs = [WHOLE, WHOLE, WHOLE, scalar_memory]
        out_shape = [jax.ShapeDtypeStruct(a.shape, a.dtype) for a in kept]
    if result is not None:
        aliases = {SCALARS + len(operands): 0}
        operands.append(result)
        specs.append(pl.BlockSpec(memory_space=pl.ANY))
    return on_scalars(
        functools.partial(
            chosen_piece_kernel, n_uly, chunk, heads, len(pieces), quarters, last
        ),
        scalars,
        operands,
        specs,
        "chosen_block",
        out_specs=out_specs,
        scratch_shapes=[
            pltpu.VMEM((rows, len(quarters) * rows), jnp.float32),
            pltpu.VMEM((rows, len(quarters) * rows), jnp.float32),
            pltpu.SMEM((1,), jnp.int32),
        ],
        out_shape=out_shape,
        input_output_aliases=aliases,
    )


def up_line(part, chips, sources):
    return lax.ppermute(part, "blk", [(b, b + 2 * chips) for b in sources])


def across_chip(part, n_blk):
    return lax.ppermute(part, "blk", [(b, b ^ 1) for b in range(n_blk)])


def along(part, bit):
    return lax.ppermute(part, "uly", [(u, u ^ bit) for u in range(4)])


CHUNKS = 2


def by_permutes(n_blk, n_uly, queries, keys, values, doc_lengths, selected):
    scalars = (doc_lengths, selected)
    heads = KVH // CHUNKS
    chunks = range(CHUNKS)
    parts = [
        jnp.concatenate([a[:, c * heads * HD : (c + 1) * heads * HD] for a in (keys, values)], axis=1)
        for c in chunks
    ]
    hold = lax.optimization_barrier
    packed = jnp.concatenate(parts, axis=0)

    def lower_blocks(part):
        reach = range(1, n_blk // 2 - 1)
        return [part] + [up_line(part, k, range(n_blk - 2 - 2 * k)) for k in reach]

    def offer(c, held):
        return share(scalars, c, heads, n_blk, held)

    def take(c, held, offered):
        kept, upward = settle(scalars, c, heads, n_blk, held, across_chip(offered, n_blk))
        return kept, upward, up_line(upward, 1, range(n_blk - 4, n_blk - 2))

    def corner_parts(near, far):
        middle = near.shape[1] // 2
        return near[:, :middle], far[:, middle:]

    near, far = along(packed, 1), along(packed, 2)
    first = lower_blocks(parts[0])
    near, far, first, parts = hold((near, far, first, parts))
    corner = [along(part, 3) for part in parts]
    second = lower_blocks(parts[1])
    kept, upward, below = take(0, first, offer(0, first))
    asked, _ = hold((queries, upward))
    own = [[parts[c], near, far, corner[c]] for c in chunks]
    partial = [own_pieces(scalars, n_uly, 0, asked, own[0])]
    second, own[1], kept, below, partial[0] = hold((second, own[1], kept, below, partial[0]))
    offered = offer(1, second)
    kept, offered = hold((kept, offered))
    chosen = [finish(scalars, 0, heads, n_blk, kept, below)]
    near, far = along(chosen[0], 1), along(chosen[0], 2)
    kept, upward, below = take(1, second, offered)
    asked, _ = hold((queries, (upward, chosen)))
    partial.append(own_pieces(scalars, n_uly, 1, asked, own[1]))
    near, far, _ = hold((near, far, partial[1]))
    passed = corner_parts(near, far)
    gathered = [[chosen[0], near, far, along(passed[0], 2), along(passed[1], 1)]]
    kept, gathered[0] = hold((kept, gathered[0]))
    chosen.append(finish(scalars, 1, heads, n_blk, kept, below))
    near, far = along(chosen[1], 1), along(chosen[1], 2)
    result = chosen_pieces(
        scalars, n_uly, 0, queries, gathered[0], partial[0], (0, 1, 2, 3), True
    )
    near, far, result = hold((near, far, result))
    passed = corner_parts(near, far)
    asked, passed = hold((queries, passed))
    corner = [along(passed[0], 2), along(passed[1], 1)]
    partial[1] = chosen_pieces(
        scalars, n_uly, 1, asked, [chosen[1], near, far], partial[1], (0, 1, 2), False
    )
    return chosen_pieces(
        scalars, n_uly, 1, queries, corner, partial[1], (3,), True, result
    )


def on_device(n_blk, n_uly, queries, keys, values, doc_lengths, selected):
    rows = queries.shape[0]
    ndoc = doc_lengths.shape[0]
    per_dev = n_uly * rows // MB
    slices = MB // rows
    if per_dev == 1 and n_uly == 4 and n_blk % 2 == 0 and n_blk >= 4:
        return by_permutes(n_blk, n_uly, queries, keys, values, doc_lengths, selected)
    blk, uly = lax.axis_index("blk"), lax.axis_index("uly")
    mine = uly // slices
    block = blk * per_dev + mine
    ends = jnp.cumsum(doc_lengths)
    place = (blk * n_uly + uly) * rows
    picks = selected[block]
    wanted = jnp.where(picks == block, -1, picks)
    info = jnp.concatenate(
        [ends, jnp.stack([place, block, mine]), wanted, picks % per_dev]
    ).astype(jnp.int32)
    head_at = ndoc + 3
    row_at = head_at + KVH

    k_all = lax.all_gather(keys, "blk", axis=0, tiled=True)
    v_all = lax.all_gather(values, "blk", axis=0, tiled=True)
    k_own = lax.all_gather(keys, "uly", axis=0, tiled=True)
    v_own = lax.all_gather(values, "uly", axis=0, tiled=True)
    acc, stat = own_attention(info, ndoc, ndoc + 2, queries, k_own, v_own)

    k_sets, v_sets = [], []
    for row in range(per_dev):
        source = selected[blk * per_dev + row] // per_dev
        k_part, v_part = pick(source, k_all, v_all, rows)
        k_sets.append(lax.all_gather(k_part, "uly", axis=0, tiled=True))
        v_sets.append(lax.all_gather(v_part, "uly", axis=0, tiled=True))
    if per_dev == 1:
        k_chosen, v_chosen = k_sets[0], v_sets[0]
    else:
        k_chosen = lax.dynamic_index_in_dim(jnp.stack(k_sets), mine, 0, keepdims=False)
        v_chosen = lax.dynamic_index_in_dim(jnp.stack(v_sets), mine, 0, keepdims=False)
    return chosen_attention(info, ndoc, head_at, row_at, queries, k_chosen, v_chosen, acc, stat)


def solution(mesh):
    placed = (P(("blk", "uly"), None), P(("blk", "uly"), None), P(("blk", "uly"), None), P(), P())
    return jax.shard_map(
        functools.partial(on_device, mesh.shape["blk"], mesh.shape["uly"]),
        mesh=mesh,
        in_specs=placed,
        out_specs=P(("blk", "uly"), None),
        check_vma=False,
    )
```

```python
import functools

import jax
import jax.numpy as jnp
from jax import lax
from jax.experimental import pallas as pl
from jax.experimental.pallas import tpu as pltpu
from jax.sharding import PartitionSpec as P

HQ = 32
KVH = 8
HD = 128
MB = 1024
GROUP = HQ // KVH
LOG2E = 1.4426950408889634
HIDDEN = -1e30
LEAST, MOST = 2.0**-60, 2.0**100
VMEM = 24 * 1024 * 1024


def pick_kernel(info, k_ref, v_ref, k_out, v_out):
    k_out[...] = k_ref[...]
    v_out[...] = v_ref[...]


def pick(source, k_all, v_all, rows):
    spec = pl.BlockSpec((rows, HD), lambda g, info: (info[g], g))
    out = pl.BlockSpec((rows, HD), lambda g, info: (0, g))
    shape = jax.ShapeDtypeStruct((rows, KVH * HD), k_all.dtype)
    return pl.pallas_call(
        pick_kernel,
        grid_spec=pltpu.PrefetchScalarGridSpec(
            num_scalar_prefetch=1, grid=(KVH,), in_specs=[spec, spec], out_specs=[out, out]
        ),
        out_shape=[shape, shape],
        cost_estimate=pl.CostEstimate(
            flops=0, bytes_accessed=4 * rows * KVH * HD * 2, transcendentals=0
        ),
        name="pick",
    )(source, k_all, v_all)


def starts_of(info, ndoc, places):
    first = jnp.zeros_like(places)
    for d in range(ndoc):
        end = info[d]
        first = jnp.maximum(first, jnp.where(end <= places, end, 0))
    return first


def split_query(q):
    scaled = q.astype(jnp.float32) * (LOG2E / HD**0.5)
    high = scaled.astype(jnp.bfloat16)
    low = (scaled - high.astype(jnp.float32)).astype(jnp.bfloat16)
    return jnp.concatenate([high, low], axis=1)


def doubled(k):
    return jnp.concatenate([k, k], axis=1)


def with_ones(v):
    return jnp.concatenate([v, jnp.ones_like(v)], axis=1)


def own_kernel(ndoc, info, q_ref, k_ref, v_ref, acc_ref, stat_ref, bias):
    rows = q_ref.shape[0]

    @pl.when(pl.program_id(0) == 0)
    def _():
        base = info[ndoc]
        place = base + lax.broadcasted_iota(jnp.int32, (rows, 1), 0)
        first = starts_of(info, ndoc, place)
        key = info[ndoc + 1] * MB + lax.broadcasted_iota(jnp.int32, (rows, MB), 1)
        bias[...] = jnp.where((key <= place) & (key >= first), 0.0, HIDDEN)

    kk = doubled(k_ref[...])
    vv = with_ones(v_ref[...])
    lane = lax.broadcasted_iota(jnp.int32, (rows, HD), 1)
    stat = jnp.zeros((rows, HD), jnp.float32)
    for h in range(GROUP):
        cols = slice(h * HD, (h + 1) * HD)
        qq = split_query(q_ref[:, cols])
        s = lax.dot_general(qq, kk, (((1,), (1,)), ((), ())), preferred_element_type=jnp.float32)
        s = s + bias[...]
        top = jnp.max(s, axis=1, keepdims=True)
        p = jnp.exp2(s - top).astype(jnp.bfloat16)
        both = lax.dot_general(p, vv, (((1,), (0,)), ((), ())), preferred_element_type=jnp.float32)
        acc_ref[:, cols] = both[:, :HD]
        stat = jnp.where(lane == h, top, stat)
        stat = jnp.where(lane == GROUP + h, both[:, HD:], stat)
    stat_ref[...] = stat


def own_attention(info, ndoc, own_row, queries, k_own, v_own):
    rows = queries.shape[0]
    wide = GROUP * HD
    per_head = lambda g, info: (0, g)
    kv = pl.BlockSpec((MB, HD), lambda g, info: (info[own_row], g))
    return pl.pallas_call(
        functools.partial(own_kernel, ndoc),
        grid_spec=pltpu.PrefetchScalarGridSpec(
            num_scalar_prefetch=1,
            grid=(KVH,),
            in_specs=[pl.BlockSpec((rows, wide), per_head), kv, kv],
            out_specs=[pl.BlockSpec((rows, wide), per_head), pl.BlockSpec((rows, HD), per_head)],
            scratch_shapes=[pltpu.VMEM((rows, MB), jnp.float32)],
        ),
        out_shape=[
            jax.ShapeDtypeStruct((rows, HQ * HD), jnp.float32),
            jax.ShapeDtypeStruct((rows, KVH * HD), jnp.float32),
        ],
        compiler_params=pltpu.CompilerParams(vmem_limit_bytes=VMEM),
        cost_estimate=pl.CostEstimate(
            flops=8 * rows * MB * HQ * HD, bytes_accessed=12 << 20, transcendentals=rows * MB * HQ
        ),
        name="own_block",
    )(info, queries, k_own, v_own)


def chosen_kernel(ndoc, head_at, info, q_ref, k_ref, v_ref, acc_ref, stat_ref, out_ref):
    rows = q_ref.shape[0]
    base = info[ndoc]
    source = info[head_at + pl.program_id(0)]

    def bound(place):
        first = jnp.int32(0)
        for d in range(ndoc):
            first = jnp.maximum(first, jnp.where(info[d] <= place, info[d], 0))
        return first - source * MB

    low, high = bound(base), bound(base + rows - 1)
    live = source >= 0

    def merge(masked):
        kk = doubled(k_ref[...])
        vv = with_ones(v_ref[...])
        stat = stat_ref[...]
        if masked:
            place = base + lax.broadcasted_iota(jnp.int32, (rows, 1), 0)
            limit = starts_of(info, ndoc, place) - source * MB
            key = lax.broadcasted_iota(jnp.int32, (rows, MB), 1)
            hide = key < limit
        for h in range(GROUP):
            cols = slice(h * HD, (h + 1) * HD)
            qq = split_query(q_ref[:, cols])
            s = lax.dot_general(
                qq, kk, (((1,), (1,)), ((), ())), preferred_element_type=jnp.float32
            )
            if masked:
                s = jnp.where(hide, HIDDEN, s)
            before = stat[:, h : h + 1]
            top = jnp.maximum(jnp.max(s, axis=1, keepdims=True), before)
            p = jnp.exp2(s - top).astype(jnp.bfloat16)
            both = lax.dot_general(
                p, vv, (((1,), (0,)), ((), ())), preferred_element_type=jnp.float32
            )
            keep = jnp.exp2(before - top)
            total = both[:, HD:] + keep * stat[:, GROUP + h : GROUP + h + 1]
            acc = both[:, :HD] + keep * acc_ref[:, cols]
            out_ref[:, cols] = (acc / total).astype(out_ref.dtype)

    some = live & (low < MB)

    @pl.when(some & (high <= 0))
    def _():
        merge(False)

    @pl.when(some & (high > 0))
    def _():
        merge(True)

    @pl.when(jnp.logical_not(some))
    def _():
        stat = stat_ref[...]
        for h in range(GROUP):
            cols = slice(h * HD, (h + 1) * HD)
            total = stat[:, GROUP + h : GROUP + h + 1]
            out_ref[:, cols] = (acc_ref[:, cols] / total).astype(out_ref.dtype)


def chosen_attention(info, ndoc, head_at, row_at, queries, k_chosen, v_chosen, acc, stat):
    rows = queries.shape[0]
    wide = GROUP * HD
    per_head = lambda g, info: (0, g)
    kv = pl.BlockSpec((MB, HD), lambda g, info: (info[row_at + g], g))
    return pl.pallas_call(
        functools.partial(chosen_kernel, ndoc, head_at),
        grid_spec=pltpu.PrefetchScalarGridSpec(
            num_scalar_prefetch=1,
            grid=(KVH,),
            in_specs=[
                pl.BlockSpec((rows, wide), per_head),
                kv,
                kv,
                pl.BlockSpec((rows, wide), per_head),
                pl.BlockSpec((rows, HD), per_head),
            ],
            out_specs=pl.BlockSpec((rows, wide), per_head),
        ),
        out_shape=jax.ShapeDtypeStruct((rows, HQ * HD), queries.dtype),
        compiler_params=pltpu.CompilerParams(vmem_limit_bytes=VMEM),
        cost_estimate=pl.CostEstimate(
            flops=8 * rows * MB * HQ * HD, bytes_accessed=14 << 20, transcendentals=rows * MB * HQ
        ),
        name="chosen_block",
    )(info, queries, k_chosen, v_chosen, acc, stat)


SCALARS = 2
WHOLE = pl.BlockSpec(memory_space=pltpu.VMEM)


def on_scalars(kernel, scalars, operands, in_specs, name, grid=(1,), **call):
    out_specs, scratch = call.pop("out_specs"), call.pop("scratch_shapes", ())
    return pl.pallas_call(
        kernel,
        grid_spec=pltpu.PrefetchScalarGridSpec(
            num_scalar_prefetch=SCALARS,
            grid=grid,
            in_specs=in_specs,
            out_specs=out_specs,
            scratch_shapes=scratch,
        ),
        compiler_params=pltpu.CompilerParams(vmem_limit_bytes=VMEM),
        cost_estimate=pl.CostEstimate(flops=1, bytes_accessed=1, transcendentals=0),
        name=name,
        **call,
    )(*scalars, *operands)


def copy_head(out, at, source, source_at, heads, g):
    rows = source.shape[0] if source_at is None else source_at[1]
    take = slice(None) if source_at is None else slice(source_at[0], source_at[0] + rows)
    for half in (g, heads + g):
        cols = slice(half * HD, (half + 1) * HD)
        out[at : at + rows, cols] = source[take, cols]


def copy_held(out, at, held, back, heads, g, usable):
    for step in range(len(held)):
        here = back == 2 * step
        if step == len(held) - 1:
            here = here | (back > 2 * step)

        @pl.when(here & usable)
        def _(step=step):
            copy_head(out, at, held[step], None, heads, g)


def share_kernel(chunk, heads, n_blk, docs, selected, *refs):
    *held, out = refs
    rows = held[0].shape[0]
    blk = lax.axis_index("blk")
    other = blk ^ 1
    above = jnp.minimum(other + 2, n_blk - 1)
    for at, consumer in ((0, other), (rows, above)):
        for g in range(heads):
            back = blk - selected[consumer, chunk * heads + g]
            usable = (back >= 0) & (back % 2 == 0)
            copy_held(out, at, held, back, heads, g, usable)

            @pl.when(jnp.logical_not(usable))
            def _():
                copy_head(out, at, held[0], None, heads, g)


def share(scalars, chunk, heads, n_blk, held):
    rows, wide = held[0].shape
    return on_scalars(
        functools.partial(share_kernel, chunk, heads, n_blk),
        scalars,
        held,
        [WHOLE] * len(held),
        "share",
        out_specs=WHOLE,
        out_shape=jax.ShapeDtypeStruct((2 * rows, wide), held[0].dtype),
    )


def settle_kernel(chunk, heads, n_blk, docs, selected, *refs):
    *held, passed, mine, upward = refs
    rows = mine.shape[0]
    blk = lax.axis_index("blk")
    above = jnp.minimum(blk + 2, n_blk - 1)
    for at, consumer, out in ((0, blk, mine), (rows, above, upward)):
        for g in range(heads):
            back = blk - selected[consumer, chunk * heads + g]
            usable = (back >= 0) & (back % 2 == 0)
            copy_held(out, 0, held, back, heads, g, usable)

            @pl.when(jnp.logical_not(usable))
            def _():
                copy_head(out, 0, passed, (at, rows), heads, g)


def settle(scalars, chunk, heads, n_blk, held, passed):
    rows, wide = held[0].shape
    shape = jax.ShapeDtypeStruct((rows, wide), held[0].dtype)
    return on_scalars(
        functools.partial(settle_kernel, chunk, heads, n_blk),
        scalars,
        [*held, passed],
        [WHOLE] * (len(held) + 1),
        "settle",
        out_specs=[WHOLE] * 2,
        out_shape=[shape, shape],
    )


def finish_kernel(chunk, heads, n_blk, docs, selected, mine, below, out):
    blk = lax.axis_index("blk")
    for g in range(heads):
        arrived = (blk >= n_blk - 2) & (selected[blk, chunk * heads + g] < n_blk - 2)

        @pl.when(arrived)
        def _():
            copy_head(out, 0, below, None, heads, g)

        @pl.when(jnp.logical_not(arrived))
        def _():
            copy_head(out, 0, mine, None, heads, g)


def finish(scalars, chunk, heads, n_blk, mine, below):
    return on_scalars(
        functools.partial(finish_kernel, chunk, heads, n_blk),
        scalars,
        [mine, below],
        [WHOLE] * 2,
        "finish",
        out_specs=WHOLE,
        out_shape=jax.ShapeDtypeStruct(mine.shape, mine.dtype),
    )


def finish_apart_kernel(chunk, heads, n_blk, docs, selected, mine, below, keys, values):
    blk = lax.axis_index("blk")
    for g in range(heads):
        arrived = (blk >= n_blk - 2) & (selected[blk, chunk * heads + g] < n_blk - 2)
        cols = slice(g * HD, (g + 1) * HD)
        more = slice((heads + g) * HD, (heads + g + 1) * HD)

        @pl.when(arrived)
        def _():
            keys[:, cols], values[:, cols] = below[:, cols], below[:, more]

        @pl.when(jnp.logical_not(arrived))
        def _():
            keys[:, cols], values[:, cols] = mine[:, cols], mine[:, more]


def finish_apart(scalars, chunk, heads, n_blk, mine, below):
    half = jax.ShapeDtypeStruct((mine.shape[0], heads * HD), mine.dtype)
    return on_scalars(
        functools.partial(finish_apart_kernel, chunk, heads, n_blk),
        scalars,
        [mine, below],
        [WHOLE] * 2,
        "finish_apart",
        out_specs=[WHOLE] * 2,
        out_shape=[half, half],
    )


def first_of(docs, place):
    end = jnp.int32(0)
    first = jnp.zeros_like(place)
    for d in range(docs.shape[0]):
        end = end + docs[d]
        first = jnp.maximum(first, jnp.where(end <= place, end, 0))
    return first


def scores(qq, kk):
    return lax.dot_general(qq, kk, (((1,), (1,)), ((), ())), preferred_element_type=jnp.float32)


def weighted(p, vv):
    return lax.dot_general(p, vv, (((1,), (0,)), ((), ())), preferred_element_type=jnp.float32)


def head_columns(ref, first, count):
    return ref[:, pl.ds(pl.multiple_of(first * HD, HD), count * HD)]


def columns_of(pieces, heads, half, chunk, g):
    found = []
    halves = [piece for piece in pieces if piece.shape[1] == heads * HD]
    for piece in [piece for piece in pieces if piece.shape[1] > heads * HD] + halves[half::2]:
        rows = MB // 4
        at = chunk * rows if piece.shape[0] > rows else 0
        first = g + (half * heads if piece.shape[1] > heads * HD else 0)
        found.append(head_columns(piece.at[pl.ds(at, rows)], first, 1))
    return jnp.concatenate(found, axis=0)


def each_head(q_ref, first, keys, values, s_ref, bias, use):
    kk, vv = doubled(keys), with_ones(values)

    def body(h, carry):
        s_ref[...] = scores(split_query(head_columns(q_ref, first + h, 1)), kk) + bias[...]
        use(h, vv)
        return carry

    lax.fori_loop(0, GROUP, body, 0)


def plain_attention(queries, keys, values, bias):
    q = jnp.concatenate(queries, axis=0)
    tile = 2 * HD
    weights = []
    for at in range(0, keys.shape[0], tile):
        s = scores(q, keys[at : at + tile]) * (LOG2E / HD**0.5)
        if bias is not None:
            s = s + jnp.concatenate([bias[:, at : at + tile]] * GROUP, axis=0)
        weights.append(jnp.exp2(s).astype(jnp.bfloat16))
    both = weighted(jnp.concatenate(weights, axis=1), with_ones(values))
    return both[:, :HD], both[:, HD:]


def first_query(chunk, heads, g):
    return (chunk * heads + g) * GROUP


def group_queries(q_ref, chunk, heads, g):
    return [head_columns(q_ref, first_query(chunk, heads, g) + h, 1) for h in range(GROUP)]


def each_key_head(heads, work):
    def body(g, carry):
        work(g)
        return carry

    lax.fori_loop(0, heads, body, 0)


def own_piece_kernel(n_uly, chunk, heads, count, docs, selected, q_ref, *refs):
    pieces, (acc_ref, total_ref, top_ref, plain, bias, s_ref) = refs[:count], refs[count:]
    rows = q_ref.shape[0]
    blk, uly = lax.axis_index("blk"), lax.axis_index("uly")
    place = (blk * n_uly + uly) * rows + lax.broadcasted_iota(jnp.int32, (rows, 1), 0)
    first = first_of(docs, place)
    lane = lax.broadcasted_iota(jnp.int32, (rows, rows), 1)
    for j in range(MB // rows):
        key = blk * MB + (uly ^ j) * rows + lane
        bias[:, j * rows : (j + 1) * rows] = jnp.where(
            (key <= place) & (key >= first), 0.0, HIDDEN
        )


    def work(g):
        queries = group_queries(q_ref, chunk, heads, g)
        keys, values = (columns_of(pieces, heads, half, chunk, g) for half in (0, 1))
        lane = lax.broadcasted_iota(jnp.int32, (rows, HD), 1)

        def keep(h, acc, total):
            at = pl.multiple_of((g * GROUP + h) * HD, HD)
            acc_ref[:, pl.ds(at, HD)] = acc
            total_ref[:, pl.ds(at, HD)] = total

        def keep_tops(tops):
            top_ref[:, pl.ds(pl.multiple_of(g * HD, HD), HD)] = tops

        acc, total = plain_attention(queries, keys, values, bias)
        for h in range(GROUP):
            keep(h, acc[h * rows : (h + 1) * rows], total[h * rows : (h + 1) * rows])
        keep_tops(jnp.zeros((rows, HD), jnp.float32))
        fits = (jnp.min(total) >= LEAST) & (jnp.max(total) <= MOST)
        plain[g] = fits.astype(jnp.int32)

        @pl.when(jnp.logical_not(fits))
        def _():
            def use(h, vv):
                top = jnp.max(s_ref[...], axis=1, keepdims=True)
                p = jnp.exp2(s_ref[...] - top).astype(jnp.bfloat16)
                both = weighted(p, vv)
                keep(h, both[:, :HD], both[:, HD:])
                keep_tops(jnp.where(lane == h, top, head_columns(top_ref, g, 1)))

            each_head(q_ref, first_query(chunk, heads, g), keys, values, s_ref, bias, use)

    each_key_head(heads, work)


def own_pieces(scalars, n_uly, chunk, queries, pieces):
    rows = queries.shape[0]
    heads = KVH // CHUNKS
    return on_scalars(
        functools.partial(own_piece_kernel, n_uly, chunk, heads, len(pieces)),
        scalars,
        [queries, *pieces],
        [WHOLE] * (1 + len(pieces)),
        "own_block",
        out_specs=[WHOLE, WHOLE, WHOLE, pl.BlockSpec(memory_space=pltpu.SMEM)],
        scratch_shapes=[
            pltpu.VMEM((rows, MB), jnp.float32),
            pltpu.VMEM((rows, MB), jnp.float32),
        ],
        out_shape=[
            jax.ShapeDtypeStruct((rows, heads * GROUP * HD), jnp.float32),
            jax.ShapeDtypeStruct((rows, heads * GROUP * HD), jnp.float32),
            jax.ShapeDtypeStruct((rows, heads * HD), jnp.float32),
            jax.ShapeDtypeStruct((heads,), jnp.int32),
        ],
    )


def chosen_piece_kernel(
    n_uly, chunk, heads, count, quarters, last, docs, selected, q_ref, *refs
):
    pieces, (acc_ref, total_ref, top_ref, plain) = refs[:count], refs[count : count + 4]
    bias, s_ref, again = refs[-3:]
    rows = q_ref.shape[0]
    blk, uly = lax.axis_index("blk"), lax.axis_index("uly")
    base = (blk * n_uly + uly) * rows

    def work(g):
        source = selected[blk, chunk * heads + g]
        low = first_of(docs, base) - source * MB
        high = first_of(docs, base + rows - 1) - source * MB
        some = (source != blk) & (low < MB)
        fits = plain[g] == 1

        @pl.when(some & ((high > 0) | jnp.logical_not(fits)))
        def _():
            place = base + lax.broadcasted_iota(jnp.int32, (rows, 1), 0)
            limit = first_of(docs, place) - source * MB
            lane = lax.broadcasted_iota(jnp.int32, (rows, rows), 1)
            for i, j in enumerate(quarters):
                key = (uly ^ j) * rows + lane
                bias[:, i * rows : (i + 1) * rows] = jnp.where(key < limit, HIDDEN, 0.0)

        def loaded():
            halves = [columns_of(pieces, heads, half, chunk, g) for half in (0, 1)]
            return [group_queries(q_ref, chunk, heads, g), *halves]

        def total_of(h):
            return head_columns(total_ref, g * GROUP + h, 1)

        def acc_of(h):
            return head_columns(acc_ref, g * GROUP + h, 1)

        if last:
            out_ref = refs[-4]

            def give(h, acc, total):
                attended = acc * pl.reciprocal(total, approx=True)
                at = pl.multiple_of((g * GROUP + h) * HD, HD)
                out_ref[:, pl.ds(at, HD)] = attended.astype(out_ref.dtype)

            def give_tops(tops, plainly):
                pass

        else:
            acc_out, total_out, top_out, plain_out = refs[-7:-3]

            def give(h, acc, total):
                at = pl.multiple_of((g * GROUP + h) * HD, HD)
                acc_out[:, pl.ds(at, HD)] = acc
                total_out[:, pl.ds(at, HD)] = total

            def give_tops(tops, plainly):
                top_out[:, pl.ds(pl.multiple_of(g * HD, HD), HD)] = tops
                plain_out[g] = plainly

        def add_plain(bias):
            acc, new = plain_attention(*loaded(), bias)
            for h in range(GROUP):
                here = slice(h * rows, (h + 1) * rows)
                give(h, acc[here] + acc_of(h), new[here] + total_of(h))
            give_tops(head_columns(top_ref, g, 1), 1)
            again[0] = jnp.logical_not(jnp.max(new) <= MOST).astype(jnp.int32)

        def add_shifted():
            tops = head_columns(top_ref, g, 1)
            lane = lax.broadcasted_iota(jnp.int32, (rows, HD), 1)
            give_tops(tops, 0)

            def use(h, vv):
                before = jnp.sum(jnp.where(lane == h, tops, 0.0), axis=1, keepdims=True)
                top = jnp.maximum(jnp.max(s_ref[...], axis=1, keepdims=True), before)
                p = jnp.exp2(s_ref[...] - top).astype(jnp.bfloat16)
                both = weighted(p, vv)
                keep = jnp.exp2(before - top)
                give(h, both[:, :HD] + keep * acc_of(h), both[:, HD:] + keep * total_of(h))
                if not last:
                    give_tops(jnp.where(lane == h, top, head_columns(top_out, g, 1)), 0)

            keys, values = loaded()[1:]
            each_head(q_ref, first_query(chunk, heads, g), keys, values, s_ref, bias, use)

        again[0] = (some & jnp.logical_not(fits)).astype(jnp.int32)

        @pl.when(some & fits & (high <= 0))
        def _():
            add_plain(None)

        @pl.when(some & fits & (high > 0))
        def _():
            add_plain(bias)

        @pl.when((again[0] == 1) & (high <= 0) & fits)
        def _():
            bias[...] = jnp.zeros_like(bias)

        @pl.when(again[0] == 1)
        def _():
            add_shifted()

        @pl.when(jnp.logical_not(some))
        def _():
            for h in range(GROUP):
                give(h, acc_of(h), total_of(h))
            give_tops(head_columns(top_ref, g, 1), plain[g])

    each_key_head(heads, work)


def chosen_pieces(scalars, n_uly, chunk, queries, pieces, kept, quarters, last, result=None):
    rows = queries.shape[0]
    heads = KVH // CHUNKS
    wide = GROUP * HD
    operands = [queries, *pieces, *kept]
    scalar_memory = pl.BlockSpec(memory_space=pltpu.SMEM)
    specs = [WHOLE] * (len(operands) - 1) + [scalar_memory]
    aliases = {}
    if last:
        out_specs = pl.BlockSpec((rows, heads * wide), lambda i, *_: (0, chunk))
        out_shape = jax.ShapeDtypeStruct((rows, HQ * HD), queries.dtype)
    else:
        out_specs = [WHOLE, WHOLE, WHOLE, scalar_memory]
        out_shape = [jax.ShapeDtypeStruct(a.shape, a.dtype) for a in kept]
    if result is not None:
        aliases = {SCALARS + len(operands): 0}
        operands.append(result)
        specs.append(pl.BlockSpec(memory_space=pl.ANY))
    return on_scalars(
        functools.partial(
            chosen_piece_kernel, n_uly, chunk, heads, len(pieces), quarters, last
        ),
        scalars,
        operands,
        specs,
        "chosen_block",
        out_specs=out_specs,
        scratch_shapes=[
            pltpu.VMEM((rows, len(quarters) * rows), jnp.float32),
            pltpu.VMEM((rows, len(quarters) * rows), jnp.float32),
            pltpu.SMEM((1,), jnp.int32),
        ],
        out_shape=out_shape,
        input_output_aliases=aliases,
    )


def up_line(part, chips, sources):
    return lax.ppermute(part, "blk", [(b, b + 2 * chips) for b in sources])


def across_chip(part, n_blk):
    return lax.ppermute(part, "blk", [(b, b ^ 1) for b in range(n_blk)])


def along(part, bit):
    return lax.ppermute(part, "uly", [(u, u ^ bit) for u in range(4)])


CHUNKS = 2


def by_permutes(n_blk, n_uly, queries, keys, values, doc_lengths, selected):
    scalars = (doc_lengths, selected)
    heads = KVH // CHUNKS
    chunks = range(CHUNKS)
    parts = [
        jnp.concatenate([a[:, c * heads * HD : (c + 1) * heads * HD] for a in (keys, values)], axis=1)
        for c in chunks
    ]
    hold = lax.optimization_barrier
    packed = jnp.concatenate(parts, axis=0)

    def lower_blocks(part):
        reach = range(1, n_blk // 2 - 1)
        return [part] + [up_line(part, k, range(n_blk - 2 - 2 * k)) for k in reach]

    def offer(c, held):
        return share(scalars, c, heads, n_blk, held)

    def take(c, held, offered):
        kept, upward = settle(scalars, c, heads, n_blk, held, across_chip(offered, n_blk))
        return kept, upward, up_line(upward, 1, range(n_blk - 4, n_blk - 2))

    def corner_parts(near, far):
        middle = near.shape[1] // 2
        return near[:, :middle], far[:, middle:]

    near, far = along(packed, 1), along(packed, 2)
    first = lower_blocks(parts[0])
    near, far, first, parts = hold((near, far, first, parts))
    corner = [along(part, 3) for part in parts]
    second = lower_blocks(parts[1])
    kept, upward, below = take(0, first, offer(0, first))
    asked, _ = hold((queries, upward))
    own = [[parts[c], near, far, corner[c]] for c in chunks]
    partial = [own_pieces(scalars, n_uly, 0, asked, own[0])]
    second, own[1], kept, below, partial[0] = hold((second, own[1], kept, below, partial[0]))
    offered = offer(1, second)
    kept, offered = hold((kept, offered))
    chosen = [finish(scalars, 0, heads, n_blk, kept, below)]
    near, far = along(chosen[0], 1), along(chosen[0], 2)
    kept, upward, below = take(1, second, offered)
    asked, _ = hold((queries, (upward, chosen)))
    partial.append(own_pieces(scalars, n_uly, 1, asked, own[1]))
    near, far, _ = hold((near, far, partial[1]))
    passed = corner_parts(near, far)
    kept, passed = hold((kept, passed))
    gathered = [chosen[0], near, far, along(passed[0], 2), along(passed[1], 1)]
    apart = finish_apart(scalars, 1, heads, n_blk, kept, below)
    near = [along(half, 1) for half in apart]
    far = [along(half, 2) for half in apart]
    result = chosen_pieces(
        scalars, n_uly, 0, queries, gathered, partial[0], (0, 1, 2, 3), True
    )
    near, far, result = hold((near, far, result))
    corner = [along(near[0], 2), along(far[1], 1)]
    partial[1] = chosen_pieces(
        scalars, n_uly, 1, queries, [*apart, *near, *far], partial[1], (0, 1, 2), False
    )
    return chosen_pieces(
        scalars, n_uly, 1, queries, corner, partial[1], (3,), True, result
    )


def on_device(n_blk, n_uly, queries, keys, values, doc_lengths, selected):
    rows = queries.shape[0]
    ndoc = doc_lengths.shape[0]
    per_dev = n_uly * rows // MB
    slices = MB // rows
    if per_dev == 1 and n_uly == 4 and n_blk % 2 == 0 and n_blk >= 4:
        return by_permutes(n_blk, n_uly, queries, keys, values, doc_lengths, selected)
    blk, uly = lax.axis_index("blk"), lax.axis_index("uly")
    mine = uly // slices
    block = blk * per_dev + mine
    ends = jnp.cumsum(doc_lengths)
    place = (blk * n_uly + uly) * rows
    picks = selected[block]
    wanted = jnp.where(picks == block, -1, picks)
    info = jnp.concatenate(
        [ends, jnp.stack([place, block, mine]), wanted, picks % per_dev]
    ).astype(jnp.int32)
    head_at = ndoc + 3
    row_at = head_at + KVH

    k_all = lax.all_gather(keys, "blk", axis=0, tiled=True)
    v_all = lax.all_gather(values, "blk", axis=0, tiled=True)
    k_own = lax.all_gather(keys, "uly", axis=0, tiled=True)
    v_own = lax.all_gather(values, "uly", axis=0, tiled=True)
    acc, stat = own_attention(info, ndoc, ndoc + 2, queries, k_own, v_own)

    k_sets, v_sets = [], []
    for row in range(per_dev):
        source = selected[blk * per_dev + row] // per_dev
        k_part, v_part = pick(source, k_all, v_all, rows)
        k_sets.append(lax.all_gather(k_part, "uly", axis=0, tiled=True))
        v_sets.append(lax.all_gather(v_part, "uly", axis=0, tiled=True))
    if per_dev == 1:
        k_chosen, v_chosen = k_sets[0], v_sets[0]
    else:
        k_chosen = lax.dynamic_index_in_dim(jnp.stack(k_sets), mine, 0, keepdims=False)
        v_chosen = lax.dynamic_index_in_dim(jnp.stack(v_sets), mine, 0, keepdims=False)
    return chosen_attention(info, ndoc, head_at, row_at, queries, k_chosen, v_chosen, acc, stat)


def solution(mesh):
    placed = (P(("blk", "uly"), None), P(("blk", "uly"), None), P(("blk", "uly"), None), P(), P())
    return jax.shard_map(
        functools.partial(on_device, mesh.shape["blk"], mesh.shape["uly"]),
        mesh=mesh,
        in_specs=placed,
        out_specs=P(("blk", "uly"), None),
        check_vma=False,
    )
```

```python
import functools

import jax
import jax.numpy as jnp
from jax import lax
from jax.experimental import pallas as pl
from jax.experimental.pallas import tpu as pltpu
from jax.sharding import PartitionSpec as P

HQ = 32
KVH = 8
HD = 128
MB = 1024
GROUP = HQ // KVH
LOG2E = 1.4426950408889634
HIDDEN = -1e30
LEAST, MOST = 2.0**-60, 2.0**100
VMEM = 24 * 1024 * 1024


def pick_kernel(info, k_ref, v_ref, k_out, v_out):
    k_out[...] = k_ref[...]
    v_out[...] = v_ref[...]


def pick(source, k_all, v_all, rows):
    spec = pl.BlockSpec((rows, HD), lambda g, info: (info[g], g))
    out = pl.BlockSpec((rows, HD), lambda g, info: (0, g))
    shape = jax.ShapeDtypeStruct((rows, KVH * HD), k_all.dtype)
    return pl.pallas_call(
        pick_kernel,
        grid_spec=pltpu.PrefetchScalarGridSpec(
            num_scalar_prefetch=1, grid=(KVH,), in_specs=[spec, spec], out_specs=[out, out]
        ),
        out_shape=[shape, shape],
        cost_estimate=pl.CostEstimate(
            flops=0, bytes_accessed=4 * rows * KVH * HD * 2, transcendentals=0
        ),
        name="pick",
    )(source, k_all, v_all)


def starts_of(info, ndoc, places):
    first = jnp.zeros_like(places)
    for d in range(ndoc):
        end = info[d]
        first = jnp.maximum(first, jnp.where(end <= places, end, 0))
    return first


def split_query(q):
    scaled = q.astype(jnp.float32) * (LOG2E / HD**0.5)
    high = scaled.astype(jnp.bfloat16)
    low = (scaled - high.astype(jnp.float32)).astype(jnp.bfloat16)
    return jnp.concatenate([high, low], axis=1)


def doubled(k):
    return jnp.concatenate([k, k], axis=1)


def with_ones(v):
    return jnp.concatenate([v, jnp.ones_like(v)], axis=1)


def own_kernel(ndoc, info, q_ref, k_ref, v_ref, acc_ref, stat_ref, bias):
    rows = q_ref.shape[0]

    @pl.when(pl.program_id(0) == 0)
    def _():
        base = info[ndoc]
        place = base + lax.broadcasted_iota(jnp.int32, (rows, 1), 0)
        first = starts_of(info, ndoc, place)
        key = info[ndoc + 1] * MB + lax.broadcasted_iota(jnp.int32, (rows, MB), 1)
        bias[...] = jnp.where((key <= place) & (key >= first), 0.0, HIDDEN)

    kk = doubled(k_ref[...])
    vv = with_ones(v_ref[...])
    lane = lax.broadcasted_iota(jnp.int32, (rows, HD), 1)
    stat = jnp.zeros((rows, HD), jnp.float32)
    for h in range(GROUP):
        cols = slice(h * HD, (h + 1) * HD)
        qq = split_query(q_ref[:, cols])
        s = lax.dot_general(qq, kk, (((1,), (1,)), ((), ())), preferred_element_type=jnp.float32)
        s = s + bias[...]
        top = jnp.max(s, axis=1, keepdims=True)
        p = jnp.exp2(s - top).astype(jnp.bfloat16)
        both = lax.dot_general(p, vv, (((1,), (0,)), ((), ())), preferred_element_type=jnp.float32)
        acc_ref[:, cols] = both[:, :HD]
        stat = jnp.where(lane == h, top, stat)
        stat = jnp.where(lane == GROUP + h, both[:, HD:], stat)
    stat_ref[...] = stat


def own_attention(info, ndoc, own_row, queries, k_own, v_own):
    rows = queries.shape[0]
    wide = GROUP * HD
    per_head = lambda g, info: (0, g)
    kv = pl.BlockSpec((MB, HD), lambda g, info: (info[own_row], g))
    return pl.pallas_call(
        functools.partial(own_kernel, ndoc),
        grid_spec=pltpu.PrefetchScalarGridSpec(
            num_scalar_prefetch=1,
            grid=(KVH,),
            in_specs=[pl.BlockSpec((rows, wide), per_head), kv, kv],
            out_specs=[pl.BlockSpec((rows, wide), per_head), pl.BlockSpec((rows, HD), per_head)],
            scratch_shapes=[pltpu.VMEM((rows, MB), jnp.float32)],
        ),
        out_shape=[
            jax.ShapeDtypeStruct((rows, HQ * HD), jnp.float32),
            jax.ShapeDtypeStruct((rows, KVH * HD), jnp.float32),
        ],
        compiler_params=pltpu.CompilerParams(vmem_limit_bytes=VMEM),
        cost_estimate=pl.CostEstimate(
            flops=8 * rows * MB * HQ * HD, bytes_accessed=12 << 20, transcendentals=rows * MB * HQ
        ),
        name="own_block",
    )(info, queries, k_own, v_own)


def chosen_kernel(ndoc, head_at, info, q_ref, k_ref, v_ref, acc_ref, stat_ref, out_ref):
    rows = q_ref.shape[0]
    base = info[ndoc]
    source = info[head_at + pl.program_id(0)]

    def bound(place):
        first = jnp.int32(0)
        for d in range(ndoc):
            first = jnp.maximum(first, jnp.where(info[d] <= place, info[d], 0))
        return first - source * MB

    low, high = bound(base), bound(base + rows - 1)
    live = source >= 0

    def merge(masked):
        kk = doubled(k_ref[...])
        vv = with_ones(v_ref[...])
        stat = stat_ref[...]
        if masked:
            place = base + lax.broadcasted_iota(jnp.int32, (rows, 1), 0)
            limit = starts_of(info, ndoc, place) - source * MB
            key = lax.broadcasted_iota(jnp.int32, (rows, MB), 1)
            hide = key < limit
        for h in range(GROUP):
            cols = slice(h * HD, (h + 1) * HD)
            qq = split_query(q_ref[:, cols])
            s = lax.dot_general(
                qq, kk, (((1,), (1,)), ((), ())), preferred_element_type=jnp.float32
            )
            if masked:
                s = jnp.where(hide, HIDDEN, s)
            before = stat[:, h : h + 1]
            top = jnp.maximum(jnp.max(s, axis=1, keepdims=True), before)
            p = jnp.exp2(s - top).astype(jnp.bfloat16)
            both = lax.dot_general(
                p, vv, (((1,), (0,)), ((), ())), preferred_element_type=jnp.float32
            )
            keep = jnp.exp2(before - top)
            total = both[:, HD:] + keep * stat[:, GROUP + h : GROUP + h + 1]
            acc = both[:, :HD] + keep * acc_ref[:, cols]
            out_ref[:, cols] = (acc / total).astype(out_ref.dtype)

    some = live & (low < MB)

    @pl.when(some & (high <= 0))
    def _():
        merge(False)

    @pl.when(some & (high > 0))
    def _():
        merge(True)

    @pl.when(jnp.logical_not(some))
    def _():
        stat = stat_ref[...]
        for h in range(GROUP):
            cols = slice(h * HD, (h + 1) * HD)
            total = stat[:, GROUP + h : GROUP + h + 1]
            out_ref[:, cols] = (acc_ref[:, cols] / total).astype(out_ref.dtype)


def chosen_attention(info, ndoc, head_at, row_at, queries, k_chosen, v_chosen, acc, stat):
    rows = queries.shape[0]
    wide = GROUP * HD
    per_head = lambda g, info: (0, g)
    kv = pl.BlockSpec((MB, HD), lambda g, info: (info[row_at + g], g))
    return pl.pallas_call(
        functools.partial(chosen_kernel, ndoc, head_at),
        grid_spec=pltpu.PrefetchScalarGridSpec(
            num_scalar_prefetch=1,
            grid=(KVH,),
            in_specs=[
                pl.BlockSpec((rows, wide), per_head),
                kv,
                kv,
                pl.BlockSpec((rows, wide), per_head),
                pl.BlockSpec((rows, HD), per_head),
            ],
            out_specs=pl.BlockSpec((rows, wide), per_head),
        ),
        out_shape=jax.ShapeDtypeStruct((rows, HQ * HD), queries.dtype),
        compiler_params=pltpu.CompilerParams(vmem_limit_bytes=VMEM),
        cost_estimate=pl.CostEstimate(
            flops=8 * rows * MB * HQ * HD, bytes_accessed=14 << 20, transcendentals=rows * MB * HQ
        ),
        name="chosen_block",
    )(info, queries, k_chosen, v_chosen, acc, stat)


SCALARS = 2
WHOLE = pl.BlockSpec(memory_space=pltpu.VMEM)


def on_scalars(kernel, scalars, operands, in_specs, name, grid=(1,), **call):
    out_specs, scratch = call.pop("out_specs"), call.pop("scratch_shapes", ())
    return pl.pallas_call(
        kernel,
        grid_spec=pltpu.PrefetchScalarGridSpec(
            num_scalar_prefetch=SCALARS,
            grid=grid,
            in_specs=in_specs,
            out_specs=out_specs,
            scratch_shapes=scratch,
        ),
        compiler_params=pltpu.CompilerParams(vmem_limit_bytes=VMEM),
        cost_estimate=pl.CostEstimate(flops=1, bytes_accessed=1, transcendentals=0),
        name=name,
        **call,
    )(*scalars, *operands)


def copy_head(out, at, source, source_at, heads, g):
    rows = source.shape[0] if source_at is None else source_at[1]
    take = slice(None) if source_at is None else slice(source_at[0], source_at[0] + rows)
    for half in (g, heads + g):
        cols = slice(half * HD, (half + 1) * HD)
        out[at : at + rows, cols] = source[take, cols]


def copy_held(out, at, held, back, heads, g, usable):
    for step in range(len(held)):
        here = back == 2 * step
        if step == len(held) - 1:
            here = here | (back > 2 * step)

        @pl.when(here & usable)
        def _(step=step):
            copy_head(out, at, held[step], None, heads, g)


def share_kernel(chunk, heads, n_blk, docs, selected, *refs):
    *held, out = refs
    rows = held[0].shape[0]
    blk = lax.axis_index("blk")
    other = blk ^ 1
    above = jnp.minimum(other + 2, n_blk - 1)
    for at, consumer in ((0, other), (rows, above)):
        for g in range(heads):
            back = blk - selected[consumer, chunk * heads + g]
            usable = (back >= 0) & (back % 2 == 0)
            copy_held(out, at, held, back, heads, g, usable)

            @pl.when(jnp.logical_not(usable))
            def _():
                copy_head(out, at, held[0], None, heads, g)


def share(scalars, chunk, heads, n_blk, held):
    rows, wide = held[0].shape
    return on_scalars(
        functools.partial(share_kernel, chunk, heads, n_blk),
        scalars,
        held,
        [WHOLE] * len(held),
        "share",
        out_specs=WHOLE,
        out_shape=jax.ShapeDtypeStruct((2 * rows, wide), held[0].dtype),
    )


def settle_kernel(chunk, heads, n_blk, docs, selected, *refs):
    *held, passed, mine, upward = refs
    rows = mine.shape[0]
    blk = lax.axis_index("blk")
    above = jnp.minimum(blk + 2, n_blk - 1)
    for at, consumer, out in ((0, blk, mine), (rows, above, upward)):
        for g in range(heads):
            back = blk - selected[consumer, chunk * heads + g]
            usable = (back >= 0) & (back % 2 == 0)
            copy_held(out, 0, held, back, heads, g, usable)

            @pl.when(jnp.logical_not(usable))
            def _():
                copy_head(out, 0, passed, (at, rows), heads, g)


def settle(scalars, chunk, heads, n_blk, held, passed):
    rows, wide = held[0].shape
    shape = jax.ShapeDtypeStruct((rows, wide), held[0].dtype)
    return on_scalars(
        functools.partial(settle_kernel, chunk, heads, n_blk),
        scalars,
        [*held, passed],
        [WHOLE] * (len(held) + 1),
        "settle",
        out_specs=[WHOLE] * 2,
        out_shape=[shape, shape],
    )


def finish_kernel(chunk, heads, n_blk, docs, selected, mine, below, out):
    blk = lax.axis_index("blk")
    for g in range(heads):
        arrived = (blk >= n_blk - 2) & (selected[blk, chunk * heads + g] < n_blk - 2)

        @pl.when(arrived)
        def _():
            copy_head(out, 0, below, None, heads, g)

        @pl.when(jnp.logical_not(arrived))
        def _():
            copy_head(out, 0, mine, None, heads, g)


def finish(scalars, chunk, heads, n_blk, mine, below):
    return on_scalars(
        functools.partial(finish_kernel, chunk, heads, n_blk),
        scalars,
        [mine, below],
        [WHOLE] * 2,
        "finish",
        out_specs=WHOLE,
        out_shape=jax.ShapeDtypeStruct(mine.shape, mine.dtype),
    )


def finish_apart_kernel(chunk, heads, n_blk, docs, selected, mine, below, keys, values):
    blk = lax.axis_index("blk")
    for g in range(heads):
        arrived = (blk >= n_blk - 2) & (selected[blk, chunk * heads + g] < n_blk - 2)
        cols = slice(g * HD, (g + 1) * HD)
        more = slice((heads + g) * HD, (heads + g + 1) * HD)

        @pl.when(arrived)
        def _():
            keys[:, cols], values[:, cols] = below[:, cols], below[:, more]

        @pl.when(jnp.logical_not(arrived))
        def _():
            keys[:, cols], values[:, cols] = mine[:, cols], mine[:, more]


def finish_apart(scalars, chunk, heads, n_blk, mine, below):
    half = jax.ShapeDtypeStruct((mine.shape[0], heads * HD), mine.dtype)
    return on_scalars(
        functools.partial(finish_apart_kernel, chunk, heads, n_blk),
        scalars,
        [mine, below],
        [WHOLE] * 2,
        "finish_apart",
        out_specs=[WHOLE] * 2,
        out_shape=[half, half],
    )


def first_of(docs, place):
    end = jnp.int32(0)
    first = jnp.zeros_like(place)
    for d in range(docs.shape[0]):
        end = end + docs[d]
        first = jnp.maximum(first, jnp.where(end <= place, end, 0))
    return first


def scores(qq, kk):
    return lax.dot_general(qq, kk, (((1,), (1,)), ((), ())), preferred_element_type=jnp.float32)


def weighted(p, vv):
    return lax.dot_general(p, vv, (((1,), (0,)), ((), ())), preferred_element_type=jnp.float32)


def head_columns(ref, first, count):
    return ref[:, pl.ds(pl.multiple_of(first * HD, HD), count * HD)]


def columns_of(pieces, heads, half, chunk, g):
    found = []
    halves = [piece for piece in pieces if piece.shape[1] == heads * HD]
    for piece in [piece for piece in pieces if piece.shape[1] > heads * HD] + halves[half::2]:
        rows = MB // 4
        at = chunk * rows if piece.shape[0] > rows else 0
        first = g + (half * heads if piece.shape[1] > heads * HD else 0)
        found.append(head_columns(piece.at[pl.ds(at, rows)], first, 1))
    return jnp.concatenate(found, axis=0)


def each_head(q_ref, first, keys, values, s_ref, bias, use):
    kk, vv = doubled(keys), with_ones(values)

    def body(h, carry):
        s_ref[...] = scores(split_query(head_columns(q_ref, first + h, 1)), kk) + bias[...]
        use(h, vv)
        return carry

    lax.fori_loop(0, GROUP, body, 0)


def plain_attention(queries, keys, values, bias):
    q = jnp.concatenate(queries, axis=0)
    tile = 2 * HD
    weights = []
    for at in range(0, keys.shape[0], tile):
        s = scores(q, keys[at : at + tile]) * (LOG2E / HD**0.5)
        if bias is not None:
            s = s + jnp.concatenate([bias[:, at : at + tile]] * GROUP, axis=0)
        weights.append(jnp.exp2(s).astype(jnp.bfloat16))
    both = weighted(jnp.concatenate(weights, axis=1), with_ones(values))
    return both[:, :HD], both[:, HD:]


def first_query(chunk, heads, g):
    return (chunk * heads + g) * GROUP


def group_queries(q_ref, chunk, heads, g):
    return [head_columns(q_ref, first_query(chunk, heads, g) + h, 1) for h in range(GROUP)]


def each_key_head(heads, work):
    def body(g, carry):
        work(g)
        return carry

    lax.fori_loop(0, heads, body, 0)


def own_piece_kernel(n_uly, chunk, heads, count, docs, selected, q_ref, *refs):
    pieces, (acc_ref, total_ref, top_ref, plain, bias, s_ref) = refs[:count], refs[count:]
    rows = q_ref.shape[0]
    blk, uly = lax.axis_index("blk"), lax.axis_index("uly")
    place = (blk * n_uly + uly) * rows + lax.broadcasted_iota(jnp.int32, (rows, 1), 0)
    first = first_of(docs, place)
    lane = lax.broadcasted_iota(jnp.int32, (rows, rows), 1)
    for j in range(MB // rows):
        key = blk * MB + (uly ^ j) * rows + lane
        bias[:, j * rows : (j + 1) * rows] = jnp.where(
            (key <= place) & (key >= first), 0.0, HIDDEN
        )


    def work(g):
        queries = group_queries(q_ref, chunk, heads, g)
        keys, values = (columns_of(pieces, heads, half, chunk, g) for half in (0, 1))
        lane = lax.broadcasted_iota(jnp.int32, (rows, HD), 1)

        def keep(h, acc, total):
            at = pl.multiple_of((g * GROUP + h) * HD, HD)
            acc_ref[:, pl.ds(at, HD)] = acc
            total_ref[:, pl.ds(at, HD)] = total

        def keep_tops(tops):
            top_ref[:, pl.ds(pl.multiple_of(g * HD, HD), HD)] = tops

        acc, total = plain_attention(queries, keys, values, bias)
        for h in range(GROUP):
            keep(h, acc[h * rows : (h + 1) * rows], total[h * rows : (h + 1) * rows])
        keep_tops(jnp.zeros((rows, HD), jnp.float32))
        fits = (jnp.min(total) >= LEAST) & (jnp.max(total) <= MOST)
        plain[g] = fits.astype(jnp.int32)

        @pl.when(jnp.logical_not(fits))
        def _():
            def use(h, vv):
                top = jnp.max(s_ref[...], axis=1, keepdims=True)
                p = jnp.exp2(s_ref[...] - top).astype(jnp.bfloat16)
                both = weighted(p, vv)
                keep(h, both[:, :HD], both[:, HD:])
                keep_tops(jnp.where(lane == h, top, head_columns(top_ref, g, 1)))

            each_head(q_ref, first_query(chunk, heads, g), keys, values, s_ref, bias, use)

    each_key_head(heads, work)


def own_pieces(scalars, n_uly, chunk, queries, pieces):
    rows = queries.shape[0]
    heads = KVH // CHUNKS
    return on_scalars(
        functools.partial(own_piece_kernel, n_uly, chunk, heads, len(pieces)),
        scalars,
        [queries, *pieces],
        [WHOLE] * (1 + len(pieces)),
        "own_block",
        out_specs=[WHOLE, WHOLE, WHOLE, pl.BlockSpec(memory_space=pltpu.SMEM)],
        scratch_shapes=[
            pltpu.VMEM((rows, MB), jnp.float32),
            pltpu.VMEM((rows, MB), jnp.float32),
        ],
        out_shape=[
            jax.ShapeDtypeStruct((rows, heads * GROUP * HD), jnp.float32),
            jax.ShapeDtypeStruct((rows, heads * GROUP * HD), jnp.float32),
            jax.ShapeDtypeStruct((rows, heads * HD), jnp.float32),
            jax.ShapeDtypeStruct((heads,), jnp.int32),
        ],
    )


def chosen_piece_kernel(
    n_uly, chunk, heads, count, quarters, last, docs, selected, q_ref, *refs
):
    pieces, (acc_ref, total_ref, top_ref, plain) = refs[:count], refs[count : count + 4]
    bias, s_ref, again = refs[-3:]
    rows = q_ref.shape[0]
    blk, uly = lax.axis_index("blk"), lax.axis_index("uly")
    base = (blk * n_uly + uly) * rows

    def work(g):
        source = selected[blk, chunk * heads + g]
        low = first_of(docs, base) - source * MB
        high = first_of(docs, base + rows - 1) - source * MB
        some = (source != blk) & (low < MB)
        fits = plain[g] == 1

        @pl.when(some & ((high > 0) | jnp.logical_not(fits)))
        def _():
            place = base + lax.broadcasted_iota(jnp.int32, (rows, 1), 0)
            limit = first_of(docs, place) - source * MB
            lane = lax.broadcasted_iota(jnp.int32, (rows, rows), 1)
            for i, j in enumerate(quarters):
                key = (uly ^ j) * rows + lane
                bias[:, i * rows : (i + 1) * rows] = jnp.where(key < limit, HIDDEN, 0.0)

        def loaded():
            halves = [columns_of(pieces, heads, half, chunk, g) for half in (0, 1)]
            return [group_queries(q_ref, chunk, heads, g), *halves]

        def total_of(h):
            return head_columns(total_ref, g * GROUP + h, 1)

        def acc_of(h):
            return head_columns(acc_ref, g * GROUP + h, 1)

        if last:
            out_ref = refs[-4]

            def give(h, acc, total):
                attended = acc * pl.reciprocal(total, approx=True)
                at = pl.multiple_of((g * GROUP + h) * HD, HD)
                out_ref[:, pl.ds(at, HD)] = attended.astype(out_ref.dtype)

            def give_tops(tops, plainly):
                pass

        else:
            acc_out, total_out, top_out, plain_out = refs[-7:-3]

            def give(h, acc, total):
                at = pl.multiple_of((g * GROUP + h) * HD, HD)
                acc_out[:, pl.ds(at, HD)] = acc
                total_out[:, pl.ds(at, HD)] = total

            def give_tops(tops, plainly):
                top_out[:, pl.ds(pl.multiple_of(g * HD, HD), HD)] = tops
                plain_out[g] = plainly

        def add_plain(bias):
            acc, new = plain_attention(*loaded(), bias)
            for h in range(GROUP):
                here = slice(h * rows, (h + 1) * rows)
                give(h, acc[here] + acc_of(h), new[here] + total_of(h))
            give_tops(head_columns(top_ref, g, 1), 1)
            again[0] = jnp.logical_not(jnp.max(new) <= MOST).astype(jnp.int32)

        def add_shifted():
            tops = head_columns(top_ref, g, 1)
            lane = lax.broadcasted_iota(jnp.int32, (rows, HD), 1)
            give_tops(tops, 0)

            def use(h, vv):
                before = jnp.sum(jnp.where(lane == h, tops, 0.0), axis=1, keepdims=True)
                top = jnp.maximum(jnp.max(s_ref[...], axis=1, keepdims=True), before)
                p = jnp.exp2(s_ref[...] - top).astype(jnp.bfloat16)
                both = weighted(p, vv)
                keep = jnp.exp2(before - top)
                give(h, both[:, :HD] + keep * acc_of(h), both[:, HD:] + keep * total_of(h))
                if not last:
                    give_tops(jnp.where(lane == h, top, head_columns(top_out, g, 1)), 0)

            keys, values = loaded()[1:]
            each_head(q_ref, first_query(chunk, heads, g), keys, values, s_ref, bias, use)

        again[0] = (some & jnp.logical_not(fits)).astype(jnp.int32)

        @pl.when(some & fits & (high <= 0))
        def _():
            add_plain(None)

        @pl.when(some & fits & (high > 0))
        def _():
            add_plain(bias)

        @pl.when((again[0] == 1) & (high <= 0) & fits)
        def _():
            bias[...] = jnp.zeros_like(bias)

        @pl.when(again[0] == 1)
        def _():
            add_shifted()

        @pl.when(jnp.logical_not(some))
        def _():
            for h in range(GROUP):
                give(h, acc_of(h), total_of(h))
            give_tops(head_columns(top_ref, g, 1), plain[g])

    each_key_head(heads, work)


def chosen_pieces(scalars, n_uly, chunk, queries, pieces, kept, quarters, last, result=None):
    rows = queries.shape[0]
    heads = KVH // CHUNKS
    wide = GROUP * HD
    operands = [queries, *pieces, *kept]
    scalar_memory = pl.BlockSpec(memory_space=pltpu.SMEM)
    specs = [WHOLE] * (len(operands) - 1) + [scalar_memory]
    aliases = {}
    if last:
        out_specs = pl.BlockSpec((rows, heads * wide), lambda i, *_: (0, chunk))
        out_shape = jax.ShapeDtypeStruct((rows, HQ * HD), queries.dtype)
    else:
        out_specs = [WHOLE, WHOLE, WHOLE, scalar_memory]
        out_shape = [jax.ShapeDtypeStruct(a.shape, a.dtype) for a in kept]
    if result is not None:
        aliases = {SCALARS + len(operands): 0}
        operands.append(result)
        specs.append(pl.BlockSpec(memory_space=pl.ANY))
    return on_scalars(
        functools.partial(
            chosen_piece_kernel, n_uly, chunk, heads, len(pieces), quarters, last
        ),
        scalars,
        operands,
        specs,
        "chosen_block",
        out_specs=out_specs,
        scratch_shapes=[
            pltpu.VMEM((rows, len(quarters) * rows), jnp.float32),
            pltpu.VMEM((rows, len(quarters) * rows), jnp.float32),
            pltpu.SMEM((1,), jnp.int32),
        ],
        out_shape=out_shape,
        input_output_aliases=aliases,
    )


def up_line(part, chips, sources):
    return lax.ppermute(part, "blk", [(b, b + 2 * chips) for b in sources])


def across_chip(part, n_blk):
    return lax.ppermute(part, "blk", [(b, b ^ 1) for b in range(n_blk)])


def along(part, bit):
    return lax.ppermute(part, "uly", [(u, u ^ bit) for u in range(4)])


CHUNKS = 2


def by_permutes(n_blk, n_uly, queries, keys, values, doc_lengths, selected):
    scalars = (doc_lengths, selected)
    heads = KVH // CHUNKS
    chunks = range(CHUNKS)
    parts = [
        jnp.concatenate([a[:, c * heads * HD : (c + 1) * heads * HD] for a in (keys, values)], axis=1)
        for c in chunks
    ]
    hold = lax.optimization_barrier
    packed = jnp.concatenate(parts, axis=0)

    def lower_blocks(part):
        reach = range(1, n_blk // 2 - 1)
        return [part] + [up_line(part, k, range(n_blk - 2 - 2 * k)) for k in reach]

    def offer(c, held):
        return share(scalars, c, heads, n_blk, held)

    def take(c, held, offered):
        kept, upward = settle(scalars, c, heads, n_blk, held, across_chip(offered, n_blk))
        return kept, upward, up_line(upward, 1, range(n_blk - 4, n_blk - 2))

    def corner_parts(near, far):
        middle = near.shape[1] // 2
        return near[:, :middle], far[:, middle:]

    near, far = along(packed, 1), along(packed, 2)
    first = lower_blocks(parts[0])
    near, far, first, parts = hold((near, far, first, parts))
    corner = [along(part, 3) for part in parts]
    second = lower_blocks(parts[1])
    kept, upward, below = take(0, first, offer(0, first))
    asked, _ = hold((queries, upward))
    own = [[parts[c], near, far, corner[c]] for c in chunks]
    partial = [own_pieces(scalars, n_uly, 0, asked, own[0])]
    second, own[1], kept, below, partial[0] = hold((second, own[1], kept, below, partial[0]))
    offered = offer(1, second)
    kept, offered = hold((kept, offered))
    chosen = [finish(scalars, 0, heads, n_blk, kept, below)]
    near, far = along(chosen[0], 1), along(chosen[0], 2)
    kept, upward, below = take(1, second, offered)
    asked, _ = hold((queries, (upward, chosen)))
    partial.append(own_pieces(scalars, n_uly, 1, asked, own[1]))
    near, far, _ = hold((near, far, partial[1]))
    passed = corner_parts(near, far)
    kept, passed = hold((kept, passed))
    gathered = [chosen[0], near, far, along(passed[0], 2), along(passed[1], 1)]
    apart = finish_apart(scalars, 1, heads, n_blk, kept, below)
    near = [along(half, 1) for half in apart]
    far = [along(half, 2) for half in apart]
    result = chosen_pieces(
        scalars, n_uly, 0, queries, gathered, partial[0], (0, 1, 2, 3), True
    )
    near[0], far[1], result = hold((near[0], far[1], result))
    corner = [along(near[0], 2), along(far[1], 1)]
    partial[1] = chosen_pieces(
        scalars, n_uly, 1, queries, [*apart, *near, *far], partial[1], (0, 1, 2), False
    )
    return chosen_pieces(
        scalars, n_uly, 1, queries, corner, partial[1], (3,), True, result
    )


def on_device(n_blk, n_uly, queries, keys, values, doc_lengths, selected):
    rows = queries.shape[0]
    ndoc = doc_lengths.shape[0]
    per_dev = n_uly * rows // MB
    slices = MB // rows
    if per_dev == 1 and n_uly == 4 and n_blk % 2 == 0 and n_blk >= 4:
        return by_permutes(n_blk, n_uly, queries, keys, values, doc_lengths, selected)
    blk, uly = lax.axis_index("blk"), lax.axis_index("uly")
    mine = uly // slices
    block = blk * per_dev + mine
    ends = jnp.cumsum(doc_lengths)
    place = (blk * n_uly + uly) * rows
    picks = selected[block]
    wanted = jnp.where(picks == block, -1, picks)
    info = jnp.concatenate(
        [ends, jnp.stack([place, block, mine]), wanted, picks % per_dev]
    ).astype(jnp.int32)
    head_at = ndoc + 3
    row_at = head_at + KVH

    k_all = lax.all_gather(keys, "blk", axis=0, tiled=True)
    v_all = lax.all_gather(values, "blk", axis=0, tiled=True)
    k_own = lax.all_gather(keys, "uly", axis=0, tiled=True)
    v_own = lax.all_gather(values, "uly", axis=0, tiled=True)
    acc, stat = own_attention(info, ndoc, ndoc + 2, queries, k_own, v_own)

    k_sets, v_sets = [], []
    for row in range(per_dev):
        source = selected[blk * per_dev + row] // per_dev
        k_part, v_part = pick(source, k_all, v_all, rows)
        k_sets.append(lax.all_gather(k_part, "uly", axis=0, tiled=True))
        v_sets.append(lax.all_gather(v_part, "uly", axis=0, tiled=True))
    if per_dev == 1:
        k_chosen, v_chosen = k_sets[0], v_sets[0]
    else:
        k_chosen = lax.dynamic_index_in_dim(jnp.stack(k_sets), mine, 0, keepdims=False)
        v_chosen = lax.dynamic_index_in_dim(jnp.stack(v_sets), mine, 0, keepdims=False)
    return chosen_attention(info, ndoc, head_at, row_at, queries, k_chosen, v_chosen, acc, stat)


def solution(mesh):
    placed = (P(("blk", "uly"), None), P(("blk", "uly"), None), P(("blk", "uly"), None), P(), P())
    return jax.shard_map(
        functools.partial(on_device, mesh.shape["blk"], mesh.shape["uly"]),
        mesh=mesh,
        in_specs=placed,
        out_specs=P(("blk", "uly"), None),
        check_vma=False,
    )
```
